128 devices in a mesh: clip: 2 (over y_hi), src: 64 (over y_lo, z, x, core).
Axes of the slice: x: 4, y: 4 (y_hi: 2, y_lo: 2; y = y_hi * 2 + y_lo), z: 4, core: 2. Of those that a mesh axis runs over, the one named last changes fastest.
Arguments:
- mask_param: float32 [2048, 1024], P(('clip', 'src')), parts along dimension 0, may hold values from -1.5 to 2.7
- pixel_weight: float32 [2048, 1024], P('clip'), parts along dimension 0, may hold values from 0.25 to 4
- source_weight: float32 [101, 101], replicated, may hold values from 0.5 to 2
- point_index: int32 [512], P('src'), may hold values from 0 to 10200, as said below
- point_count: int32 [64], P('src'), may hold values from 1 to 8, as said below
- target_rects: int32 [256, 4], P('clip'), parts along dimension 0, may hold values from 0 to 1024, as said below
Outputs:
- mask_grad: float32 [2048, 1024], P(('clip', 'src')), parts along dimension 0
- aerial_image: float32 [2048, 1024], P(('clip', 'src')), parts along dimension 0
- source_grad: float32 [1024], P(('clip', 'src')), parts along dimension 0
- loss_value: float32 [2], P('clip'), parts along dimension 0
The draws below stay inside these ranges and needn't reach their ends.
There are 2 independent parts, one for each index of `clip`. The reference program is written for one: setup_inputs(seed, part) draws one part's arguments, and reference() takes and returns one part's arrays. A program takes and returns all parts, laid end to end along the dimension named above; an argument that names none is the same for every part. Nothing has to cross between parts.
Inputs may be any that keep to these rules, and one draw needn't show every extreme that they name: `point_index`: entries are distinct; entry p names the source-grid point of row p div 101 and column p mod 101. Index d of src uses the first point_count[d] of its 8 slots of point_index; some index uses all 8. `target_rects`: each row (x0, x1, y0, y1) has x0 < x1 and y0 < y1.
All inputs are finite; a program needn't handle non-finite values.
Results may differ from the reference program's by a relative error of at most 0.0003.
Values sent between devices are 32-bit elements; how exact they have to be, the bound alone decides.
No kernel may reach another device: no remote copies, remote signals or barrier semaphores. Data moves between devices by JAX's collectives and lax.ppermute only.
A program may use at most 128 MiB of HBM per device.

```python
import math
import jax
import jax.numpy as jnp
from jax import lax

NPIX = 1024
KS = 128
KP = 64
SG = 101
CAP = 8
NRECT = 128
SLOTS = 512


def draw_mask_param(key, part):
    key = jax.random.fold_in(key, 53)
    features = 48
    extent_rows = jax.random.randint(jax.random.fold_in(key, 1), (features,), NPIX // 32 + 1, NPIX // 6 + 1)
    anchor_rows = jax.random.randint(jax.random.fold_in(key, 2), (features,), 0, NPIX - extent_rows + 1)
    extent_cols = jax.random.randint(jax.random.fold_in(key, 3), (features,), NPIX // 32 + 1, NPIX // 6 + 1)
    anchor_cols = jax.random.randint(jax.random.fold_in(key, 4), (features,), 0, NPIX - extent_cols + 1)
    pixels = jnp.arange(NPIX, dtype=jnp.int32)

    def paint(index, canvas):
        row_in = (pixels >= anchor_rows[index]) & (pixels < anchor_rows[index] + extent_rows[index])
        col_in = (pixels >= anchor_cols[index]) & (pixels < anchor_cols[index] + extent_cols[index])
        inside = (row_in[:, None] & col_in[None, :]).astype(jnp.float32)
        return jnp.maximum(canvas, inside)
    canvas = lax.fori_loop(0, features, paint, jnp.zeros((NPIX, NPIX), jnp.float32))
    noise = 0.5 * jax.random.truncated_normal(jax.random.fold_in(key, 5), -3.0, 3.0, (NPIX, NPIX), jnp.float32)
    level = 1.2
    return (level * canvas + noise).astype(jnp.float32)


def draw_point_index(key, part):
    key = jax.random.fold_in(key, 11)
    grid_size = SG * SG
    interior = 1 + jax.random.permutation(jax.random.fold_in(key, 1), grid_size - 2)[:SLOTS - 2]
    listed = jnp.concatenate([jnp.array([0, grid_size - 1], dtype=jnp.int32), interior.astype(jnp.int32)])
    shuffle = jax.random.permutation(jax.random.fold_in(key, 2), SLOTS)
    return listed[shuffle].astype(jnp.int32)


def draw_point_count(key, part):
    key = jax.random.fold_in(key, 23)
    devices = SLOTS // CAP
    base_counts = jax.random.randint(jax.random.fold_in(key, 1), (devices,), 1, max(CAP // 2, 1) + 1)
    shuffle = jax.random.permutation(jax.random.fold_in(key, 2), devices)
    full_number = jax.random.randint(jax.random.fold_in(key, 3), (), 1, max(devices // 8, 1) + 1)
    counts = jnp.where(shuffle < full_number, CAP, base_counts)
    counts = jnp.where(shuffle == devices - 1, 1, counts)
    return counts.astype(jnp.int32)


def rect_side(sub_key):
    extent = jax.random.randint(jax.random.fold_in(sub_key, 1), (NRECT,), NPIX // 64 + 1, NPIX // 8 + 1)
    anchor = jax.random.randint(jax.random.fold_in(sub_key, 2), (NRECT,), 0, NPIX - extent + 1)
    anchor = anchor.at[0].set(0)
    anchor = anchor.at[1].set(NPIX - extent[1])
    return (anchor, anchor + extent)


def draw_target_rects(key, part):
    key = jax.random.fold_in(key, 37)
    row_lo, row_hi = rect_side(jax.random.fold_in(key, 3))
    col_lo, col_hi = rect_side(jax.random.fold_in(key, 4))
    return jnp.stack([row_lo, row_hi, col_lo, col_hi], 1).astype(jnp.int32)


def setup_inputs(seed: int = 0, part: int = 0) -> dict:
    key_of = jax.random.split(jax.random.key(seed), 7)
    own_keys = jax.random.split(jax.random.fold_in(key_of[6], part), 7)
    mask_param = draw_mask_param(jax.random.fold_in(jax.random.fold_in(key_of[6], part), 71), part)
    pixel_weight = jnp.clip(jnp.exp(jax.random.uniform(own_keys[1], (NPIX, NPIX), jnp.float32, math.log(0.25), math.log(4.0))), 0.25, 4.0)
    source_weight = jnp.clip(jnp.exp(jax.random.uniform(key_of[2], (SG, SG), jnp.float32, math.log(0.5), math.log(2.0))), 0.5, 2.0)
    point_index = draw_point_index(jax.random.fold_in(key_of[6], 71), part)
    point_count = draw_point_count(jax.random.fold_in(key_of[6], 71), part)
    target_rects = draw_target_rects(jax.random.fold_in(jax.random.fold_in(key_of[6], part), 71), part)
    return {"mask_param": mask_param, "pixel_weight": pixel_weight, "source_weight": source_weight, "point_index": point_index, "point_count": point_count, "target_rects": target_rects}


STEEP = 10.0
THRESH = 0.3
HIGHEST = lax.Precision.HIGHEST

def forward_tables(pixels):
    frequency = jnp.arange(KS, dtype=jnp.int32) - KS // 2
    phases = jnp.mod(frequency[:, None] * pixels[None, :], NPIX).astype(jnp.float32) * (2.0 * math.pi / NPIX)
    scaling = 1.0 / NPIX
    return (scaling * jnp.cos(phases), -scaling * jnp.sin(phases))

def inverse_tables():
    pixels = jnp.arange(NPIX, dtype=jnp.int32)
    frequency = jnp.arange(KP, dtype=jnp.int32) - KP // 2
    phases = jnp.mod(pixels[:, None] * frequency[None, :], NPIX).astype(jnp.float32) * (2.0 * math.pi / NPIX)
    cos_part = jnp.cos(phases)
    sin_part = jnp.sin(phases)
    left_table = jnp.concatenate([cos_part, sin_part], 1)
    right_table = jnp.concatenate([jnp.concatenate([cos_part.T, sin_part.T], 1), jnp.concatenate([-sin_part.T, cos_part.T], 1)], 0)
    return (left_table, right_table)

def pupil_mask():
    pupil_freq = jnp.arange(KP, dtype=jnp.int32) - KP // 2
    radius = KP // 2 * (KP // 2)
    return (pupil_freq[:, None] * pupil_freq[:, None] + pupil_freq[None, :] * pupil_freq[None, :] < radius).astype(jnp.float32)

def spectrum_of(transmit, cos_rows, sin_rows, cos_all, sin_all):
    projected = jnp.dot(transmit, jnp.concatenate([cos_all.T, sin_all.T], 1), precision=HIGHEST, preferred_element_type=jnp.float32)
    swapped = jnp.concatenate([-projected[:, KS:], projected[:, :KS]], 1)
    first = jnp.dot(cos_rows, projected, precision=HIGHEST, preferred_element_type=jnp.float32)
    return first + jnp.dot(sin_rows, swapped, precision=HIGHEST, preferred_element_type=jnp.float32)

def window_offsets(source_point):
    grid_row = source_point // SG
    grid_col = source_point % SG
    row_start = (grid_row - SG // 2) * (KP // 2) // (SG // 2 + 1) + KP // 2
    col_start = (grid_col - SG // 2) * (KP // 2) // (SG // 2 + 1) + KP // 2
    return (row_start.astype(jnp.int32), col_start.astype(jnp.int32))

def take_window(spectrum, row_start, col_start):
    win_re = lax.dynamic_slice(spectrum, (row_start, col_start), (KP, KP))
    win_im = lax.dynamic_slice(spectrum, (row_start, col_start + KS), (KP, KP))
    return (win_re, win_im)

def add_window(grad_spec, row_start, col_start, grad_re, grad_im):
    old_re = lax.dynamic_slice(grad_spec, (row_start, col_start), (KP, KP))
    grad_spec = lax.dynamic_update_slice(grad_spec, old_re + grad_re, (row_start, col_start))
    old_im = lax.dynamic_slice(grad_spec, (row_start, col_start + KS), (KP, KP))
    return lax.dynamic_update_slice(grad_spec, old_im + grad_im, (row_start, col_start + KS))

def point_field(win_re, win_im, pupil, left_table, right_table):
    masked_re = win_re * pupil
    masked_im = win_im * pupil
    stacked = jnp.concatenate([jnp.concatenate([masked_re, masked_im], 1), jnp.concatenate([-masked_im, masked_re], 1)], 0)
    left_prod = jnp.dot(left_table, stacked, precision=HIGHEST, preferred_element_type=jnp.float32)
    return jnp.dot(left_prod, right_table, precision=HIGHEST, preferred_element_type=jnp.float32)

def intensity_of(fields):
    squared = fields * fields
    return squared[:, :NPIX] + squared[:, NPIX:]

def coverage(target_rects, row_start, row_count):
    pixel_rows = row_start + jnp.arange(row_count, dtype=jnp.int32)
    pixel_cols = jnp.arange(NPIX, dtype=jnp.int32)
    row_inside = ((pixel_rows[:, None] >= target_rects[None, :, 0]) & (pixel_rows[:, None] < target_rects[None, :, 1])).astype(jnp.bfloat16)
    col_inside = ((pixel_cols[None, :] >= target_rects[:, 2:3]) & (pixel_cols[None, :] < target_rects[:, 3:4])).astype(jnp.bfloat16)
    counted = jnp.dot(row_inside, col_inside, preferred_element_type=jnp.float32)
    return jnp.minimum(counted, 1.0)

def reference(mask_param, pixel_weight, source_weight, point_index, point_count, target_rects):
    cos_all, sin_all = forward_tables(jnp.arange(NPIX, dtype=jnp.int32))
    left_table, right_table = inverse_tables()
    pupil = pupil_mask()
    transmit = jnp.tanh(mask_param)

    def full_spectrum(values):
        return spectrum_of(values, cos_all, sin_all, cos_all, sin_all)
    spectrum, spectrum_pull = jax.vjp(full_spectrum, transmit)
    slot_ids = jnp.arange(SLOTS, dtype=jnp.int32)
    active = slot_ids % CAP < jnp.repeat(point_count, CAP)
    weight = jnp.where(active, source_weight.reshape(-1)[point_index], jnp.float32(0.0))
    weight_total = jnp.sum(weight)

    def add_point(summed, scan_item):
        source_point, point_weight = scan_item
        row_start, col_start = window_offsets(source_point)
        win_re, win_im = take_window(spectrum, row_start, col_start)
        fields = point_field(win_re, win_im, pupil, left_table, right_table)
        return (summed + point_weight * intensity_of(fields), None)
    summed, unused = lax.scan(add_point, jnp.zeros((NPIX, NPIX), jnp.float32), (point_index, weight))
    aerial = summed / weight_total
    target = coverage(target_rects, 0, NPIX)
    resist = jax.nn.sigmoid(STEEP * (aerial - THRESH))
    mismatch = resist - target
    loss_sum = jnp.sum(pixel_weight * mismatch * mismatch)
    image_grad = 2.0 * STEEP * pixel_weight * mismatch * resist * (1.0 - resist)
    common = jnp.sum(image_grad * aerial)

    def back_point(grad_spec, scan_item):
        source_point, point_weight = scan_item
        row_start, col_start = window_offsets(source_point)
        win_re, win_im = take_window(spectrum, row_start, col_start)

        def local_field(first, second):
            return point_field(first, second, pupil, left_table, right_table)
        fields, pull_back = jax.vjp(local_field, win_re, win_im)
        strength = intensity_of(fields)
        cotangent = fields * jnp.concatenate([image_grad, image_grad], 1) * (2.0 * point_weight / weight_total)
        grad_re, grad_im = pull_back(cotangent)
        grad_spec = add_window(grad_spec, row_start, col_start, grad_re, grad_im)
        source_term = (jnp.sum(image_grad * strength) - common) / (weight_total * NPIX)
        return (grad_spec, source_term)
    grad_spec, source_terms = lax.scan(back_point, jnp.zeros((KS, 2 * KS), jnp.float32), (point_index, weight))
    source_grad = jnp.where(active, source_terms, jnp.float32(0.0))
    grad_transmit = spectrum_pull(grad_spec)[0]
    mask_grad = grad_transmit * (1.0 - transmit * transmit)
    loss_value = jnp.reshape(loss_sum / (NPIX * NPIX), (1,))
    return (mask_grad, aerial, source_grad, loss_value)
```

```python
import functools
import math

import jax
import jax.numpy as jnp
import ml_dtypes
import numpy as np
from jax import lax
from jax.experimental import pallas as pl
from jax.experimental.pallas import tpu as pltpu
from jax.sharding import PartitionSpec as P

NPIX = 1024
KS = 128
KP = 64
SG = 101
CAP = 8
SRC = 64
SLOTS = SRC * CAP
ROWS = NPIX // SRC
SUB = 128
BLOCK = 256
CHUNK = 16
STEEP = 10.0
THRESH = 0.3

EXTRA = 136
SLOT_ROWS = 144
WEIGHT_ROWS = 148
PACK = 152
SUMS = 136

CORE, XAXIS, ZAXIS, YAXIS = (1, 1), (2, 3), (8, 3), (32, 1)
GROUP = 8

F32 = jnp.float32
BF16 = jnp.bfloat16


def halves(table):
    table = np.asarray(table, np.float64)
    high = table.astype(ml_dtypes.bfloat16)
    low = (table - high.astype(np.float64)).astype(ml_dtypes.bfloat16)
    return np.stack([high, low])


def angles(left, right, period):
    return 2.0 * math.pi * np.mod(np.multiply.outer(left, right), period) / period


@functools.lru_cache(None)
def tables():
    pixels = np.arange(NPIX)
    cols = np.zeros((NPIX, 2 * KS))
    phase = angles(pixels, np.arange(KS // 2), NPIX)
    cols[:, : KS // 2] = np.cos(phase)
    cols[:, KS // 2 : KS] = -np.sin(phase)
    edge = angles(pixels, -KS // 2, NPIX)
    cols[:, KS] = np.cos(edge)
    cols[:, KS + 1] = -np.sin(edge)
    cols[:, KS + 8] = -np.sin(edge)
    cols[:, KS + 9] = -np.cos(edge)
    cols /= NPIX

    phase = angles(np.arange(KS + 1) - KS // 2, pixels, NPIX).reshape(KS + 1, SRC, ROWS)
    rows = np.zeros((SRC, SLOT_ROWS, 2 * ROWS))
    rows[:, : KS + 1, :ROWS] = np.cos(phase).transpose(1, 0, 2)
    rows[:, : KS + 1, ROWS:] = np.sin(phase).transpose(1, 0, 2)
    rows /= NPIX

    flip = np.zeros((KS, EXTRA))
    flip[np.arange(KS), KS - np.arange(KS)] = 1.0
    mirror = np.zeros((KS, 2 * KS))
    keep = np.zeros((KS, 2 * KS))
    half = KS // 2
    for freq in range(half):
        keep[freq, half + freq] = 1.0
        keep[half + freq, KS + half + freq] = 1.0
        if freq:
            mirror[freq, half - freq] = 1.0
            mirror[half + freq, KS + half - freq] = -1.0

    phase = angles(np.arange(KP) - KP // 2, np.arange(SUB), SUB)
    cos_part, sin_part = np.cos(phase), np.sin(phase)
    right = np.block([[cos_part, sin_part], [-sin_part, cos_part]])
    left = np.concatenate([cos_part.T, sin_part.T], 1)

    shift = pixels[:, None] - (NPIX // SUB) * np.arange(SUB)[None, :]
    interp = np.ones((NPIX, SUB))
    for freq in range(1, SUB // 2):
        interp += 2.0 * np.cos(2.0 * math.pi * np.mod(freq * shift, NPIX) / NPIX)
    interp /= SUB

    freq = np.arange(KP) - KP // 2
    pupil = (freq[:, None] ** 2 + freq[None, :] ** 2 < (KP // 2) ** 2).astype(np.float32)
    as_bf16 = lambda table: table.astype(ml_dtypes.bfloat16)
    return dict(
        cols=halves(cols),
        cols_t=halves(cols.T),
        rows=halves(rows).transpose(1, 0, 2, 3),
        rows_t=halves(rows).transpose(1, 0, 3, 2),
        flip=as_bf16(flip),
        flip_t=as_bf16(flip.T),
        mirror=as_bf16(mirror),
        mirror_t=as_bf16(mirror.T),
        keep=as_bf16(keep),
        keep_t=as_bf16(keep.T),
        right=halves(right),
        right_t=halves(right.T),
        left=halves(left),
        left_t=halves(left.T),
        interp=halves(interp),
        interp_t=halves(interp.T),
        pupil=np.concatenate([pupil, pupil], 1),
    )


def split(values):
    high = values.astype(BF16)
    low = (values - high.astype(F32)).astype(BF16)
    return high, low


def mul(first, second, dims=((1,), (0,))):
    return lax.dot_general(first, second, (dims, ((), ())), preferred_element_type=F32)


def mul3(first, second, dims=((1,), (0,))):
    return (
        mul(first[0], second[0], dims) + mul(first[0], second[1], dims) + mul(first[1], second[0], dims)
    )


def pair(ref):
    return ref[0], ref[1]


def div_sg(number):
    return (number * 41529) >> 22


def offset(grid):
    return ((grid - SG // 2) * (KP // 2) + 51 * 64) // 51 - 64 + KP // 2


def lanes_of(shape):
    return lax.broadcasted_iota(jnp.int32, shape, 1)


def slot_numbers():
    shape = (SLOTS // 128, 128)
    return lax.broadcasted_iota(jnp.int32, shape, 0) * 128 + lanes_of(shape)


def project_kernel(me_ref, index_ref, count_ref, weight_ref, mask_ref, cols_ref, rows_ref, rowst_ref, out_ref):
    me = me_ref[0]
    transmit = split(jnp.tanh(mask_ref[...]))
    projected = mul3(transmit, pair(cols_ref))
    main = projected[:, :KS]
    lane = lanes_of(main.shape)
    turned = pltpu.roll(main, KS // 2, 1) * jnp.where(lane < KS // 2, 1.0, -1.0)
    stacked = split(jnp.concatenate([main, turned], 0))
    rows = (rows_ref[0, 0], rows_ref[0, 1])
    out_ref[0:SLOT_ROWS, :] = mul3(rows, stacked)
    edge = split(projected[:, KS:])
    cos_rows = (rowst_ref[0, 0, :ROWS, :KS], rowst_ref[0, 1, :ROWS, :KS])
    sin_rows = (rowst_ref[0, 0, ROWS:, :KS], rowst_ref[0, 1, ROWS:, :KS])
    contract = ((0,), (0,))
    edge_rows = mul3(edge, cos_rows, contract)[0:8] + mul3(edge, sin_rows, contract)[8:16]
    shape = (8, 128)
    sub = lax.broadcasted_iota(jnp.int32, shape, 0)
    lane = lanes_of(shape)
    count = count_ref[0]
    edge_rows = jnp.where(sub < 2, edge_rows, 0.0)
    out_ref[EXTRA:SLOT_ROWS, :] = jnp.where(
        (sub == 2) & (lane == me), count.astype(F32), edge_rows
    )
    number = slot_numbers()
    codes = jnp.zeros(number.shape, F32)
    weights = jnp.zeros(number.shape, F32)
    for slot in range(CAP):
        point = index_ref[slot]
        grid_row = div_sg(point)
        grid_col = point - grid_row * SG
        code = offset(grid_row) * KP + offset(grid_col)
        here = (number == me * CAP + slot) & (slot < count)
        codes = jnp.where(here, code.astype(F32), codes)
        weights = jnp.where(here, weight_ref[grid_row, grid_col], weights)
    out_ref[SLOT_ROWS:WEIGHT_ROWS, :] = codes
    out_ref[WEIGHT_ROWS:PACK, :] = weights


def unpack_spectrum(packed, flip_ref, mirror_ref, keep_ref, re_ref, im_ref):
    high, low = split(packed[0:EXTRA])
    flip = flip_ref[...]
    full = jnp.zeros((KS, 2 * KS), F32)
    for part in (high, low):
        flipped = mul(flip, part).astype(BF16)
        full = full + mul(flipped, mirror_ref[...]) + mul(part[:KS], keep_ref[...])
    edge = jnp.transpose(packed[EXTRA:SLOT_ROWS])
    lane = lanes_of((KS, KS))
    re_ref[...] = jnp.where(lane == 0, edge[:, 0:1], full[:, :KS])
    im_ref[...] = jnp.where(lane == 0, edge[:, 1:2], full[:, KS:])


def list_slots(rank, counts_ref, list_ref):
    def step(index, carry):
        listed, before = carry
        count = counts_ref[0, index]
        first = (rank - before) & (GROUP - 1)
        for turn in range(CAP // GROUP):
            position = first + turn * GROUP
            list_ref[listed] = index * CAP + position
            listed = listed + jnp.where(position < count, 1, 0)
        return listed, before + count

    listed, unused = lax.fori_loop(0, SRC, step, (jnp.int32(0), jnp.int32(0)))
    return listed


def load_slots(packed, codes_ref, counts_ref, weights_ref, ints_ref, vals_ref, sems):
    ints_ref[0:8, :] = packed[EXTRA:SLOT_ROWS].astype(jnp.int32)
    ints_ref[8:12, :] = packed[SLOT_ROWS:WEIGHT_ROWS].astype(jnp.int32)
    vals_ref[...] = packed[WEIGHT_ROWS:PACK]
    copies = [
        pltpu.make_async_copy(ints_ref.at[pl.ds(2, 1)], counts_ref, sems.at[0]),
        pltpu.make_async_copy(ints_ref.at[pl.ds(8, 4)], codes_ref, sems.at[1]),
        pltpu.make_async_copy(vals_ref, weights_ref, sems.at[2]),
    ]
    for copy in copies:
        copy.start()
    return copies


def window(code, re_ref, im_ref, pupil):
    row = code >> 6
    col = code & (KP - 1)
    rows = pl.ds(row, KP)
    real = pltpu.roll(re_ref[rows, :], (KS - col) & (KS - 1), 1)
    imag = pltpu.roll(im_ref[rows, :], KP - col, 1)
    return jnp.where(lanes_of((KP, KS)) < KP, real, imag) * pupil


def field(masked, right, left):
    inner = mul3(split(masked), right)
    real, imag = inner[:, :SUB], inner[:, SUB:]
    stacked = jnp.concatenate(
        [jnp.concatenate([real, imag], 1), jnp.concatenate([-imag, real], 1)], 0
    )
    return mul3(left, split(stacked))


SLOT_SCRATCH = [
    pltpu.SMEM((4, 128), jnp.int32),
    pltpu.SMEM((1, 128), jnp.int32),
    pltpu.SMEM((4, 128), F32),
    pltpu.SMEM((SLOTS + CAP,), jnp.int32),
    pltpu.VMEM((16, 128), jnp.int32),
    pltpu.VMEM((4, 128), F32),
    pltpu.SemaphoreType.DMA((3,)),
]


def slot_place(slot):
    return slot >> 7, slot & 127


def image_kernel(
    parts, me_ref, *refs
):
    packs = refs[:parts]
    flip_ref, mirror_ref, keep_ref, right_ref, left_ref, pupil_ref = refs[parts : parts + 6]
    out_ref, re_out, im_out, meta_out = refs[parts + 6 : parts + 10]
    codes_ref, counts_ref, weights_ref, list_ref, ints_ref, vals_ref, sems = refs[parts + 10 :]
    packed = packs[0][...]
    for ref in packs[1:]:
        packed = packed + ref[...]
    copies = load_slots(packed, codes_ref, counts_ref, weights_ref, ints_ref, vals_ref, sems)
    meta_out[...] = packed[EXTRA:PACK]
    unpack_spectrum(packed, flip_ref, mirror_ref, keep_ref, re_out, im_out)
    for copy in copies:
        copy.wait()
    listed = list_slots(me_ref[0] & (GROUP - 1), counts_ref, list_ref)
    right, left = pair(right_ref), pair(left_ref)
    pupil = pupil_ref[...]
    out_ref[...] = jnp.zeros_like(out_ref)

    def step(index, total):
        high, low = slot_place(list_ref[index])
        weight = weights_ref[high, low]
        values = field(window(codes_ref[high, low], re_out, im_out, pupil), right, left)
        real, imag = values[:, :SUB], values[:, SUB:]
        out_ref[0:SUB, :] += weight * (real * real + imag * imag)
        return total + weight

    total = lax.fori_loop(0, listed, step, jnp.float32(0.0))
    out_ref[SUB:SUMS, :] = jnp.full((SUMS - SUB, 128), total, F32)


def grad_kernel(parts, me_ref, *refs):
    sums = refs[:parts]
    (
        pixel_ref, rects_ref, rects_t_ref, re_ref, im_ref, meta_ref, interp_ref, interp_t_ref,
        full_ref, full_t_ref, mine_ref, right_ref, right_t_ref, left_ref, left_t_ref, pupil_ref, flip_t_ref,
        mirror_t_ref, keep_t_ref,
    ) = refs[parts : parts + 19]
    out_ref, aerial_ref, loss_ref = refs[parts + 19 : parts + 22]
    (
        image_ref, total_ref, aer_ref, cnt_ref, g_ref, k_ref, grad_re, grad_im, lossacc_ref,
        codes_ref, counts_ref, weights_ref, list_ref, ints_ref, vals_ref, sems,
    ) = refs[parts + 22 :]
    step_id = pl.program_id(0)
    full_t = pair(full_t_ref)

    @pl.when(step_id == 0)
    def start():
        image = sums[0][...]
        for ref in sums[1:]:
            image = image + ref[...]
        total_ref[...] = image[SUB:SUMS]
        scaled = split(image[0:SUB] / image[SUB : SUB + 1])
        image_ref[0] = scaled[0]
        image_ref[1] = scaled[1]
        k_ref[...] = jnp.zeros_like(k_ref)
        lossacc_ref[...] = jnp.zeros_like(lossacc_ref)
        mine = mul3(pair(mine_ref), scaled)
        aerial_ref[...] = mul3(split(mine), full_t)

    half = mul3(pair(interp_ref), pair(image_ref))
    aer_ref[...] = mul3(split(half), full_t)
    first = step_id * BLOCK
    row = lax.broadcasted_iota(jnp.int32, (BLOCK, 128), 0) + first
    row_in = ((row >= rects_t_ref[0:1, :]) & (row < rects_t_ref[1:2, :])).astype(F32).astype(BF16)
    col = lax.broadcasted_iota(jnp.int32, (128, NPIX), 1)
    col_in = ((col >= rects_ref[:, 2:3]) & (col < rects_ref[:, 3:4])).astype(F32).astype(BF16)
    cnt_ref[...] = mul(row_in, col_in)

    def chunk(index, carry):
        rows = pl.ds(pl.multiple_of(index * CHUNK, CHUNK), CHUNK)
        aerial = aer_ref[rows, :]
        target = jnp.minimum(cnt_ref[rows, :], 1.0)
        resist = 1.0 / (1.0 + jnp.exp(-STEEP * (aerial - THRESH)))
        mismatch = resist - target
        weighted = pixel_ref[rows, :] * mismatch
        lossacc_ref[...] += weighted * mismatch
        high, low = split(2.0 * STEEP * weighted * resist * (1.0 - resist))
        g_ref[0, rows, :] = high
        g_ref[1, rows, :] = low
        return carry

    lax.fori_loop(0, BLOCK // CHUNK, chunk, 0)
    reduced = mul3(pair(g_ref), pair(full_ref))
    k_ref[...] += mul3(pair(interp_t_ref), split(reduced))

    @pl.when(step_id == pl.num_programs(0) - 1)
    def finish():
        loss_ref[...] = jnp.full((8, 128), jnp.sum(lossacc_ref[...]) / (NPIX * NPIX), F32)
        meta = meta_ref[...]
        ints_ref[0:8, :] = meta[0:8].astype(jnp.int32)
        ints_ref[8:12, :] = meta[8:12].astype(jnp.int32)
        vals_ref[...] = meta[12:16]
        copies = [
            pltpu.make_async_copy(ints_ref.at[pl.ds(2, 1)], counts_ref, sems.at[0]),
            pltpu.make_async_copy(ints_ref.at[pl.ds(8, 4)], codes_ref, sems.at[1]),
            pltpu.make_async_copy(vals_ref, weights_ref, sems.at[2]),
        ]
        for copy in copies:
            copy.start()
        for copy in copies:
            copy.wait()
        listed = list_slots(me_ref[0] & (GROUP - 1), counts_ref, list_ref)
        right, left = pair(right_ref), pair(left_ref)
        right_t, left_t = pair(right_t_ref), pair(left_t_ref)
        pupil = pupil_ref[...]
        kernel = k_ref[...]
        total = total_ref[0:1, 0:1]
        image = image_ref[0].astype(F32) + image_ref[1].astype(F32)
        common = jnp.sum(kernel * image)
        grad_re[...] = jnp.zeros_like(grad_re)
        grad_im[...] = jnp.zeros_like(grad_im)
        number = slot_numbers()
        lane = lanes_of((KP, KS))

        def back(index, terms):
            slot = list_ref[index]
            high, low = slot_place(slot)
            code = codes_ref[high, low]
            weight = weights_ref[high, low]
            masked = window(code, re_ref, im_ref, pupil)
            values = field(masked, right, left)
            real, imag = values[:, :SUB] * kernel, values[:, SUB:] * kernel
            pulled = mul3(left_t, split(jnp.concatenate([real, imag], 1)))
            top, low_half = pulled[:KP], pulled[KP:]
            inner = jnp.concatenate(
                [top[:, :SUB] + low_half[:, SUB:], top[:, SUB:] - low_half[:, :SUB]], 1
            )
            grad = mul3(split(inner), right_t) * pupil
            strength = jnp.sum(grad * masked)
            terms = jnp.where(number == slot, strength - common, terms)
            scaled = grad * (2.0 * weight)
            row = code >> 6
            col = code & (KP - 1)
            rows = pl.ds(row, KP)
            grad_re[rows, :] += pltpu.roll(jnp.where(lane < KP, scaled, 0.0), col, 1)
            grad_im[rows, :] += pltpu.roll(jnp.where(lane < KP, 0.0, scaled), col + KP, 1)
            return terms

        terms = lax.fori_loop(0, listed, back, jnp.zeros(number.shape, F32))
        out_ref[SLOT_ROWS:WEIGHT_ROWS, :] = terms / (total * NPIX)
        out_ref[WEIGHT_ROWS:PACK, :] = jnp.zeros((PACK - WEIGHT_ROWS, 128), F32)
        real, imag = grad_re[...] / total, grad_im[...] / total
        edge = jnp.where(
            lax.broadcasted_iota(jnp.int32, (8, 128), 0) == 0,
            jnp.transpose(real)[0:1],
            jnp.transpose(imag)[0:1],
        )
        out_ref[EXTRA:SLOT_ROWS, :] = jnp.where(
            lax.broadcasted_iota(jnp.int32, (8, 128), 0) < 2, edge, 0.0
        )
        mirrored = jnp.zeros((EXTRA, KS), F32)
        kept = jnp.zeros((KS, KS), F32)
        for part in split(jnp.concatenate([real, imag], 1)):
            mirrored = mirrored + mul(flip_t_ref[...], mul(part, mirror_t_ref[...]).astype(BF16))
            kept = kept + mul(part, keep_t_ref[...])
        out_ref[0:KS, :] = mirrored[0:KS] + kept
        out_ref[KS:EXTRA, :] = mirrored[KS:EXTRA]


def mask_kernel(parts, me_ref, *refs):
    packs = refs[:parts]
    mask_ref, rowst_ref, cols_t_ref = refs[parts : parts + 3]
    out_ref, terms_ref = refs[parts + 3 : parts + 5]
    packed = packs[0][...]
    for ref in packs[1:]:
        packed = packed + ref[...]
    pulled = mul3((rowst_ref[0, 0], rowst_ref[0, 1]), split(packed[0:SLOT_ROWS]))
    sin_part = pltpu.roll(pulled[ROWS:], KS // 2, 1)
    lane = lanes_of((ROWS, KS))
    main = pulled[:ROWS] + jnp.where(lane < KS // 2, -sin_part, sin_part)
    edge = packed[EXTRA:SLOT_ROWS]
    blank = jnp.zeros((KS - 16, KS), F32)
    none = jnp.zeros((8, KS), F32)
    cos_rows = (rowst_ref[0, 0, :ROWS, :KS], rowst_ref[0, 1, :ROWS, :KS])
    sin_rows = (rowst_ref[0, 0, ROWS:, :KS], rowst_ref[0, 1, ROWS:, :KS])
    contract = ((1,), (1,))
    side = mul3(cos_rows, split(jnp.concatenate([edge, none, blank], 0)), contract) + mul3(
        sin_rows, split(jnp.concatenate([none, edge, blank], 0)), contract
    )
    gathered = split(jnp.concatenate([main, side], 1))
    transmit = jnp.tanh(mask_ref[...])
    out_ref[...] = mul3(gathered, pair(cols_t_ref)) * (1.0 - transmit * transmit)
    terms_ref[...] = packed[SLOT_ROWS:PACK]


def exchange(value, axis):
    stride, mask = axis
    received = [value]
    for other in range(1, mask + 1):
        pairs = [(index, index ^ (other * stride)) for index in range(SRC)]
        received.append(lax.ppermute(value, "src", pairs))
    return received


def added(values):
    return functools.reduce(jnp.add, values)


VMEM_LIMIT = 48 * 1024 * 1024


def full_spec(array, memory=pltpu.VMEM):
    rank = len(array.shape)
    return pl.BlockSpec(array.shape, lambda *unused: (0,) * rank, memory_space=memory)


def body(mask_param, pixel_weight, source_weight, point_index, point_count, target_rects):
    table = tables()
    me = lax.axis_index("src").astype(jnp.int32)
    me_array = jnp.reshape(me, (1,))
    params = pltpu.CompilerParams(vmem_limit_bytes=VMEM_LIMIT)
    smem = pl.BlockSpec(memory_space=pltpu.SMEM)
    rows_spec = pl.BlockSpec((1, 2, SLOT_ROWS, 2 * ROWS), lambda step, me: (me[0], 0, 0, 0))
    rowst_spec = pl.BlockSpec((1, 2, 2 * ROWS, SLOT_ROWS), lambda step, me: (me[0], 0, 0, 0))

    pack = pl.pallas_call(
        project_kernel,
        grid_spec=pltpu.PrefetchScalarGridSpec(
            num_scalar_prefetch=1,
            grid=(1,),
            in_specs=[smem, smem, smem, full_spec(mask_param), full_spec(table["cols"]), rows_spec, rowst_spec],
            out_specs=pl.BlockSpec((PACK, 128), lambda step, me: (0, 0)),
        ),
        out_shape=jax.ShapeDtypeStruct((PACK, 128), F32),
        compiler_params=params,
        name="project",
    )(me_array, point_index, point_count, source_weight, mask_param, table["cols"], table["rows"], table["rows_t"])

    pack = added(exchange(pack, CORE))
    pack = added(exchange(pack, YAXIS))
    pack = added(exchange(pack, XAXIS))
    packs = exchange(pack, ZAXIS)

    constants = [table[name] for name in ("flip", "mirror", "keep", "right", "left", "pupil")]
    sums, spec_re, spec_im, meta = pl.pallas_call(
        functools.partial(image_kernel, len(packs)),
        grid_spec=pltpu.PrefetchScalarGridSpec(
            num_scalar_prefetch=1,
            grid=(1,),
            in_specs=[full_spec(array) for array in packs + constants],
            out_specs=[
                pl.BlockSpec((SUMS, 128), lambda step, me: (0, 0)),
                pl.BlockSpec((KS, KS), lambda step, me: (0, 0)),
                pl.BlockSpec((KS, KS), lambda step, me: (0, 0)),
                pl.BlockSpec((PACK - EXTRA, 128), lambda step, me: (0, 0)),
            ],
            scratch_shapes=SLOT_SCRATCH,
        ),
        out_shape=[
            jax.ShapeDtypeStruct((SUMS, 128), F32),
            jax.ShapeDtypeStruct((KS, KS), F32),
            jax.ShapeDtypeStruct((KS, KS), F32),
            jax.ShapeDtypeStruct((PACK - EXTRA, 128), F32),
        ],
        compiler_params=params,
        name="image",
    )(me_array, *packs, *constants)

    sums = added(exchange(sums, CORE))
    all_sums = exchange(sums, XAXIS)

    interp, interp_t = table["interp"], table["interp_t"]
    grad_in = [
        (pixel_weight, pl.BlockSpec((BLOCK, NPIX), lambda step, me: (step, 0))),
        (target_rects, None),
        (target_rects.T, None),
        (spec_re, None),
        (spec_im, None),
        (meta, None),
        (interp, pl.BlockSpec((2, BLOCK, SUB), lambda step, me: (0, step, 0))),
        (interp_t, pl.BlockSpec((2, SUB, BLOCK), lambda step, me: (0, 0, step))),
        (interp, None),
        (interp_t, None),
        (interp, pl.BlockSpec((2, ROWS, SUB), lambda step, me: (0, me[0], 0))),
        (table["right"], None),
        (table["right_t"], None),
        (table["left"], None),
        (table["left_t"], None),
        (table["pupil"], None),
        (table["flip_t"], None),
        (table["mirror_t"], None),
        (table["keep_t"], None),
    ]
    grad_pack, aerial, loss = pl.pallas_call(
        functools.partial(grad_kernel, len(all_sums)),
        grid_spec=pltpu.PrefetchScalarGridSpec(
            num_scalar_prefetch=1,
            grid=(NPIX // BLOCK,),
            in_specs=[full_spec(array) for array in all_sums]
            + [full_spec(array) if spec is None else spec for array, spec in grad_in],
            out_specs=[
                pl.BlockSpec((PACK, 128), lambda step, me: (0, 0)),
                pl.BlockSpec((ROWS, NPIX), lambda step, me: (0, 0)),
                pl.BlockSpec((8, 128), lambda step, me: (0, 0)),
            ],
            scratch_shapes=[
                pltpu.VMEM((2, SUB, SUB), BF16),
                pltpu.VMEM((8, 128), F32),
                pltpu.VMEM((BLOCK, NPIX), F32),
                pltpu.VMEM((BLOCK, NPIX), F32),
                pltpu.VMEM((2, BLOCK, NPIX), BF16),
                pltpu.VMEM((SUB, SUB), F32),
                pltpu.VMEM((KS, KS), F32),
                pltpu.VMEM((KS, KS), F32),
                pltpu.VMEM((CHUNK, NPIX), F32),
            ]
            + SLOT_SCRATCH,
        ),
        out_shape=[
            jax.ShapeDtypeStruct((PACK, 128), F32),
            jax.ShapeDtypeStruct((ROWS, NPIX), F32),
            jax.ShapeDtypeStruct((8, 128), F32),
        ],
        compiler_params=params,
        name="gradient",
    )(me_array, *all_sums, *[array for array, unused in grad_in])

    grad_pack = added(exchange(grad_pack, CORE))
    grads = exchange(grad_pack, XAXIS)

    mask_grad, terms = pl.pallas_call(
        functools.partial(mask_kernel, len(grads)),
        grid_spec=pltpu.PrefetchScalarGridSpec(
            num_scalar_prefetch=1,
            grid=(1,),
            in_specs=[full_spec(array) for array in grads]
            + [full_spec(mask_param), rowst_spec, full_spec(table["cols_t"])],
            out_specs=[
                pl.BlockSpec((ROWS, NPIX), lambda step, me: (0, 0)),
                pl.BlockSpec((8, 128), lambda step, me: (0, 0)),
            ],
        ),
        out_shape=[
            jax.ShapeDtypeStruct((ROWS, NPIX), F32),
            jax.ShapeDtypeStruct((8, 128), F32),
        ],
        compiler_params=params,
        name="mask",
    )(me_array, *grads, mask_param, table["rows_t"], table["cols_t"])
    source_grad = lax.dynamic_slice(terms.reshape(8 * 128), (me * CAP,), (CAP,))
    return mask_grad, aerial, source_grad, loss[0, 0:1]


def solution(mesh):
    in_specs = (P(("clip", "src"), None), P("clip", None), P(), P("src"), P("src"), P("clip", None))
    out_specs = (P(("clip", "src"), None), P(("clip", "src"), None), P(("clip", "src")), P("clip"))
    return jax.shard_map(body, mesh=mesh, in_specs=in_specs, out_specs=out_specs, check_vma=False)
```

```python
import functools
import math

import jax
import jax.numpy as jnp
import ml_dtypes
import numpy as np
from jax import lax
from jax.experimental import pallas as pl
from jax.experimental.pallas import tpu as pltpu
from jax.sharding import PartitionSpec as P

NPIX = 1024
KS = 128
KP = 64
SG = 101
CAP = 8
SRC = 64
SLOTS = SRC * CAP
ROWS = NPIX // SRC
SUB = 128
BLOCK = 256
CHUNK = 16
STEEP = 10.0
THRESH = 0.3

EDGE = ROWS
META = EDGE + 2
PACK = 24
GATHER = 32
SUMS = 136
MIRROR_ROW = KS
EDGE_ROWS = KS + 8
TERM_ROWS = KS + 16
GRAD = KS + 24

CORE = (1,)
GROUP_DEVICES = (1, 32, 33)
GROUP = 4
BATCH = 4

F32 = jnp.float32
BF16 = jnp.bfloat16


def halves(table):
    table = np.asarray(table, np.float64)
    high = table.astype(ml_dtypes.bfloat16)
    low = (table - high.astype(np.float64)).astype(ml_dtypes.bfloat16)
    return np.stack([high, low])


def angles(left, right, period):
    return 2.0 * math.pi * np.mod(np.multiply.outer(left, right), period) / period


@functools.lru_cache(None)
def tables():
    pixels = np.arange(NPIX)
    cols = np.zeros((NPIX, 2 * KS))
    phase = angles(pixels, np.arange(KS // 2), NPIX)
    cols[:, : KS // 2] = np.cos(phase)
    cols[:, KS // 2 : KS] = -np.sin(phase)
    edge = angles(pixels, -KS // 2, NPIX)
    cols[:, KS] = np.cos(edge)
    cols[:, KS + 1] = -np.sin(edge)
    cols[:, KS + 8] = -np.sin(edge)
    cols[:, KS + 9] = -np.cos(edge)
    cols /= NPIX

    phase = angles(np.arange(KS + 1) - KS // 2, pixels, NPIX).reshape(KS + 1, SRC, ROWS)
    wave = np.stack([np.cos(phase), np.sin(phase)]) / NPIX
    by_core = wave[:, :KS].reshape(2 * KS, GATHER, 2, ROWS).transpose(2, 0, 1, 3)
    waves = by_core.reshape(2, 2 * KS, GATHER * ROWS)
    own = np.zeros((SRC, 2 * ROWS, 2 * KS))
    own[:, :, : KS + 1] = wave.transpose(2, 0, 3, 1).reshape(SRC, 2 * ROWS, KS + 1)

    half = KS // 2
    keep = np.zeros((KS, 2 * KS))
    mirror = np.zeros((KS, 2 * KS))
    for freq in range(half):
        keep[freq, half + freq] = 1.0
        keep[half + freq, KS + half + freq] = 1.0
        if freq:
            mirror[freq, half - freq] = 1.0
            mirror[half + freq, KS + half - freq] = 1.0
    flip = np.zeros((EDGE_ROWS, KS))
    flip[KS - np.arange(KS), np.arange(KS)] = 1.0
    conj = mirror * np.where(np.arange(KS) < half, 1.0, -1.0)[:, None]

    phase = angles(np.arange(KP) - KP // 2, np.arange(SUB), SUB)
    cos_part, sin_part = np.cos(phase), np.sin(phase)
    right = np.block([[cos_part, sin_part], [-sin_part, cos_part]])
    left = np.concatenate([cos_part.T, sin_part.T], 1)

    shift = pixels[:, None] - (NPIX // SUB) * np.arange(SUB)[None, :]
    interp = np.ones((NPIX, SUB))
    for freq in range(1, SUB // 2):
        interp += 2.0 * np.cos(2.0 * math.pi * np.mod(freq * shift, NPIX) / NPIX)
    interp /= SUB

    freq = np.arange(KP) - KP // 2
    pupil = (freq[:, None] ** 2 + freq[None, :] ** 2 < (KP // 2) ** 2).astype(np.float32)
    as_bf16 = lambda table: table.astype(ml_dtypes.bfloat16)
    high_low = lambda table, axis: np.concatenate(list(halves(table)), axis)
    twice = lambda table, axis: np.concatenate([halves(table)[0]] * 2, axis)
    return dict(
        cols=halves(cols),
        cols_t=halves(cols.T),
        waves=halves(waves).transpose(1, 0, 2, 3),
        own=halves(own).transpose(1, 0, 2, 3),
        unfold=as_bf16(np.concatenate([keep, mirror], 0)),
        fold=as_bf16(np.concatenate([keep.T, conj.T], 1)),
        flip=as_bf16(flip),
        right=twice(right, 0),
        right_low=halves(right)[1],
        left=twice(left, 1),
        left_low=halves(left)[1],
        right_t=high_low(right.T, 1),
        left_t=twice(left.T, 1),
        left_t_low=halves(left.T)[1],
        interp=high_low(interp, 1),
        interp_t=twice(interp.T, 0),
        interp_t_low=halves(interp.T)[1],
        pupil=np.concatenate([pupil, pupil], 1),
    )


def split(values):
    high = values.astype(BF16)
    low = (values - high.astype(F32)).astype(BF16)
    return high, low


def mul(first, second, dims=((1,), (0,))):
    return lax.dot_general(first, second, (dims, ((), ())), preferred_element_type=F32)


def mul3(first, second, dims=((1,), (0,))):
    return (
        mul(first[0], second[0], dims) + mul(first[0], second[1], dims) + mul(first[1], second[0], dims)
    )


def pair(ref):
    return ref[0], ref[1]


def div_sg(number):
    return (number * 41529) >> 22


def offset(grid):
    return ((grid - SG // 2) * (KP // 2) + 51 * 64) // 51 - 64 + KP // 2


def lanes_of(shape):
    return lax.broadcasted_iota(jnp.int32, shape, 1)


def slot_numbers():
    shape = (SLOTS // 128, 128)
    return lax.broadcasted_iota(jnp.int32, shape, 0) * 128 + lanes_of(shape)


def start_all(sources, targets, sems):
    copies = [
        pltpu.make_async_copy(source, target, sems.at[place])
        for place, (source, target) in enumerate(zip(sources, targets))
    ]
    for copy in copies:
        copy.start()
    return copies


def wait_all(copies):
    for copy in copies:
        copy.wait()


def project_kernel(
    me_ref, index_hbm, count_hbm, weight_hbm, mask_hbm, cols_hbm, own_hbm, out_ref,
    index_ref, count_ref, weight_ref, mask_ref, cols_ref, own_ref, sems,
):
    me = me_ref[0]
    copies = start_all(
        (mask_hbm, cols_hbm, own_hbm.at[me], index_hbm, count_hbm, weight_hbm),
        (mask_ref, cols_ref, own_ref, index_ref, count_ref, weight_ref),
        sems,
    )
    copies[0].wait()
    transmit = split(jnp.tanh(mask_ref[...]))
    copies[1].wait()
    projected = mul3(transmit, pair(cols_ref))
    wait_all(copies[2:])
    edge = split(projected[:, KS:])
    cos_rows = (own_ref[0, :ROWS, :KS], own_ref[1, :ROWS, :KS])
    sin_rows = (own_ref[0, ROWS:, :KS], own_ref[1, ROWS:, :KS])
    contract = ((0,), (0,))
    edge_rows = mul3(edge, cos_rows, contract)[0:8] + mul3(edge, sin_rows, contract)[8:16]
    shape = (PACK - EDGE, 128)
    lane = lanes_of(shape)
    sub = lax.broadcasted_iota(jnp.int32, shape, 0)
    count = count_ref[0]
    meta = jnp.where(lane == 2 * CAP, count.astype(F32), 0.0)
    for slot in range(CAP):
        point = index_ref[slot]
        grid_row = div_sg(point)
        grid_col = point - grid_row * SG
        code = offset(grid_row) * KP + offset(grid_col)
        meta = jnp.where(lane == slot, code.astype(F32), meta)
        meta = jnp.where(lane == CAP + slot, weight_ref[grid_row, grid_col], meta)
    tail = jnp.where(sub < 2, edge_rows, jnp.where(sub == 2, meta, 0.0))
    block = jnp.concatenate([projected[:, :KS], tail], 0)
    for place in range(GATHER):
        out_ref[place] = block


def unpack_spectrum(mine_ref, other_ref, waves_ref, core, unfold, re_ref, im_ref):
    total = jnp.zeros((2 * KS, KS), F32)
    edge = jnp.zeros((PACK - EDGE, KS), F32)
    for ref, which in ((mine_ref, core), (other_ref, 1 - core)):
        gathered = ref[...]
        high, low = split(gathered[:, :ROWS].reshape(GATHER * ROWS, KS))
        both = mul(waves_ref[which, 0], jnp.concatenate([high, low], 1))
        total = total + both[:, :KS] + both[:, KS:] + mul(waves_ref[which, 1], high)
        edge = edge + jnp.sum(gathered[:, EDGE:], 0)
    lower = lanes_of((KS, KS)) < KS // 2
    cos_part = total[:KS]
    sin_part = pltpu.roll(total[KS:], KS // 2, 1)
    near = cos_part + jnp.where(lower, sin_part, -sin_part)
    far = jnp.where(lower, cos_part - sin_part, -cos_part - sin_part)
    full = jnp.zeros((KS, 2 * KS), F32)
    for part in split(jnp.concatenate([near, far], 1)):
        full = full + mul(part, unfold)
    column = jnp.transpose(edge)
    lane = lanes_of((KS, KS))
    re_ref[...] = jnp.where(lane == 0, column[:, 0:1], full[:, :KS])
    im_ref[...] = jnp.where(lane == 0, column[:, 1:2], full[:, KS:])


def list_slots(rank, core, ints_ref, floats_ref, codes_ref, weights_ref, slots_ref):
    def step(index, carry):
        listed, before = carry
        row = (index >> 1) + ((index + core) & 1) * GATHER
        count = ints_ref[row, 2 * CAP]
        first = (rank - before) & (GROUP - 1)
        for turn in range(CAP // GROUP):
            position = first + turn * GROUP
            codes_ref[listed] = ints_ref[row, position]
            weights_ref[listed] = floats_ref[row, CAP + position]
            slots_ref[listed] = index * CAP + position
            listed = listed + jnp.where(position < count, 1, 0)
        return listed, before + count

    listed, unused = lax.fori_loop(0, SRC, step, (jnp.int32(0), jnp.int32(0)))
    for extra in range(BATCH):
        codes_ref[listed + extra] = 0
        weights_ref[listed + extra] = jnp.float32(0.0)
        slots_ref[listed + extra] = -1
    return listed


def window(code, re_ref, im_ref, pupil):
    row = code >> 6
    col = code & (KP - 1)
    rows = pl.ds(row, KP)
    real = pltpu.roll(re_ref[rows, :], (KS - col) & (KS - 1), 1)
    imag = pltpu.roll(im_ref[rows, :], KP - col, 1)
    return jnp.where(lanes_of((KP, KS)) < KP, real, imag) * pupil


def fields(masked, right, right_low, left, left_low):
    high, low = split(jnp.concatenate(masked, 0))
    inner = mul(jnp.concatenate([high, low], 1), right) + mul(high, right_low)
    tops, turned = [], []
    for part in split(inner):
        pieces = [part[place * KP : (place + 1) * KP] for place in range(len(masked))]
        tops.append(jnp.concatenate(pieces, 1))
        turned.append(
            jnp.concatenate([half for piece in pieces for half in (-piece[:, SUB:], piece[:, :SUB])], 1)
        )
    first = jnp.concatenate([tops[0], turned[0]], 0)
    second = jnp.concatenate([tops[1], turned[1]], 0)
    return mul(left, jnp.concatenate([first, second], 0)) + mul(left_low, first)


def image_kernel(
    me_ref, mine_ref, other_ref, waves_hbm, unfold_hbm, right_hbm, right_low_hbm, left_hbm, left_low_hbm,
    pupil_hbm, out_ref, re_out, im_out, codes_out, weights_out, slots_out, listed_out,
    waves_ref, unfold_ref, right_ref, right_low_ref, left_ref, left_low_ref, pupil_ref,
    ints_ref, floats_ref, ints_smem, floats_smem, sems,
):
    core = me_ref[0] & 1
    copies = start_all(
        (waves_hbm, unfold_hbm, right_hbm, right_low_hbm, left_hbm, left_low_hbm, pupil_hbm),
        (waves_ref, unfold_ref, right_ref, right_low_ref, left_ref, left_low_ref, pupil_ref),
        sems,
    )
    meta = jnp.concatenate([mine_ref[:, META, :], other_ref[:, META, :]], 0)
    ints_ref[...] = meta.astype(jnp.int32)
    floats_ref[...] = meta
    metas = [
        pltpu.make_async_copy(ints_ref, ints_smem, sems.at[7]),
        pltpu.make_async_copy(floats_ref, floats_smem, sems.at[8]),
    ]
    for copy in metas:
        copy.start()
    wait_all(copies)
    unpack_spectrum(mine_ref, other_ref, waves_ref, core, unfold_ref[...], re_out, im_out)
    wait_all(metas)
    rank = core + 2 * (me_ref[0] >> 5)
    listed = list_slots(rank, core, ints_smem, floats_smem, codes_out, weights_out, slots_out)
    listed_out[0] = listed
    consts = (right_ref[...], right_low_ref[...], left_ref[...], left_low_ref[...])
    pupil = pupil_ref[...]
    out_ref[...] = jnp.zeros_like(out_ref)

    def step(index, total):
        base = index * BATCH
        masked = [window(codes_out[base + place], re_out, im_out, pupil) for place in range(BATCH)]
        values = fields(masked, *consts)
        acc = out_ref[0:SUB, :]
        for place in range(BATCH):
            weight = weights_out[base + place]
            real = values[:, place * 2 * SUB : place * 2 * SUB + SUB]
            imag = values[:, place * 2 * SUB + SUB : (place + 1) * 2 * SUB]
            acc = acc + weight * (real * real + imag * imag)
            total = total + weight
        out_ref[0:SUB, :] = acc
        return total

    total = lax.fori_loop(0, (listed + BATCH - 1) // BATCH, step, jnp.float32(0.0))
    out_ref[SUB:SUMS, :] = jnp.full((SUMS - SUB, 128), total, F32)


def grad_kernel(
    me_ref, *refs
):
    sums = refs[:GROUP]
    (
        pixel_ref, rects_ref, rects_t_ref, re_ref, im_ref, codes_ref, weights_ref, slots_ref, listed_ref,
    ) = refs[GROUP : GROUP + 9]
    hbms = refs[GROUP + 9 : GROUP + 22]
    out_ref, aerial_ref, loss_ref = refs[GROUP + 22 : GROUP + 25]
    tabs = refs[GROUP + 25 : GROUP + 38]
    image_ref, total_ref, aer_ref, cnt_ref, g_ref, k_ref, grad_re, grad_im, lossacc_ref, sems = refs[GROUP + 38 :]
    (
        interp_ref, interp_t_ref, interp_t_low_ref, right_ref, right_low_ref, left_ref, left_low_ref,
        right_t_ref, left_t_ref, left_t_low_ref, pupil_ref, fold_ref, flip_ref,
    ) = tabs
    step_id = pl.program_id(0)
    me = me_ref[0]

    def table_copies():
        return [
            pltpu.make_async_copy(source, target, sems.at[place])
            for place, (source, target) in enumerate(zip(hbms, tabs))
        ]

    def interpolated(rows):
        table = interp_ref[rows, :]
        both = mul(table[:, :SUB], image_ref[...])
        half = both[:, :SUB] + both[:, SUB:] + mul(table[:, SUB:], image_ref[:, :SUB])
        high, low = split(half)
        return mul(jnp.concatenate([high, low], 1), interp_t_ref[...]) + mul(high, interp_t_low_ref[...])

    @pl.when(step_id == 0)
    def start():
        copies = table_copies()
        for copy in copies:
            copy.start()
        image = sums[0][...]
        for ref in sums[1:]:
            image = image + ref[...]
        total_ref[...] = image[SUB:SUMS]
        image_ref[...] = jnp.concatenate(split(image[0:SUB] / image[SUB : SUB + 1]), 1)
        k_ref[...] = jnp.zeros_like(k_ref)
        lossacc_ref[...] = jnp.zeros_like(lossacc_ref)
        wait_all(copies)
        aerial_ref[...] = interpolated(pl.ds(pl.multiple_of(me * ROWS, ROWS), ROWS))

    first = pl.multiple_of(step_id * BLOCK, BLOCK)
    block_rows = pl.ds(first, BLOCK)
    aer_ref[...] = interpolated(block_rows)
    row = lax.broadcasted_iota(jnp.int32, (BLOCK, 128), 0) + first
    row_in = ((row >= rects_t_ref[0:1, :]) & (row < rects_t_ref[1:2, :])).astype(F32).astype(BF16)
    col = lax.broadcasted_iota(jnp.int32, (128, NPIX), 1)
    col_in = ((col >= rects_ref[:, 2:3]) & (col < rects_ref[:, 3:4])).astype(F32).astype(BF16)
    cnt_ref[...] = mul(row_in, col_in)

    loss = lossacc_ref[...]
    for place in range(BLOCK // CHUNK):
        rows = pl.ds(place * CHUNK, CHUNK)
        target = jnp.minimum(cnt_ref[rows, :], 1.0)
        resist = 1.0 / (1.0 + jnp.exp(STEEP * THRESH - STEEP * aer_ref[rows, :]))
        mismatch = resist - target
        weighted = pixel_ref[rows, :] * mismatch
        loss = loss + weighted * mismatch
        high, low = split((2.0 * STEEP) * weighted * (resist * (1.0 - resist)))
        g_ref[0, rows, :] = high
        g_ref[1, rows, :] = low
    lossacc_ref[...] = loss

    both = mul(g_ref[0], interp_ref[...])
    reduced = both[:, :SUB] + both[:, SUB:] + mul(g_ref[1], interp_ref[:, :SUB])
    high, low = split(reduced)
    both = mul(interp_t_ref[0:SUB, block_rows], jnp.concatenate([high, low], 1))
    k_ref[...] += both[:, :SUB] + both[:, SUB:] + mul(interp_t_low_ref[:, block_rows], high)

    @pl.when(step_id == pl.num_programs(0) - 1)
    def finish():
        loss_ref[0] = jnp.sum(lossacc_ref[...]) / (NPIX * NPIX)
        consts = (right_ref[...], right_low_ref[...], left_ref[...], left_low_ref[...])
        right_t = right_t_ref[...]
        left_t, left_t_low = left_t_ref[...], left_t_low_ref[...]
        pupil = pupil_ref[...]
        kernel = k_ref[...]
        total = total_ref[0:1, 0:1]
        image = image_ref[:, :SUB].astype(F32) + image_ref[:, SUB:].astype(F32)
        common = jnp.sum(kernel * image)
        grad_re[...] = jnp.zeros_like(grad_re)
        grad_im[...] = jnp.zeros_like(grad_im)
        number = slot_numbers()
        lane = lanes_of((KP, KS))
        kernel2 = jnp.concatenate([kernel, kernel], 1)

        def back(index, terms):
            base = index * BATCH
            masked = [window(codes_ref[base + place], re_ref, im_ref, pupil) for place in range(BATCH)]
            values = fields(masked, *consts)
            high, low = split(values * jnp.concatenate([kernel2] * BATCH, 1))
            pulled = mul(left_t, jnp.concatenate([high, low], 0)) + mul(left_t_low, high)
            inner = []
            for place in range(BATCH):
                piece = pulled[:, place * 2 * SUB : (place + 1) * 2 * SUB]
                top, bottom = piece[:KP], piece[KP:]
                inner.append(
                    jnp.concatenate(
                        [top[:, :SUB] + bottom[:, SUB:], top[:, SUB:] - bottom[:, :SUB]], 1
                    )
                )
            high, low = split(jnp.concatenate(inner, 0))
            both = mul(high, right_t)
            grads = both[:, :KS] + both[:, KS:] + mul(low, right_t[:, :KS])
            for place in range(BATCH):
                grad = grads[place * KP : (place + 1) * KP] * pupil
                strength = jnp.sum(grad * masked[place])
                terms = jnp.where(number == slots_ref[base + place], strength - common, terms)
                scaled = grad * (2.0 * weights_ref[base + place])
                code = codes_ref[base + place]
                row = code >> 6
                col = code & (KP - 1)
                rows = pl.ds(row, KP)
                grad_re[rows, :] += pltpu.roll(jnp.where(lane < KP, scaled, 0.0), col, 1)
                grad_im[rows, :] += pltpu.roll(jnp.where(lane < KP, 0.0, scaled), col + KP, 1)
            return terms

        batches = (listed_ref[0] + BATCH - 1) // BATCH
        terms = lax.fori_loop(0, batches, back, jnp.zeros(number.shape, F32))
        real, imag = grad_re[...] / total, grad_im[...] / total
        sub = lax.broadcasted_iota(jnp.int32, (8, KS), 0)
        edge = jnp.where(sub == 0, jnp.transpose(real)[0:1], jnp.transpose(imag)[0:1])
        kept = jnp.zeros((KS, KS), F32)
        mirrored = jnp.zeros((EDGE_ROWS, KS), F32)
        for part in split(jnp.concatenate([real, imag], 1)):
            folded = mul(part, fold_ref[...])
            kept = kept + folded[:, :KS]
            mirrored = mirrored + mul(flip_ref[...], folded[:, KS:].astype(BF16))
        out_ref[0:KS, :] = kept + mirrored[0:KS]
        out_ref[MIRROR_ROW:EDGE_ROWS, :] = mirrored[KS:]
        out_ref[EDGE_ROWS:TERM_ROWS, :] = jnp.where(sub < 2, edge, 0.0)
        blank = jnp.zeros((GRAD - TERM_ROWS - SLOTS // 128, 128), F32)
        out_ref[TERM_ROWS:GRAD, :] = jnp.concatenate([terms / (total * NPIX), blank], 0)


def mask_kernel(me_ref, *refs):
    packs = refs[:GROUP]
    mask_hbm, own_hbm, cols_hbm, out_ref, slot_ref = refs[GROUP : GROUP + 5]
    mask_ref, own_ref, cols_ref, terms_vmem, terms_smem, sems = refs[GROUP + 5 :]
    me = me_ref[0]
    copies = start_all((own_hbm.at[me], cols_hbm, mask_hbm), (own_ref, cols_ref, mask_ref), sems)
    packed = packs[0][...]
    for ref in packs[1:]:
        packed = packed + ref[...]
    terms_vmem[...] = packed[TERM_ROWS:GRAD]
    fetch = pltpu.make_async_copy(terms_vmem, terms_smem, sems.at[3])
    fetch.start()
    copies[0].wait()
    used = EDGE_ROWS
    pulled = mul3((own_ref[0, :, :used], own_ref[1, :, :used]), split(packed[0:used]))
    sin_part = pltpu.roll(pulled[ROWS:], KS // 2, 1)
    lane = lanes_of((ROWS, KS))
    main = pulled[:ROWS] + jnp.where(lane < KS // 2, -sin_part, sin_part)
    edge = packed[EDGE_ROWS:TERM_ROWS]
    blank = jnp.zeros((KS - 16, KS), F32)
    none = jnp.zeros((8, KS), F32)
    cos_rows = (own_ref[0, :ROWS, :KS], own_ref[1, :ROWS, :KS])
    sin_rows = (own_ref[0, ROWS:, :KS], own_ref[1, ROWS:, :KS])
    contract = ((1,), (1,))
    side = mul3(cos_rows, split(jnp.concatenate([edge, none, blank], 0)), contract) + mul3(
        sin_rows, split(jnp.concatenate([none, edge, blank], 0)), contract
    )
    gathered = split(jnp.concatenate([main, side], 1))
    wait_all(copies[1:])
    transmit = jnp.tanh(mask_ref[...])
    out_ref[...] = mul3(gathered, pair(cols_ref)) * (1.0 - transmit * transmit)
    fetch.wait()
    for slot in range(CAP):
        place = me * CAP + slot
        slot_ref[slot] = terms_smem[place >> 7, place & 127]


def exchange(value, others):
    received = [value]
    for other in others:
        pairs = [(index, index ^ other) for index in range(SRC)]
        received.append(lax.ppermute(value, "src", pairs))
    return received


MIB = 1024 * 1024


def full_spec(array):
    rank = len(array.shape)
    return pl.BlockSpec(array.shape, lambda *unused: (0,) * rank)


def body(mask_param, pixel_weight, source_weight, point_index, point_count, target_rects):
    table = tables()
    me = lax.axis_index("src").astype(jnp.int32)
    me_array = jnp.reshape(me, (1,))
    smem = pl.BlockSpec(memory_space=pltpu.SMEM)
    hbm = pl.BlockSpec(memory_space=pltpu.HBM)
    buffers = lambda names: [pltpu.VMEM(table[name].shape, table[name].dtype) for name in names]

    block = pl.pallas_call(
        project_kernel,
        grid_spec=pltpu.PrefetchScalarGridSpec(
            num_scalar_prefetch=1,
            grid=(1,),
            in_specs=[hbm] * 6,
            out_specs=pl.BlockSpec((GATHER, PACK, 128), lambda step, me: (0, 0, 0)),
            scratch_shapes=[
                pltpu.SMEM((CAP,), jnp.int32),
                pltpu.SMEM((1,), jnp.int32),
                pltpu.SMEM((SG, SG), F32),
                pltpu.VMEM((ROWS, NPIX), F32),
                pltpu.VMEM(table["cols"].shape, BF16),
                pltpu.VMEM(table["own"].shape[1:], BF16),
                pltpu.SemaphoreType.DMA((6,)),
            ],
        ),
        out_shape=jax.ShapeDtypeStruct((GATHER, PACK, 128), F32),
        compiler_params=pltpu.CompilerParams(vmem_limit_bytes=24 * MIB),
        name="project",
    )(me_array, point_index, point_count, source_weight, mask_param, table["cols"], table["own"])

    same_core = [list(range(core, SRC, 2)) for core in range(2)]
    mine = lax.all_to_all(block, "src", 0, 0, axis_index_groups=same_core, tiled=True)
    unused, other = exchange(mine, CORE)

    names = ("waves", "unfold", "right", "right_low", "left", "left_low", "pupil")
    lists = [((SLOTS + 2 * BATCH,), jnp.int32), ((SLOTS + 2 * BATCH,), F32), ((SLOTS + 2 * BATCH,), jnp.int32), ((1,), jnp.int32)]
    sums, spec_re, spec_im, *listed = pl.pallas_call(
        image_kernel,
        grid_spec=pltpu.PrefetchScalarGridSpec(
            num_scalar_prefetch=1,
            grid=(1,),
            in_specs=[full_spec(mine), full_spec(other)] + [hbm] * len(names),
            out_specs=[
                pl.BlockSpec((SUMS, 128), lambda step, me: (0, 0)),
                pl.BlockSpec((KS, KS), lambda step, me: (0, 0)),
                pl.BlockSpec((KS, KS), lambda step, me: (0, 0)),
            ]
            + [smem] * len(lists),
            scratch_shapes=buffers(names)
            + [
                pltpu.VMEM((SRC, 128), jnp.int32),
                pltpu.VMEM((SRC, 128), F32),
                pltpu.SMEM((SRC, 128), jnp.int32),
                pltpu.SMEM((SRC, 128), F32),
                pltpu.SemaphoreType.DMA((9,)),
            ],
        ),
        out_shape=[
            jax.ShapeDtypeStruct((SUMS, 128), F32),
            jax.ShapeDtypeStruct((KS, KS), F32),
            jax.ShapeDtypeStruct((KS, KS), F32),
        ]
        + [jax.ShapeDtypeStruct(shape, dtype) for shape, dtype in lists],
        compiler_params=pltpu.CompilerParams(vmem_limit_bytes=24 * MIB),
        name="image",
    )(me_array, mine, other, *[table[name] for name in names])

    all_sums = exchange(sums, GROUP_DEVICES)

    names = (
        "interp", "interp_t", "interp_t_low", "right", "right_low", "left", "left_low", "right_t", "left_t",
        "left_t_low", "pupil", "fold", "flip",
    )
    operands = all_sums + [pixel_weight, target_rects, target_rects.T, spec_re, spec_im]
    specs = [full_spec(array) for array in operands]
    specs[GROUP] = pl.BlockSpec((BLOCK, NPIX), lambda step, me: (step, 0))
    grad, aerial, loss = pl.pallas_call(
        grad_kernel,
        grid_spec=pltpu.PrefetchScalarGridSpec(
            num_scalar_prefetch=1,
            grid=(NPIX // BLOCK,),
            in_specs=specs + [smem] * len(listed) + [hbm] * len(names),
            out_specs=[
                pl.BlockSpec((GRAD, 128), lambda step, me: (0, 0)),
                pl.BlockSpec((ROWS, NPIX), lambda step, me: (0, 0)),
                smem,
            ],
            scratch_shapes=buffers(names)
            + [
                pltpu.VMEM((SUB, 2 * SUB), BF16),
                pltpu.VMEM((8, 128), F32),
                pltpu.VMEM((BLOCK, NPIX), F32),
                pltpu.VMEM((BLOCK, NPIX), F32),
                pltpu.VMEM((2, BLOCK, NPIX), BF16),
                pltpu.VMEM((SUB, SUB), F32),
                pltpu.VMEM((KS, KS), F32),
                pltpu.VMEM((KS, KS), F32),
                pltpu.VMEM((CHUNK, NPIX), F32),
                pltpu.SemaphoreType.DMA((len(names),)),
            ],
        ),
        out_shape=[
            jax.ShapeDtypeStruct((GRAD, 128), F32),
            jax.ShapeDtypeStruct((ROWS, NPIX), F32),
            jax.ShapeDtypeStruct((1,), F32),
        ],
        compiler_params=pltpu.CompilerParams(vmem_limit_bytes=32 * MIB),
        name="gradient",
    )(me_array, *operands, *listed, *[table[name] for name in names])

    grads = exchange(grad, GROUP_DEVICES)

    mask_grad, source_grad = pl.pallas_call(
        mask_kernel,
        grid_spec=pltpu.PrefetchScalarGridSpec(
            num_scalar_prefetch=1,
            grid=(1,),
            in_specs=[full_spec(array) for array in grads] + [hbm] * 3,
            out_specs=[pl.BlockSpec((ROWS, NPIX), lambda step, me: (0, 0)), smem],
            scratch_shapes=[
                pltpu.VMEM((ROWS, NPIX), F32),
                pltpu.VMEM(table["own"].shape[1:], BF16),
                pltpu.VMEM(table["cols_t"].shape, BF16),
                pltpu.VMEM((8, 128), F32),
                pltpu.SMEM((8, 128), F32),
                pltpu.SemaphoreType.DMA((4,)),
            ],
        ),
        out_shape=[
            jax.ShapeDtypeStruct((ROWS, NPIX), F32),
            jax.ShapeDtypeStruct((CAP,), F32),
        ],
        compiler_params=pltpu.CompilerParams(vmem_limit_bytes=24 * MIB),
        name="mask",
    )(me_array, *grads, mask_param, table["own"], table["cols_t"])
    return mask_grad, aerial, source_grad, loss


def solution(mesh):
    in_specs = (P(("clip", "src"), None), P("clip", None), P(), P("src"), P("src"), P("clip", None))
    out_specs = (P(("clip", "src"), None), P(("clip", "src"), None), P(("clip", "src")), P("clip"))
    return jax.shard_map(body, mesh=mesh, in_specs=in_specs, out_specs=out_specs, check_vma=False)
```

```python
import functools
import math

import jax
import jax.numpy as jnp
import ml_dtypes
import numpy as np
from jax import lax
from jax.experimental import pallas as pl
from jax.experimental.pallas import tpu as pltpu
from jax.sharding import PartitionSpec as P

NPIX = 1024
KS = 128
KP = 64
SG = 101
CAP = 8
SRC = 64
SLOTS = SRC * CAP
ROWS = NPIX // SRC
SUB = 128
BLOCK = 256
CHUNK = 16
STEEP = 10.0
THRESH = 0.3

EDGE = ROWS
META = EDGE + 2
PACK = 24
GATHER = 32
SUMS = 136
MIRROR_ROW = KS
EDGE_ROWS = KS + 8
TERM_ROWS = KS + 16
GRAD = KS + 24

CORE = (1,)
GROUP_DEVICES = (1, 32, 33)
GROUP = 4
BATCH = 8
BATCHES = SLOTS // GROUP // BATCH

F32 = jnp.float32
BF16 = jnp.bfloat16


def halves(table):
    table = np.asarray(table, np.float64)
    high = table.astype(ml_dtypes.bfloat16)
    low = (table - high.astype(np.float64)).astype(ml_dtypes.bfloat16)
    return np.stack([high, low])


def angles(left, right, period):
    return 2.0 * math.pi * np.mod(np.multiply.outer(left, right), period) / period


@functools.lru_cache(None)
def tables():
    pixels = np.arange(NPIX)
    cols = np.zeros((NPIX, 2 * KS))
    phase = angles(pixels, np.arange(KS // 2), NPIX)
    cols[:, : KS // 2] = np.cos(phase)
    cols[:, KS // 2 : KS] = -np.sin(phase)
    edge = angles(pixels, -KS // 2, NPIX)
    cols[:, KS] = np.cos(edge)
    cols[:, KS + 1] = -np.sin(edge)
    cols[:, KS + 8] = -np.sin(edge)
    cols[:, KS + 9] = -np.cos(edge)
    cols /= NPIX

    phase = angles(np.arange(KS + 1) - KS // 2, pixels, NPIX).reshape(KS + 1, SRC, ROWS)
    wave = np.stack([np.cos(phase), np.sin(phase)]) / NPIX
    by_core = wave[:, :KS].reshape(2 * KS, GATHER, 2, ROWS).transpose(2, 0, 1, 3)
    waves = by_core.reshape(2, 2 * KS, GATHER * ROWS)
    own = np.zeros((SRC, 2 * ROWS, 2 * KS))
    own[:, :, : KS + 1] = wave.transpose(2, 0, 3, 1).reshape(SRC, 2 * ROWS, KS + 1)

    half = KS // 2
    keep = np.zeros((KS, 2 * KS))
    mirror = np.zeros((KS, 2 * KS))
    for freq in range(half):
        keep[freq, half + freq] = 1.0
        keep[half + freq, KS + half + freq] = 1.0
        if freq:
            mirror[freq, half - freq] = 1.0
            mirror[half + freq, KS + half - freq] = 1.0
    flip = np.zeros((EDGE_ROWS, KS))
    flip[KS - np.arange(KS), np.arange(KS)] = 1.0
    conj = mirror * np.where(np.arange(KS) < half, 1.0, -1.0)[:, None]

    phase = angles(np.arange(KP) - KP // 2, np.arange(SUB), SUB)
    cos_part, sin_part = np.cos(phase), np.sin(phase)
    right = np.block([[cos_part, sin_part], [-sin_part, cos_part]])
    left = np.concatenate([cos_part.T, sin_part.T], 1)

    shift = pixels[:, None] - (NPIX // SUB) * np.arange(SUB)[None, :]
    interp = np.ones((NPIX, SUB))
    for freq in range(1, SUB // 2):
        interp += 2.0 * np.cos(2.0 * math.pi * np.mod(freq * shift, NPIX) / NPIX)
    interp /= SUB

    freq = np.arange(KP) - KP // 2
    pupil = (freq[:, None] ** 2 + freq[None, :] ** 2 < (KP // 2) ** 2).astype(np.float32)
    as_bf16 = lambda table: table.astype(ml_dtypes.bfloat16)
    high_low = lambda table, axis: np.concatenate(list(halves(table)), axis)
    twice = lambda table, axis: np.concatenate([halves(table)[0]] * 2, axis)
    return dict(
        cols=halves(cols),
        cols_t=halves(cols.T),
        waves=halves(waves).transpose(1, 0, 2, 3),
        own=halves(own).transpose(1, 0, 2, 3),
        unfold=as_bf16(np.concatenate([keep, mirror], 0)),
        fold=as_bf16(np.concatenate([keep.T, conj.T], 1)),
        flip=as_bf16(flip),
        right=twice(right, 0),
        right_low=halves(right)[1],
        left=twice(left, 1),
        left_low=halves(left)[1],
        right_t=high_low(right.T, 1),
        left_t=twice(left.T, 1),
        left_t_low=halves(left.T)[1],
        interp=high_low(interp, 1),
        interp_t=twice(interp.T, 0),
        interp_t_low=halves(interp.T)[1],
        pupil=np.concatenate([pupil, pupil], 1),
    )


def split(values):
    high = values.astype(BF16)
    low = (values - high.astype(F32)).astype(BF16)
    return high, low


def mul(first, second, dims=((1,), (0,))):
    return lax.dot_general(first, second, (dims, ((), ())), preferred_element_type=F32)


def mul3(first, second, dims=((1,), (0,))):
    return (
        mul(first[0], second[0], dims) + mul(first[0], second[1], dims) + mul(first[1], second[0], dims)
    )


def pair(ref):
    return ref[0], ref[1]


def div_sg(number):
    return (number * 41529) >> 22


def offset(grid):
    return ((grid - SG // 2) * (KP // 2) + 51 * 64) // 51 - 64 + KP // 2


def lanes_of(shape):
    return lax.broadcasted_iota(jnp.int32, shape, 1)


def slot_numbers():
    shape = (SLOTS // 128, 128)
    return lax.broadcasted_iota(jnp.int32, shape, 0) * 128 + lanes_of(shape)


def start_all(sources, targets, sems):
    copies = [
        pltpu.make_async_copy(source, target, sems.at[place])
        for place, (source, target) in enumerate(zip(sources, targets))
    ]
    for copy in copies:
        copy.start()
    return copies


def wait_all(copies):
    for copy in copies:
        copy.wait()


def project_kernel(
    index_hbm, count_hbm, weight_hbm, mask_hbm, cols_hbm, own_hbm, out_ref,
    index_ref, count_ref, weight_ref, mask_ref, cols_ref, own_ref, sems,
):
    me = lax.axis_index("src")
    copies = start_all(
        (mask_hbm, cols_hbm, own_hbm.at[me], index_hbm, count_hbm, weight_hbm),
        (mask_ref, cols_ref, own_ref, index_ref, count_ref, weight_ref),
        sems,
    )
    copies[0].wait()
    transmit = split(jnp.tanh(mask_ref[...]))
    copies[1].wait()
    projected = mul3(transmit, pair(cols_ref))
    wait_all(copies[2:])
    edge = split(projected[:, KS:])
    cos_rows = (own_ref[0, :ROWS, :KS], own_ref[1, :ROWS, :KS])
    sin_rows = (own_ref[0, ROWS:, :KS], own_ref[1, ROWS:, :KS])
    contract = ((0,), (0,))
    edge_rows = mul3(edge, cos_rows, contract)[0:8] + mul3(edge, sin_rows, contract)[8:16]
    shape = (PACK - EDGE, 128)
    lane = lanes_of(shape)
    sub = lax.broadcasted_iota(jnp.int32, shape, 0)
    count = count_ref[0]
    meta = jnp.where(lane == 2 * CAP, count.astype(F32), 0.0)
    for slot in range(CAP):
        point = index_ref[slot]
        grid_row = div_sg(point)
        grid_col = point - grid_row * SG
        code = offset(grid_row) * KP + offset(grid_col)
        meta = jnp.where(lane == slot, code.astype(F32), meta)
        meta = jnp.where(lane == CAP + slot, weight_ref[grid_row, grid_col], meta)
    tail = jnp.where(sub < 2, edge_rows, jnp.where(sub == 2, meta, 0.0))
    block = jnp.concatenate([projected[:, :KS], tail], 0)
    for place in range(GATHER):
        out_ref[place] = block


def unpack_spectrum(mine_ref, other_ref, waves_ref, core, unfold, re_ref, im_ref):
    total = jnp.zeros((2 * KS, KS), F32)
    edge = jnp.zeros((PACK - EDGE, KS), F32)
    for ref, which in ((mine_ref, core), (other_ref, 1 - core)):
        gathered = ref[...]
        high, low = split(gathered[:, :ROWS].reshape(GATHER * ROWS, KS))
        both = mul(waves_ref[which, 0], jnp.concatenate([high, low], 1))
        total = total + both[:, :KS] + both[:, KS:] + mul(waves_ref[which, 1], high)
        edge = edge + jnp.sum(gathered[:, EDGE:], 0)
    lower = lanes_of((KS, KS)) < KS // 2
    cos_part = total[:KS]
    sin_part = pltpu.roll(total[KS:], KS // 2, 1)
    near = cos_part + jnp.where(lower, sin_part, -sin_part)
    far = jnp.where(lower, cos_part - sin_part, -cos_part - sin_part)
    full = jnp.zeros((KS, 2 * KS), F32)
    for part in split(jnp.concatenate([near, far], 1)):
        full = full + mul(part, unfold)
    column = jnp.transpose(edge)
    lane = lanes_of((KS, KS))
    re_ref[...] = jnp.where(lane == 0, column[:, 0:1], full[:, :KS])
    im_ref[...] = jnp.where(lane == 0, column[:, 1:2], full[:, KS:])


def list_slots(rank, core, ints_ref, floats_ref, codes_ref, weights_ref, slots_ref):
    def step(index, carry):
        listed, before = carry
        row = (index >> 1) + ((index + core) & 1) * GATHER
        count = ints_ref[row, 2 * CAP]
        first = (rank - before) & (GROUP - 1)
        for turn in range(CAP // GROUP):
            position = first + turn * GROUP
            codes_ref[listed] = ints_ref[row, position]
            weights_ref[listed] = floats_ref[row, CAP + position]
            slots_ref[listed] = index * CAP + position
            listed = listed + jnp.where(position < count, 1, 0)
        return listed, before + count

    listed, unused = lax.fori_loop(0, SRC, step, (jnp.int32(0), jnp.int32(0)))
    for extra in range(BATCH):
        codes_ref[listed + extra] = 0
        weights_ref[listed + extra] = jnp.float32(0.0)
        slots_ref[listed + extra] = -1
    return listed


def window(code, re_ref, im_ref, pupil):
    row = code >> 6
    col = code & (KP - 1)
    rows = pl.ds(row, KP)
    real = pltpu.roll(re_ref[rows, :], (KS - col) & (KS - 1), 1)
    imag = pltpu.roll(im_ref[rows, :], KP - col, 1)
    return jnp.where(lanes_of((KP, KS)) < KP, real, imag) * pupil


def swapped(window_values):
    sign = jnp.where(lanes_of(window_values.shape) < KP, -1.0, 1.0)
    return pltpu.roll(window_values, KP, 1) * sign


def fields(masked, right, right_low, left, left_low):
    parts = [split(jnp.concatenate([piece, swapped(piece)], 0)) for piece in masked]
    high = jnp.concatenate([part[0] for part in parts], 1)
    low = jnp.concatenate([part[1] for part in parts], 1)
    inner = mul(left, jnp.concatenate([high, low], 0)) + mul(left_low, high)
    pieces = [inner[:, place * KS : (place + 1) * KS] for place in range(len(masked))]
    high, low = split(jnp.concatenate(pieces, 0))
    return mul(jnp.concatenate([high, low], 1), right) + mul(high, right_low)


def pull_fields(cotangent, right_t, left_t, left_t_low):
    high, low = split(cotangent)
    both = mul(high, right_t)
    inner = both[:, :KS] + both[:, KS:] + mul(low, right_t[:, :KS])
    count = cotangent.shape[0] // SUB
    high, low = split(jnp.concatenate([inner[place * SUB : (place + 1) * SUB] for place in range(count)], 1))
    pulled = mul(left_t, jnp.concatenate([high, low], 0)) + mul(left_t_low, high)
    grads = []
    for place in range(count):
        piece = pulled[:, place * KS : (place + 1) * KS]
        grads.append(piece[:KP] - swapped(piece[KP:]))
    return grads


IMAGE_TABLES = ("waves", "unfold", "right", "right_low", "left", "left_low", "pupil")


def image_kernel(*refs):
    inputs, refs = refs[:9], refs[9:]
    (out_ref, codes_out, weights_out, slots_out, listed_out, field_out), refs = refs[:6], refs[6:]
    buffers, refs = refs[:9], refs[9:]
    re_ref, im_ref, field_ref, ints_ref, floats_ref, ints_smem, floats_smem, sems, field_sems = refs
    mine_ref, other_ref, waves_ref, unfold_ref, right_ref, right_low_ref, left_ref, left_low_ref, pupil_ref = buffers
    me = lax.axis_index("src")
    core = me & 1
    copies = start_all(inputs, buffers, sems)
    wait_all(copies[:2])
    meta = jnp.concatenate([mine_ref[:, META, :], other_ref[:, META, :]], 0)
    ints_ref[...] = meta.astype(jnp.int32)
    floats_ref[...] = meta
    metas = [
        pltpu.make_async_copy(ints_ref, ints_smem, sems.at[9]),
        pltpu.make_async_copy(floats_ref, floats_smem, sems.at[10]),
    ]
    for copy in metas:
        copy.start()
    wait_all(copies[2:])
    unpack_spectrum(mine_ref, other_ref, waves_ref, core, unfold_ref[...], re_ref, im_ref)
    wait_all(metas)
    rank = core + 2 * (me >> 5)
    listed = list_slots(rank, core, ints_smem, floats_smem, codes_out, weights_out, slots_out)
    listed_out[0] = listed
    consts = (right_ref[...], right_low_ref[...], left_ref[...], left_low_ref[...])
    pupil = pupil_ref[...]
    out_ref[...] = jnp.zeros_like(out_ref)
    batches = (listed + BATCH - 1) // BATCH

    def store(index):
        return pltpu.make_async_copy(field_ref.at[index], field_out.at[index], field_sems.at[index])

    def step(index, total):
        base = index * BATCH
        masked = [window(codes_out[base + place], re_ref, im_ref, pupil) for place in range(BATCH)]
        values = fields(masked, *consts)
        field_ref[index] = values
        store(index).start()
        acc = out_ref[0:SUB, :]
        for place in range(BATCH):
            weight = weights_out[base + place]
            piece = values[place * SUB : (place + 1) * SUB]
            squares = piece * piece
            acc = acc + weight * (squares[:, :SUB] + squares[:, SUB:])
            total = total + weight
        out_ref[0:SUB, :] = acc
        return total

    total = lax.fori_loop(0, batches, step, jnp.float32(0.0))
    out_ref[SUB:SUMS, :] = jnp.full((SUMS - SUB, 128), total, F32)

    def finish(index, carry):
        store(index).wait()
        return carry

    lax.fori_loop(0, batches, finish, 0)


GRAD_TABLES = (
    "interp", "interp_t", "interp_t_low", "right_t", "left_t", "left_t_low", "fold", "flip", "pupil",
)


def grad_kernel(*refs):
    sums_hbm, refs = refs[:GROUP], refs[GROUP:]
    (pixel_hbm, rects_hbm, rects_t_hbm, field_hbm), refs = refs[:4], refs[4:]
    lists_hbm, refs = refs[:4], refs[4:]
    tabs_hbm, refs = refs[: len(GRAD_TABLES)], refs[len(GRAD_TABLES) :]
    (out_ref, aerial_ref, loss_ref), refs = refs[:3], refs[3:]
    sums, refs = refs[:GROUP], refs[GROUP:]
    (pixel_ref, rects_ref, rects_t_ref, field_ref), refs = refs[:4], refs[4:]
    lists, refs = refs[:4], refs[4:]
    tabs, refs = refs[: len(GRAD_TABLES)], refs[len(GRAD_TABLES) :]
    image_ref, aer_ref, cnt_ref, g_ref, k_ref, grad_refs, sems, pixel_sems, field_sems = refs
    (
        interp_ref, interp_t_ref, interp_t_low_ref, right_t_ref, left_t_ref, left_t_low_ref, fold_ref,
        flip_ref, pupil_ref,
    ) = tabs
    codes_ref, weights_ref, slots_ref, listed_ref = lists
    me = lax.axis_index("src")
    blocks = NPIX // BLOCK

    firsts = start_all(
        tuple(sums_hbm) + (rects_hbm, rects_t_hbm) + tuple(tabs_hbm[:3]),
        tuple(sums) + (rects_ref, rects_t_ref) + tuple(tabs[:3]),
        sems,
    )
    pixel_copies = [
        pltpu.make_async_copy(
            pixel_hbm.at[pl.ds(place * BLOCK, BLOCK)], pixel_ref.at[pl.ds(place * BLOCK, BLOCK)], pixel_sems.at[place]
        )
        for place in range(blocks)
    ]
    for copy in pixel_copies:
        copy.start()
    begun = len(firsts)
    rest = [
        pltpu.make_async_copy(source, target, sems.at[begun + place])
        for place, (source, target) in enumerate(
            zip(tuple(lists_hbm) + tuple(tabs_hbm[3:]), tuple(lists) + tuple(tabs[3:]))
        )
    ]
    for copy in rest:
        copy.start()

    def load(index):
        return pltpu.make_async_copy(field_hbm.at[index], field_ref.at[index], field_sems.at[index])

    wait_all(firsts)
    image = sums[0][...]
    for ref in sums[1:]:
        image = image + ref[...]
    total = image[SUB : SUB + 1, 0:1]
    scaled = image[0:SUB] / total
    image_ref[...] = jnp.concatenate(split(scaled), 1)

    def interpolated(rows):
        table = interp_ref[rows, :]
        both = mul(table[:, :SUB], image_ref[...])
        half = both[:, :SUB] + both[:, SUB:] + mul(table[:, SUB:], image_ref[:, :SUB])
        high, low = split(half)
        return mul(jnp.concatenate([high, low], 1), interp_t_ref[...]) + mul(high, interp_t_low_ref[...])

    col = lax.broadcasted_iota(jnp.int32, (128, NPIX), 1)
    col_in = ((col >= rects_ref[:, 2:3]) & (col < rects_ref[:, 3:4])).astype(F32).astype(BF16)

    def prepare(place):
        first = place * BLOCK
        aer_ref[place % 2] = interpolated(pl.ds(first, BLOCK))
        row = lax.broadcasted_iota(jnp.int32, (BLOCK, 128), 0) + first
        row_in = ((row >= rects_t_ref[0:1, :]) & (row < rects_t_ref[1:2, :])).astype(F32).astype(BF16)
        cnt_ref[place % 2] = mul(row_in, col_in)

    loss = jnp.zeros((CHUNK, NPIX), F32)
    k_ref[...] = jnp.zeros_like(k_ref)
    prepare(0)
    for place in range(blocks):
        if place + 1 < blocks:
            prepare(place + 1)
        pixel_copies[place].wait()
        for index in range(BLOCK // CHUNK):
            rows = pl.ds(index * CHUNK, CHUNK)
            wave = jnp.tanh((STEEP / 2.0) * aer_ref[place % 2, rows, :] - (STEEP * THRESH / 2.0))
            mismatch = 0.5 * wave + (0.5 - jnp.minimum(cnt_ref[place % 2, rows, :], 1.0))
            weighted = pixel_ref[pl.ds(place * BLOCK + index * CHUNK, CHUNK), :] * mismatch
            loss = loss + weighted * mismatch
            high, low = split(weighted * ((STEEP / 2.0) - (STEEP / 2.0) * (wave * wave)))
            g_ref[place % 2, 0, rows, :] = high
            g_ref[place % 2, 1, rows, :] = low
        both = mul(g_ref[place % 2, 0], interp_ref[...])
        reduced = both[:, :SUB] + both[:, SUB:] + mul(g_ref[place % 2, 1], interp_ref[:, :SUB])
        high, low = split(reduced)
        cols = pl.ds(place * BLOCK, BLOCK)
        both = mul(interp_t_ref[0:SUB, cols], jnp.concatenate([high, low], 1))
        k_ref[...] += both[:, :SUB] + both[:, SUB:] + mul(interp_t_low_ref[:, cols], high)
        if place == 0:
            wait_all(rest)
            batches = (listed_ref[0] + BATCH - 1) // BATCH

            def begin(index, carry):
                load(index).start()
                return carry

            lax.fori_loop(0, batches, begin, 0)

    aerial_ref[...] = interpolated(pl.ds(pl.multiple_of(me * ROWS, ROWS), ROWS))
    loss_ref[0] = jnp.sum(loss) / (NPIX * NPIX)
    right_t, left_t, left_t_low = right_t_ref[...], left_t_ref[...], left_t_low_ref[...]
    pupil = pupil_ref[...]
    kernel = k_ref[...]
    common = jnp.sum(kernel * scaled)
    grad_refs[...] = jnp.zeros_like(grad_refs)
    number = slot_numbers()
    lane = lanes_of((KP, KS))
    kernel2 = jnp.concatenate([kernel, kernel], 1)

    def back(index, terms):
        load(index).wait()
        base = index * BATCH
        pulled = []
        for place in range(BATCH):
            piece = field_ref[index, pl.ds(place * SUB, SUB), :]
            cotangent = piece * kernel2
            strength = jnp.sum(piece * cotangent, axis=(0, 1), keepdims=True)
            terms = jnp.where(number == slots_ref[base + place], strength - common, terms)
            pulled.append(cotangent)
        grads = pull_fields(jnp.concatenate(pulled, 0), right_t, left_t, left_t_low)
        for place in range(BATCH):
            scaled_grad = grads[place] * pupil * (2.0 * weights_ref[base + place])
            code = codes_ref[base + place]
            row = code >> 6
            col = code & (KP - 1)
            rows = pl.ds(row, KP)
            grad_refs[0, rows, :] += pltpu.roll(jnp.where(lane < KP, scaled_grad, 0.0), col, 1)
            grad_refs[1, rows, :] += pltpu.roll(jnp.where(lane < KP, 0.0, scaled_grad), col + KP, 1)
        return terms

    terms = lax.fori_loop(0, batches, back, jnp.zeros(number.shape, F32))
    real, imag = grad_refs[0] / total, grad_refs[1] / total
    sub = lax.broadcasted_iota(jnp.int32, (8, KS), 0)
    edge = jnp.where(sub == 0, jnp.transpose(real)[0:1], jnp.transpose(imag)[0:1])
    kept = jnp.zeros((KS, KS), F32)
    mirrored = jnp.zeros((EDGE_ROWS, KS), F32)
    for part in split(jnp.concatenate([real, imag], 1)):
        folded = mul(part, fold_ref[...])
        kept = kept + folded[:, :KS]
        mirrored = mirrored + mul(flip_ref[...], folded[:, KS:].astype(BF16))
    out_ref[0:KS, :] = kept + mirrored[0:KS]
    out_ref[MIRROR_ROW:EDGE_ROWS, :] = mirrored[KS:]
    out_ref[EDGE_ROWS:TERM_ROWS, :] = jnp.where(sub < 2, edge, 0.0)
    blank = jnp.zeros((GRAD - TERM_ROWS - SLOTS // 128, 128), F32)
    out_ref[TERM_ROWS:GRAD, :] = jnp.concatenate([terms / (total * NPIX), blank], 0)


def mask_kernel(*refs):
    packs_hbm, refs = refs[:GROUP], refs[GROUP:]
    (mask_hbm, own_hbm, cols_hbm, out_ref, slot_ref), refs = refs[:5], refs[5:]
    packs, refs = refs[:GROUP], refs[GROUP:]
    mask_ref, own_ref, cols_ref, terms_vmem, terms_smem, sems = refs
    me = lax.axis_index("src")
    copies = start_all(
        tuple(packs_hbm) + (own_hbm.at[me], cols_hbm, mask_hbm), tuple(packs) + (own_ref, cols_ref, mask_ref), sems
    )
    wait_all(copies[:GROUP])
    packed = packs[0][...]
    for ref in packs[1:]:
        packed = packed + ref[...]
    terms_vmem[...] = packed[TERM_ROWS:GRAD]
    fetch = pltpu.make_async_copy(terms_vmem, terms_smem, sems.at[GROUP + 3])
    fetch.start()
    copies[GROUP].wait()
    used = EDGE_ROWS
    pulled = mul3((own_ref[0, :, :used], own_ref[1, :, :used]), split(packed[0:used]))
    sin_part = pltpu.roll(pulled[ROWS:], KS // 2, 1)
    lane = lanes_of((ROWS, KS))
    main = pulled[:ROWS] + jnp.where(lane < KS // 2, -sin_part, sin_part)
    edge = packed[EDGE_ROWS:TERM_ROWS]
    blank = jnp.zeros((KS - 16, KS), F32)
    none = jnp.zeros((8, KS), F32)
    cos_rows = (own_ref[0, :ROWS, :KS], own_ref[1, :ROWS, :KS])
    sin_rows = (own_ref[0, ROWS:, :KS], own_ref[1, ROWS:, :KS])
    contract = ((1,), (1,))
    side = mul3(cos_rows, split(jnp.concatenate([edge, none, blank], 0)), contract) + mul3(
        sin_rows, split(jnp.concatenate([none, edge, blank], 0)), contract
    )
    gathered = split(jnp.concatenate([main, side], 1))
    wait_all(copies[GROUP + 1 :])
    transmit = jnp.tanh(mask_ref[...])
    out_ref[...] = mul3(gathered, pair(cols_ref)) * (1.0 - transmit * transmit)
    fetch.wait()
    for slot in range(CAP):
        place = me * CAP + slot
        slot_ref[slot] = terms_smem[place >> 7, place & 127]


def exchange(value, others):
    received = [value]
    for other in others:
        pairs = [(index, index ^ other) for index in range(SRC)]
        received.append(lax.ppermute(value, "src", pairs))
    return received


MIB = 1024 * 1024


def run(kernel, name, operands, outputs, scratch):
    smem = pl.BlockSpec(memory_space=pltpu.SMEM)
    hbm = pl.BlockSpec(memory_space=pltpu.HBM)
    vmem = pl.BlockSpec(memory_space=pltpu.VMEM)
    kinds = {"smem": smem, "hbm": hbm, "vmem": vmem}
    return pl.pallas_call(
        kernel,
        in_specs=[hbm] * len(operands),
        out_specs=[kinds[kind] for kind, unused, unused in outputs],
        out_shape=[jax.ShapeDtypeStruct(shape, dtype) for unused, shape, dtype in outputs],
        scratch_shapes=scratch,
        compiler_params=pltpu.CompilerParams(vmem_limit_bytes=60 * MIB),
        name=name,
    )(*operands)


def body(mask_param, pixel_weight, source_weight, point_index, point_count, target_rects):
    table = tables()
    vmem = lambda array: pltpu.VMEM(array.shape, array.dtype)
    smem = lambda array: pltpu.SMEM(array.shape, array.dtype)
    dma = lambda count: pltpu.SemaphoreType.DMA((count,))

    (block,) = run(
        project_kernel,
        "project",
        [point_index, point_count, source_weight, mask_param, table["cols"], table["own"]],
        [("vmem", (GATHER, PACK, 128), F32)],
        [
            smem(point_index), smem(point_count), smem(source_weight), vmem(mask_param), vmem(table["cols"]),
            vmem(table["own"][0]), dma(6),
        ],
    )

    same_core = [list(range(core, SRC, 2)) for core in range(2)]
    mine = lax.all_to_all(block, "src", 0, 0, axis_index_groups=same_core, tiled=True)
    unused, other = exchange(mine, CORE)

    operands = [mine, other] + [table[name] for name in IMAGE_TABLES]
    listed = SLOTS // GROUP + BATCH
    sums, codes, weights, slots, count, field = run(
        image_kernel,
        "image",
        operands,
        [
            ("vmem", (SUMS, 128), F32),
            ("smem", (listed,), jnp.int32),
            ("smem", (listed,), F32),
            ("smem", (listed,), jnp.int32),
            ("smem", (1,), jnp.int32),
            ("hbm", (BATCHES, BATCH * SUB, 2 * SUB), F32),
        ],
        [vmem(array) for array in operands]
        + [
            pltpu.VMEM((KS, KS), F32),
            pltpu.VMEM((KS, KS), F32),
            pltpu.VMEM((BATCHES, BATCH * SUB, 2 * SUB), F32),
            pltpu.VMEM((SRC, 128), jnp.int32),
            pltpu.VMEM((SRC, 128), F32),
            pltpu.SMEM((SRC, 128), jnp.int32),
            pltpu.SMEM((SRC, 128), F32),
            dma(11),
            dma(BATCHES),
        ],
    )

    all_sums = exchange(sums, GROUP_DEVICES)
    rects_t = target_rects.T
    lists = [codes, weights, slots, count]
    constants = [table[name] for name in GRAD_TABLES]
    grad, aerial, loss = run(
        grad_kernel,
        "gradient",
        all_sums + [pixel_weight, target_rects, rects_t, field] + lists + constants,
        [("vmem", (GRAD, 128), F32), ("vmem", (ROWS, NPIX), F32), ("smem", (1,), F32)],
        [vmem(array) for array in all_sums + [pixel_weight, target_rects, rects_t, field]]
        + [smem(array) for array in lists]
        + [vmem(array) for array in constants]
        + [
            pltpu.VMEM((SUB, 2 * SUB), BF16),
            pltpu.VMEM((2, BLOCK, NPIX), F32),
            pltpu.VMEM((2, BLOCK, NPIX), F32),
            pltpu.VMEM((2, 2, BLOCK, NPIX), BF16),
            pltpu.VMEM((SUB, SUB), F32),
            pltpu.VMEM((2, KS, KS), F32),
            dma(GROUP + 2 + len(lists) + len(constants)),
            dma(NPIX // BLOCK),
            dma(BATCHES),
        ],
    )

    grads = exchange(grad, GROUP_DEVICES)
    operands = grads + [mask_param, table["own"], table["cols_t"]]
    mask_grad, source_grad = run(
        mask_kernel,
        "mask",
        operands,
        [("vmem", (ROWS, NPIX), F32), ("smem", (CAP,), F32)],
        [vmem(array) for array in grads]
        + [
            vmem(mask_param), vmem(table["own"][0]), vmem(table["cols_t"]), pltpu.VMEM((8, 128), F32),
            pltpu.SMEM((8, 128), F32), dma(GROUP + 4),
        ],
    )
    return mask_grad, aerial, source_grad, loss


def solution(mesh):
    in_specs = (P(("clip", "src"), None), P("clip", None), P(), P("src"), P("src"), P("clip", None))
    out_specs = (P(("clip", "src"), None), P(("clip", "src"), None), P(("clip", "src")), P("clip"))
    return jax.shard_map(body, mesh=mesh, in_specs=in_specs, out_specs=out_specs, check_vma=False)
```

```python
import functools
import math

import jax
import jax.numpy as jnp
import ml_dtypes
import numpy as np
from jax import lax
from jax.experimental import pallas as pl
from jax.experimental.pallas import tpu as pltpu
from jax.sharding import PartitionSpec as P

NPIX = 1024
KS = 128
KP = 64
SG = 101
CAP = 8
SRC = 64
SLOTS = SRC * CAP
ROWS = NPIX // SRC
SUB = 128
BLOCK = 256
CHUNK = 16
STEEP = 10.0
THRESH = 0.3

EDGE = ROWS
META = EDGE + 2
PACK = 24
META_LANES = 32
UNUSED = 3 * CAP
GATHER = 32
SUMS = 136
MIRROR_ROW = KS
EDGE_ROWS = KS + 8
TERM_ROWS = KS + 16
GRAD = KS + 24

CORE = (1,)
GROUP_DEVICES = (1, 32, 33)
GROUP = 4
BATCH = 8
BATCHES = SLOTS // GROUP // BATCH

F32 = jnp.float32
BF16 = jnp.bfloat16


def halves(table):
    table = np.asarray(table, np.float64)
    high = table.astype(ml_dtypes.bfloat16)
    low = (table - high.astype(np.float64)).astype(ml_dtypes.bfloat16)
    return np.stack([high, low])


def angles(left, right, period):
    return 2.0 * math.pi * np.mod(np.multiply.outer(left, right), period) / period


@functools.lru_cache(None)
def tables():
    pixels = np.arange(NPIX)
    cols = np.zeros((NPIX, 2 * KS))
    phase = angles(pixels, np.arange(KS // 2), NPIX)
    cols[:, : KS // 2] = np.cos(phase)
    cols[:, KS // 2 : KS] = -np.sin(phase)
    edge = angles(pixels, -KS // 2, NPIX)
    cols[:, KS] = np.cos(edge)
    cols[:, KS + 1] = -np.sin(edge)
    cols[:, KS + 8] = -np.sin(edge)
    cols[:, KS + 9] = -np.cos(edge)
    cols /= NPIX

    phase = angles(np.arange(KS + 1) - KS // 2, pixels, NPIX).reshape(KS + 1, SRC, ROWS)
    wave = np.stack([np.cos(phase), np.sin(phase)]) / NPIX
    by_core = wave[:, :KS].reshape(2 * KS, GATHER, 2, ROWS).transpose(2, 0, 1, 3)
    waves = by_core.reshape(2, 2 * KS, GATHER * ROWS)
    own = np.zeros((SRC, 2 * ROWS, 2 * KS))
    own[:, :, : KS + 1] = wave.transpose(2, 0, 3, 1).reshape(SRC, 2 * ROWS, KS + 1)

    half = KS // 2
    keep = np.zeros((KS, 2 * KS))
    mirror = np.zeros((KS, 2 * KS))
    for freq in range(half):
        keep[freq, half + freq] = 1.0
        keep[half + freq, KS + half + freq] = 1.0
        if freq:
            mirror[freq, half - freq] = 1.0
            mirror[half + freq, KS + half - freq] = 1.0
    flip = np.zeros((EDGE_ROWS, KS))
    flip[KS - np.arange(KS), np.arange(KS)] = 1.0
    conj = mirror * np.where(np.arange(KS) < half, 1.0, -1.0)[:, None]

    phase = angles(np.arange(KP) - KP // 2, np.arange(SUB), SUB)
    cos_part, sin_part = np.cos(phase), np.sin(phase)
    right = np.block([[cos_part, sin_part], [-sin_part, cos_part]])
    left = np.concatenate([cos_part.T, sin_part.T], 1)

    shift = pixels[:, None] - (NPIX // SUB) * np.arange(SUB)[None, :]
    interp = np.ones((NPIX, SUB))
    for freq in range(1, SUB // 2):
        interp += 2.0 * np.cos(2.0 * math.pi * np.mod(freq * shift, NPIX) / NPIX)
    interp /= SUB

    freq = np.arange(KP) - KP // 2
    pupil = (freq[:, None] ** 2 + freq[None, :] ** 2 < (KP // 2) ** 2).astype(np.float32)
    as_bf16 = lambda table: table.astype(ml_dtypes.bfloat16)
    high_low = lambda table, axis: np.concatenate(list(halves(table)), axis)
    twice = lambda table, axis: np.concatenate([halves(table)[0]] * 2, axis)
    return dict(
        cols=halves(cols),
        cols_t=halves(cols.T),
        waves=halves(waves).transpose(1, 0, 2, 3),
        own=halves(own).transpose(1, 0, 2, 3),
        unfold=as_bf16(np.concatenate([keep, mirror], 0)),
        fold=as_bf16(np.concatenate([keep.T, conj.T], 1)),
        flip=as_bf16(flip),
        right=twice(right, 0),
        right_low=halves(right)[1],
        left=twice(left, 1),
        left_low=halves(left)[1],
        right_t=high_low(right.T, 1),
        left_t=twice(left.T, 1),
        left_t_low=halves(left.T)[1],
        interp=high_low(interp, 1),
        interp_t=twice(interp.T, 0),
        interp_t_low=halves(interp.T)[1],
        pupil=np.concatenate([pupil, pupil], 1),
    )


def split(values):
    high = values.astype(BF16)
    low = (values - high.astype(F32)).astype(BF16)
    return high, low


def mul(first, second, dims=((1,), (0,))):
    return lax.dot_general(first, second, (dims, ((), ())), preferred_element_type=F32)


def mul3(first, second, dims=((1,), (0,))):
    return (
        mul(first[0], second[0], dims) + mul(first[0], second[1], dims) + mul(first[1], second[0], dims)
    )


def mul3_few(first, second):
    rows = first[0].shape[0]
    both = mul(jnp.concatenate(first, 0), second[0])
    return both[:rows] + both[rows:] + mul(first[0], second[1])


def pair(ref):
    return ref[0], ref[1]


def div_sg(number):
    return (number * 41529) >> 22


def offset(grid):
    return ((grid - SG // 2) * (KP // 2) + 51 * 64) // 51 - 64 + KP // 2


def lanes_of(shape):
    return lax.broadcasted_iota(jnp.int32, shape, 1)


def slot_numbers():
    shape = (SLOTS // 128, 128)
    return lax.broadcasted_iota(jnp.int32, shape, 0) * 128 + lanes_of(shape)


def start_all(sources, targets, sems):
    copies = [
        pltpu.make_async_copy(source, target, sems.at[place])
        for place, (source, target) in enumerate(zip(sources, targets))
    ]
    for copy in copies:
        copy.start()
    return copies


def wait_all(copies):
    for copy in copies:
        copy.wait()


def project_kernel(
    index_hbm, count_hbm, weight_hbm, mask_hbm, cols_hbm, own_hbm, out_ref,
    index_ref, count_ref, weight_ref, mask_ref, cols_ref, own_ref, sems,
):
    me = lax.axis_index("src")
    copies = start_all(
        (mask_hbm, cols_hbm, own_hbm.at[me], index_hbm, count_hbm, weight_hbm),
        (mask_ref, cols_ref, own_ref, index_ref, count_ref, weight_ref),
        sems,
    )
    copies[0].wait()
    transmit = split(jnp.tanh(mask_ref[...]))
    copies[1].wait()
    projected = mul3_few(transmit, pair(cols_ref))
    wait_all(copies[2:])
    edge = split(projected[:, KS:])
    cos_rows = (own_ref[0, :ROWS, :KS], own_ref[1, :ROWS, :KS])
    sin_rows = (own_ref[0, ROWS:, :KS], own_ref[1, ROWS:, :KS])
    contract = ((0,), (0,))
    edge_rows = mul3(edge, cos_rows, contract)[0:8] + mul3(edge, sin_rows, contract)[8:16]
    shape = (PACK - EDGE, 128)
    lane = lanes_of(shape)
    sub = lax.broadcasted_iota(jnp.int32, shape, 0)
    count = count_ref[0]
    meta = jnp.where(lane == 2 * CAP, count.astype(F32), 0.0)
    for slot in range(CAP):
        point = index_ref[slot]
        grid_row = div_sg(point)
        grid_col = point - grid_row * SG
        code = offset(grid_row) * KP + offset(grid_col)
        meta = jnp.where(lane == slot, code.astype(F32), meta)
        meta = jnp.where(lane == CAP + slot, weight_ref[grid_row, grid_col], meta)
    tail = jnp.where(sub < 2, edge_rows, jnp.where(sub == 2, meta, 0.0))
    block = jnp.concatenate([projected[:, :KS], tail], 0)
    for place in range(GATHER):
        out_ref[place] = block


def unpack_spectrum(mine_ref, other_ref, waves_ref, core, unfold, re_ref, im_ref):
    total = jnp.zeros((2 * KS, KS), F32)
    edge = jnp.zeros((PACK - EDGE, KS), F32)
    for ref, which in ((mine_ref, core), (other_ref, 1 - core)):
        gathered = ref[...]
        high, low = split(gathered[:, :ROWS].reshape(GATHER * ROWS, KS))
        both = mul(waves_ref[which, 0], jnp.concatenate([high, low], 1))
        total = total + both[:, :KS] + both[:, KS:] + mul(waves_ref[which, 1], high)
        edge = edge + jnp.sum(gathered[:, EDGE:], 0)
    lower = lanes_of((KS, KS)) < KS // 2
    cos_part = total[:KS]
    sin_part = pltpu.roll(total[KS:], KS // 2, 1)
    near = cos_part + jnp.where(lower, sin_part, -sin_part)
    far = jnp.where(lower, cos_part - sin_part, -cos_part - sin_part)
    full = jnp.zeros((KS, 2 * KS), F32)
    for part in split(jnp.concatenate([near, far], 1)):
        full = full + mul(part, unfold)
    column = jnp.transpose(edge)
    lane = lanes_of((KS, KS))
    re_ref[...] = jnp.where(lane == 0, column[:, 0:1], full[:, :KS])
    im_ref[...] = jnp.where(lane == 0, column[:, 1:2], full[:, KS:])


def list_slots(rank, core, meta_ref, list_ref):
    listed = jnp.int32(0)
    before = jnp.int32(0)
    for index in range(SRC):
        row = (index >> 1) + ((index + core) & 1) * GATHER
        count = meta_ref[row, 2 * CAP].astype(jnp.int32)
        first = (rank - before) & (GROUP - 1)
        for turn in range(CAP // GROUP):
            position = first + turn * GROUP
            list_ref[listed] = row * META_LANES + position
            listed = listed + jnp.where(position < count, 1, 0)
        before = before + count
    for extra in range(BATCH):
        list_ref[listed + extra] = UNUSED
    return listed


def window(code, re_ref, im_ref, pupil):
    row = code >> 6
    col = code & (KP - 1)
    rows = pl.ds(row, KP)
    real = pltpu.roll(re_ref[rows, :], (KS - col) & (KS - 1), 1)
    imag = pltpu.roll(im_ref[rows, :], KP - col, 1)
    return jnp.where(lanes_of((KP, KS)) < KP, real, imag) * pupil


def swapped(window_values):
    sign = jnp.where(lanes_of(window_values.shape) < KP, -1.0, 1.0)
    return pltpu.roll(window_values, KP, 1) * sign


def side_by_side(values, height):
    return jnp.concatenate(
        [values[place * height : (place + 1) * height] for place in range(values.shape[0] // height)], 1
    )


def on_top(values, width):
    return jnp.concatenate(
        [values[:, place * width : (place + 1) * width] for place in range(values.shape[1] // width)], 0
    )


def left_transform(masked, left, left_low):
    parts = [split(jnp.concatenate([piece, swapped(piece)], 0)) for piece in masked]
    high = jnp.concatenate([part[0] for part in parts], 1)
    low = jnp.concatenate([part[1] for part in parts], 1)
    inner = mul(left, jnp.concatenate([high, low], 0)) + mul(left_low, high)
    return jnp.concatenate(split(on_top(inner, KS)), 1)


def right_transform(inner, right, right_low):
    return mul(inner, right) + mul(inner[:, :KS], right_low)


def pull_right(cotangent, right_t):
    high, low = split(cotangent)
    both = mul(high, right_t)
    inner = both[:, :KS] + both[:, KS:] + mul(low, right_t[:, :KS])
    return jnp.concatenate(split(side_by_side(inner, SUB)), 0)


def pull_left(inner, left_t, left_t_low):
    pulled = mul(left_t, inner) + mul(left_t_low, inner[:SUB])
    grads = []
    for place in range(BATCH):
        piece = pulled[:, place * KS : (place + 1) * KS]
        grads.append(piece[:KP] - swapped(piece[KP:]))
    return grads


IMAGE_TABLES = ("waves", "unfold", "right", "right_low", "left", "left_low", "pupil")


def image_kernel(*refs):
    inputs, refs = refs[:9], refs[9:]
    (out_ref, codes_out, weights_out, slots_out, listed_out, field_out), refs = refs[:6], refs[6:]
    buffers, refs = refs[:9], refs[9:]
    re_ref, im_ref, field_ref, inner_ref, meta_ref, list_ref, sems, field_sems = refs
    mine_ref, other_ref, waves_ref, unfold_ref, right_ref, right_low_ref, left_ref, left_low_ref, pupil_ref = buffers
    me = lax.axis_index("src")
    core = me & 1
    metas = [
        pltpu.make_async_copy(
            inputs[place].at[:, META], meta_ref.at[pl.ds(place * GATHER, GATHER)], sems.at[len(inputs) + place]
        )
        for place in range(2)
    ]
    for copy in metas:
        copy.start()
    copies = start_all(inputs, buffers, sems)
    wait_all(metas + copies)
    rank = core + 2 * (me >> 5)
    listed = list_slots(rank, core, meta_ref, list_ref)
    listed_out[0] = listed
    unpack_spectrum(mine_ref, other_ref, waves_ref, core, unfold_ref[...], re_ref, im_ref)
    right, right_low, left, left_low = right_ref[...], right_low_ref[...], left_ref[...], left_low_ref[...]
    pupil = pupil_ref[...]
    out_ref[...] = jnp.zeros_like(out_ref)
    batches = (listed + BATCH - 1) // BATCH

    def store(index):
        return pltpu.make_async_copy(field_ref.at[index], field_out.at[index], field_sems.at[index])

    def first_stage(index):
        masked = []
        for place in range(BATCH):
            position = index * BATCH + place
            where = list_ref[position]
            row, lane = where >> 5, where & (META_LANES - 1)
            code = meta_ref[row, lane].astype(jnp.int32)
            codes_out[position] = code
            weights_out[position] = meta_ref[row, CAP + lane]
            source = 2 * (row & (GATHER - 1)) + ((core + (row >> 5)) & 1)
            slots_out[position] = jnp.where(lane == UNUSED, -1, source * CAP + lane)
            masked.append(window(code, re_ref, im_ref, pupil))
        inner_ref[...] = left_transform(masked, left, left_low)

    def step(index, total):
        base = index * BATCH
        values = right_transform(inner_ref[...], right, right_low)
        field_ref[index] = values
        store(index).start()
        acc = out_ref[0:SUB, :]
        for place in range(BATCH):
            weight = weights_out[base + place]
            piece = values[place * SUB : (place + 1) * SUB]
            squares = piece * piece
            acc = acc + weight * (squares[:, :SUB] + squares[:, SUB:])
            total = total + weight
        out_ref[0:SUB, :] = acc
        first_stage(jnp.minimum(index + 1, batches - 1))
        return total

    first_stage(0)
    total = lax.fori_loop(0, batches, step, jnp.float32(0.0))
    out_ref[SUB:SUMS, :] = jnp.full((SUMS - SUB, 128), total, F32)

    def finish(index, carry):
        store(index).wait()
        return carry

    lax.fori_loop(0, batches, finish, 0)


GRAD_TABLES = (
    "interp", "interp_t", "interp_t_low", "right_t", "left_t", "left_t_low", "fold", "flip", "pupil",
)


def grad_kernel(*refs):
    sums_hbm, refs = refs[:GROUP], refs[GROUP:]
    (pixel_hbm, rects_hbm, rects_t_hbm, field_hbm), refs = refs[:4], refs[4:]
    lists_hbm, refs = refs[:4], refs[4:]
    tabs_hbm, refs = refs[: len(GRAD_TABLES)], refs[len(GRAD_TABLES) :]
    (out_ref, aerial_ref, loss_ref), refs = refs[:3], refs[3:]
    sums, refs = refs[:GROUP], refs[GROUP:]
    (pixel_ref, rects_ref, rects_t_ref, field_ref), refs = refs[:4], refs[4:]
    lists, refs = refs[:4], refs[4:]
    tabs, refs = refs[: len(GRAD_TABLES)], refs[len(GRAD_TABLES) :]
    image_ref, aer_ref, cnt_ref, g_ref, k_ref, grad_refs, inner_ref, sems, pixel_sems, field_sems = refs
    (
        interp_ref, interp_t_ref, interp_t_low_ref, right_t_ref, left_t_ref, left_t_low_ref, fold_ref,
        flip_ref, pupil_ref,
    ) = tabs
    codes_ref, weights_ref, slots_ref, listed_ref = lists
    me = lax.axis_index("src")
    blocks = NPIX // BLOCK

    firsts = start_all(
        tuple(sums_hbm) + (rects_hbm, rects_t_hbm) + tuple(tabs_hbm[:3]),
        tuple(sums) + (rects_ref, rects_t_ref) + tuple(tabs[:3]),
        sems,
    )
    pixel_copies = [
        pltpu.make_async_copy(
            pixel_hbm.at[pl.ds(place * BLOCK, BLOCK)], pixel_ref.at[pl.ds(place * BLOCK, BLOCK)], pixel_sems.at[place]
        )
        for place in range(blocks)
    ]
    for copy in pixel_copies:
        copy.start()
    begun = len(firsts)
    rest = [
        pltpu.make_async_copy(source, target, sems.at[begun + place])
        for place, (source, target) in enumerate(
            zip(tuple(lists_hbm) + tuple(tabs_hbm[3:]), tuple(lists) + tuple(tabs[3:]))
        )
    ]
    for copy in rest:
        copy.start()

    def load(index):
        return pltpu.make_async_copy(field_hbm.at[index], field_ref.at[index], field_sems.at[index])

    wait_all(firsts)
    image = sums[0][...]
    for ref in sums[1:]:
        image = image + ref[...]
    total = image[SUB : SUB + 1, 0:1]
    scaled = image[0:SUB] / total
    image_ref[...] = jnp.concatenate(split(scaled), 1)

    def interpolated(rows):
        table = interp_ref[rows, :]
        both = mul(table[:, :SUB], image_ref[...])
        half = both[:, :SUB] + both[:, SUB:] + mul(table[:, SUB:], image_ref[:, :SUB])
        high, low = split(half)
        return mul(jnp.concatenate([high, low], 1), interp_t_ref[...]) + mul(high, interp_t_low_ref[...])

    col = lax.broadcasted_iota(jnp.int32, (128, NPIX), 1)
    col_in = ((col >= rects_ref[:, 2:3]) & (col < rects_ref[:, 3:4])).astype(F32).astype(BF16)

    def prepare(place):
        first = place * BLOCK
        aer_ref[place % 2] = interpolated(pl.ds(first, BLOCK))
        row = lax.broadcasted_iota(jnp.int32, (BLOCK, 128), 0) + first
        row_in = ((row >= rects_t_ref[0:1, :]) & (row < rects_t_ref[1:2, :])).astype(F32).astype(BF16)
        cnt_ref[place % 2] = mul(row_in, col_in)

    loss = jnp.zeros((CHUNK, NPIX), F32)
    k_ref[...] = jnp.zeros_like(k_ref)
    prepare(0)
    for place in range(blocks):
        if place + 1 < blocks:
            prepare(place + 1)
        pixel_copies[place].wait()
        for index in range(BLOCK // CHUNK):
            rows = pl.ds(index * CHUNK, CHUNK)
            wave = jnp.tanh((STEEP / 2.0) * aer_ref[place % 2, rows, :] - (STEEP * THRESH / 2.0))
            mismatch = 0.5 * wave + (0.5 - jnp.minimum(cnt_ref[place % 2, rows, :], 1.0))
            weighted = pixel_ref[pl.ds(place * BLOCK + index * CHUNK, CHUNK), :] * mismatch
            loss = loss + weighted * mismatch
            high, low = split(weighted * ((STEEP / 2.0) - (STEEP / 2.0) * (wave * wave)))
            g_ref[place % 2, 0, rows, :] = high
            g_ref[place % 2, 1, rows, :] = low
        both = mul(g_ref[place % 2, 0], interp_ref[...])
        reduced = both[:, :SUB] + both[:, SUB:] + mul(g_ref[place % 2, 1], interp_ref[:, :SUB])
        high, low = split(reduced)
        cols = pl.ds(place * BLOCK, BLOCK)
        both = mul(interp_t_ref[0:SUB, cols], jnp.concatenate([high, low], 1))
        k_ref[...] += both[:, :SUB] + both[:, SUB:] + mul(interp_t_low_ref[:, cols], high)
        if place == 0:
            wait_all(rest)
            batches = (listed_ref[0] + BATCH - 1) // BATCH

            def begin(index, carry):
                load(index).start()
                return carry

            lax.fori_loop(0, batches, begin, 0)

    aerial_ref[...] = interpolated(pl.ds(pl.multiple_of(me * ROWS, ROWS), ROWS))
    loss_ref[0] = jnp.sum(loss) / (NPIX * NPIX)
    right_t, left_t, left_t_low = right_t_ref[...], left_t_ref[...], left_t_low_ref[...]
    pupil = pupil_ref[...]
    kernel = k_ref[...]
    common = jnp.sum(kernel * scaled)
    grad_refs[...] = jnp.zeros_like(grad_refs)
    number = slot_numbers()
    lane = lanes_of((KP, KS))
    kernel2 = jnp.concatenate([kernel, kernel], 1)

    def finish_load(index, carry):
        load(index).wait()
        return carry

    lax.fori_loop(0, batches, finish_load, 0)

    def first_stage(index, terms):
        cotangents = []
        for place in range(BATCH):
            piece = field_ref[index, pl.ds(place * SUB, SUB), :]
            cotangent = piece * kernel2
            strength = jnp.sum(piece * cotangent, axis=(0, 1), keepdims=True)
            terms = jnp.where(number == slots_ref[index * BATCH + place], strength - common, terms)
            cotangents.append(cotangent)
        inner_ref[...] = pull_right(jnp.concatenate(cotangents, 0), right_t)
        return terms

    def back(index, terms):
        grads = pull_left(inner_ref[...], left_t, left_t_low)
        for place in range(BATCH):
            scaled_grad = grads[place] * pupil * (2.0 * weights_ref[index * BATCH + place])
            code = codes_ref[index * BATCH + place]
            row = code >> 6
            col = code & (KP - 1)
            rows = pl.ds(row, KP)
            grad_refs[0, rows, :] += pltpu.roll(jnp.where(lane < KP, scaled_grad, 0.0), col, 1)
            grad_refs[1, rows, :] += pltpu.roll(jnp.where(lane < KP, 0.0, scaled_grad), col + KP, 1)
        return first_stage(jnp.minimum(index + 1, batches - 1), terms)

    terms = first_stage(0, jnp.zeros(number.shape, F32))
    terms = lax.fori_loop(0, batches, back, terms)
    real, imag = grad_refs[0] / total, grad_refs[1] / total
    sub = lax.broadcasted_iota(jnp.int32, (8, KS), 0)
    edge = jnp.where(sub == 0, jnp.transpose(real)[0:1], jnp.transpose(imag)[0:1])
    kept = jnp.zeros((KS, KS), F32)
    mirrored = jnp.zeros((EDGE_ROWS, KS), F32)
    for part in split(jnp.concatenate([real, imag], 1)):
        folded = mul(part, fold_ref[...])
        kept = kept + folded[:, :KS]
        mirrored = mirrored + mul(flip_ref[...], folded[:, KS:].astype(BF16))
    out_ref[0:KS, :] = kept + mirrored[0:KS]
    out_ref[MIRROR_ROW:EDGE_ROWS, :] = mirrored[KS:]
    out_ref[EDGE_ROWS:TERM_ROWS, :] = jnp.where(sub < 2, edge, 0.0)
    blank = jnp.zeros((GRAD - TERM_ROWS - SLOTS // 128, 128), F32)
    out_ref[TERM_ROWS:GRAD, :] = jnp.concatenate([terms / (total * NPIX), blank], 0)


def mask_kernel(*refs):
    packs_hbm, refs = refs[:GROUP], refs[GROUP:]
    (mask_hbm, own_hbm, cols_hbm, out_ref, slot_ref), refs = refs[:5], refs[5:]
    packs, refs = refs[:GROUP], refs[GROUP:]
    mask_ref, own_ref, cols_ref, terms_vmem, terms_smem, sems = refs
    me = lax.axis_index("src")
    copies = start_all(
        tuple(packs_hbm) + (own_hbm.at[me], cols_hbm, mask_hbm), tuple(packs) + (own_ref, cols_ref, mask_ref), sems
    )
    wait_all(copies[:GROUP])
    packed = packs[0][...]
    for ref in packs[1:]:
        packed = packed + ref[...]
    terms_vmem[...] = packed[TERM_ROWS:GRAD]
    fetch = pltpu.make_async_copy(terms_vmem, terms_smem, sems.at[GROUP + 3])
    fetch.start()
    copies[GROUP].wait()
    used = EDGE_ROWS
    pulled = mul3((own_ref[0, :, :used], own_ref[1, :, :used]), split(packed[0:used]))
    sin_part = pltpu.roll(pulled[ROWS:], KS // 2, 1)
    lane = lanes_of((ROWS, KS))
    main = pulled[:ROWS] + jnp.where(lane < KS // 2, -sin_part, sin_part)
    edge = packed[EDGE_ROWS:TERM_ROWS]
    blank = jnp.zeros((KS - 16, KS), F32)
    none = jnp.zeros((8, KS), F32)
    cos_rows = (own_ref[0, :ROWS, :KS], own_ref[1, :ROWS, :KS])
    sin_rows = (own_ref[0, ROWS:, :KS], own_ref[1, ROWS:, :KS])
    contract = ((1,), (1,))
    side = mul3(cos_rows, split(jnp.concatenate([edge, none, blank], 0)), contract) + mul3(
        sin_rows, split(jnp.concatenate([none, edge, blank], 0)), contract
    )
    gathered = split(jnp.concatenate([main, side], 1))
    wait_all(copies[GROUP + 1 :])
    transmit = jnp.tanh(mask_ref[...])
    out_ref[...] = mul3_few(gathered, pair(cols_ref)) * (1.0 - transmit * transmit)
    fetch.wait()
    for slot in range(CAP):
        place = me * CAP + slot
        slot_ref[slot] = terms_smem[place >> 7, place & 127]


def exchange(value, others):
    received = [value]
    for other in others:
        pairs = [(index, index ^ other) for index in range(SRC)]
        received.append(lax.ppermute(value, "src", pairs))
    return received


MIB = 1024 * 1024


def run(kernel, name, operands, outputs, scratch):
    smem = pl.BlockSpec(memory_space=pltpu.SMEM)
    hbm = pl.BlockSpec(memory_space=pltpu.HBM)
    vmem = pl.BlockSpec(memory_space=pltpu.VMEM)
    kinds = {"smem": smem, "hbm": hbm, "vmem": vmem}
    return pl.pallas_call(
        kernel,
        in_specs=[hbm] * len(operands),
        out_specs=[kinds[kind] for kind, unused, unused in outputs],
        out_shape=[jax.ShapeDtypeStruct(shape, dtype) for unused, shape, dtype in outputs],
        scratch_shapes=scratch,
        compiler_params=pltpu.CompilerParams(vmem_limit_bytes=60 * MIB),
        name=name,
    )(*operands)


def body(mask_param, pixel_weight, source_weight, point_index, point_count, target_rects):
    table = tables()
    vmem = lambda array: pltpu.VMEM(array.shape, array.dtype)
    smem = lambda array: pltpu.SMEM(array.shape, array.dtype)
    dma = lambda count: pltpu.SemaphoreType.DMA((count,))

    (block,) = run(
        project_kernel,
        "project",
        [point_index, point_count, source_weight, mask_param, table["cols"], table["own"]],
        [("vmem", (GATHER, PACK, 128), F32)],
        [
            smem(point_index), smem(point_count), smem(source_weight), vmem(mask_param), vmem(table["cols"]),
            vmem(table["own"][0]), dma(6),
        ],
    )

    same_core = [list(range(core, SRC, 2)) for core in range(2)]
    mine = lax.all_to_all(block, "src", 0, 0, axis_index_groups=same_core, tiled=True)
    unused, other = exchange(mine, CORE)

    operands = [mine, other] + [table[name] for name in IMAGE_TABLES]
    listed = SLOTS // GROUP + BATCH
    sums, codes, weights, slots, count, field = run(
        image_kernel,
        "image",
        operands,
        [
            ("vmem", (SUMS, 128), F32),
            ("smem", (listed,), jnp.int32),
            ("smem", (listed,), F32),
            ("smem", (listed,), jnp.int32),
            ("smem", (1,), jnp.int32),
            ("hbm", (BATCHES, BATCH * SUB, 2 * SUB), F32),
        ],
        [vmem(array) for array in operands]
        + [
            pltpu.VMEM((KS, KS), F32),
            pltpu.VMEM((KS, KS), F32),
            pltpu.VMEM((BATCHES, BATCH * SUB, 2 * SUB), F32),
            pltpu.VMEM((BATCH * SUB, 2 * KS), BF16),
            pltpu.SMEM((SRC, 128), F32),
            pltpu.SMEM((listed,), jnp.int32),
            dma(11),
            dma(BATCHES),
        ],
    )

    all_sums = exchange(sums, GROUP_DEVICES)
    rects_t = target_rects.T
    lists = [codes, weights, slots, count]
    constants = [table[name] for name in GRAD_TABLES]
    grad, aerial, loss = run(
        grad_kernel,
        "gradient",
        all_sums + [pixel_weight, target_rects, rects_t, field] + lists + constants,
        [("vmem", (GRAD, 128), F32), ("vmem", (ROWS, NPIX), F32), ("smem", (1,), F32)],
        [vmem(array) for array in all_sums + [pixel_weight, target_rects, rects_t, field]]
        + [smem(array) for array in lists]
        + [vmem(array) for array in constants]
        + [
            pltpu.VMEM((SUB, 2 * SUB), BF16),
            pltpu.VMEM((2, BLOCK, NPIX), F32),
            pltpu.VMEM((2, BLOCK, NPIX), F32),
            pltpu.VMEM((2, 2, BLOCK, NPIX), BF16),
            pltpu.VMEM((SUB, SUB), F32),
            pltpu.VMEM((2, KS, KS), F32),
            pltpu.VMEM((2 * SUB, BATCH * KS), BF16),
            dma(GROUP + 2 + len(lists) + len(constants)),
            dma(NPIX // BLOCK),
            dma(BATCHES),
        ],
    )

    grads = exchange(grad, GROUP_DEVICES)
    operands = grads + [mask_param, table["own"], table["cols_t"]]
    mask_grad, source_grad = run(
        mask_kernel,
        "mask",
        operands,
        [("vmem", (ROWS, NPIX), F32), ("smem", (CAP,), F32)],
        [vmem(array) for array in grads]
        + [
            vmem(mask_param), vmem(table["own"][0]), vmem(table["cols_t"]), pltpu.VMEM((8, 128), F32),
            pltpu.SMEM((8, 128), F32), dma(GROUP + 4),
        ],
    )
    return mask_grad, aerial, source_grad, loss


def solution(mesh):
    in_specs = (P(("clip", "src"), None), P("clip", None), P(), P("src"), P("src"), P("clip", None))
    out_specs = (P(("clip", "src"), None), P(("clip", "src"), None), P(("clip", "src")), P("clip"))
    return jax.shard_map(body, mesh=mesh, in_specs=in_specs, out_specs=out_specs, check_vma=False)
```

```python
import functools
import math

import jax
import jax.numpy as jnp
import ml_dtypes
import numpy as np
from jax import lax
from jax.experimental import pallas as pl
from jax.experimental.pallas import tpu as pltpu
from jax.sharding import PartitionSpec as P

NPIX = 1024
KS = 128
KP = 64
SG = 101
CAP = 8
SRC = 64
SLOTS = SRC * CAP
ROWS = NPIX // SRC
SUB = 128
BLOCK = 256
CHUNK = 16
STEEP = 10.0
THRESH = 0.3

EDGE = ROWS
META = EDGE + 2
PACK = 24
META_LANES = 32
UNUSED = 3 * CAP
GATHER = 32
SUMS = 136
MIRROR_ROW = KS
EDGE_ROWS = KS + 8
TERM_ROWS = KS + 16
GRAD = KS + 24

CORE = (1,)
GROUP_DEVICES = (1, 32, 33)
GROUP = 4
BATCH = 8
BATCHES = SLOTS // GROUP // BATCH

F32 = jnp.float32
BF16 = jnp.bfloat16


def halves(table):
    table = np.asarray(table, np.float64)
    high = table.astype(ml_dtypes.bfloat16)
    low = (table - high.astype(np.float64)).astype(ml_dtypes.bfloat16)
    return np.stack([high, low])


def angles(left, right, period):
    return 2.0 * math.pi * np.mod(np.multiply.outer(left, right), period) / period


@functools.lru_cache(None)
def tables():
    pixels = np.arange(NPIX)
    cols = np.zeros((NPIX, 2 * KS))
    phase = angles(pixels, np.arange(KS // 2), NPIX)
    cols[:, : KS // 2] = np.cos(phase)
    cols[:, KS // 2 : KS] = -np.sin(phase)
    edge = angles(pixels, -KS // 2, NPIX)
    cols[:, KS] = np.cos(edge)
    cols[:, KS + 1] = -np.sin(edge)
    cols[:, KS + 8] = -np.sin(edge)
    cols[:, KS + 9] = -np.cos(edge)
    cols /= NPIX

    phase = angles(np.arange(KS + 1) - KS // 2, pixels, NPIX).reshape(KS + 1, SRC, ROWS)
    wave = np.stack([np.cos(phase), np.sin(phase)]) / NPIX
    by_core = wave[:, :KS].reshape(2 * KS, GATHER, 2, ROWS).transpose(2, 0, 1, 3)
    waves = by_core.reshape(2, 2 * KS, GATHER * ROWS)
    own = np.zeros((SRC, 2 * ROWS, 2 * KS))
    own[:, :, : KS + 1] = wave.transpose(2, 0, 3, 1).reshape(SRC, 2 * ROWS, KS + 1)

    half = KS // 2
    keep = np.zeros((KS, 2 * KS))
    mirror = np.zeros((KS, 2 * KS))
    for freq in range(half):
        keep[freq, half + freq] = 1.0
        keep[half + freq, KS + half + freq] = 1.0
        if freq:
            mirror[freq, half - freq] = 1.0
            mirror[half + freq, KS + half - freq] = 1.0
    flip = np.zeros((EDGE_ROWS, KS))
    flip[KS - np.arange(KS), np.arange(KS)] = 1.0
    conj = mirror * np.where(np.arange(KS) < half, 1.0, -1.0)[:, None]

    phase = angles(np.arange(KP) - KP // 2, np.arange(SUB), SUB)
    cos_part, sin_part = np.cos(phase), np.sin(phase)
    right = np.block([[cos_part, sin_part], [-sin_part, cos_part]])

    shift = pixels[: NPIX // 2, None] - (NPIX // SUB) * np.arange(SUB // 2)[None, :]
    interp = np.zeros((2, NPIX // 2, SUB // 2))
    interp[0] = 1.0
    for freq in range(1, SUB // 2):
        interp[freq % 2] += 2.0 * np.cos(2.0 * math.pi * np.mod(freq * shift, NPIX) / NPIX)
    interp /= SUB

    freq = np.arange(KP) - KP // 2
    pupil = (freq[:, None] ** 2 + freq[None, :] ** 2 < (KP // 2) ** 2).astype(np.float32)
    as_bf16 = lambda table: table.astype(ml_dtypes.bfloat16)
    high_low = lambda table, axis: np.concatenate(list(halves(table)), axis)
    twice = lambda table, axis: np.concatenate([halves(table)[0]] * 2, axis)
    return dict(
        cols=halves(cols),
        cols_t=halves(cols.T),
        waves=halves(waves).transpose(1, 0, 2, 3),
        own=halves(own).transpose(1, 0, 2, 3),
        unfold=as_bf16(np.concatenate([keep, mirror], 0)),
        fold=as_bf16(np.concatenate([keep.T, conj.T], 1)),
        flip=as_bf16(flip),
        right=twice(right, 0),
        right_low=halves(right)[1],
        right_t=high_low(right.T, 1),
        interp=high_low(interp, 2),
        interp_t=high_low(interp.transpose(0, 2, 1), 1),
        pupil=np.concatenate([pupil, pupil], 1),
    )


def split(values):
    high = values.astype(BF16)
    low = (values - high.astype(F32)).astype(BF16)
    return high, low


def mul(first, second, dims=((1,), (0,))):
    return lax.dot_general(first, second, (dims, ((), ())), preferred_element_type=F32)


def mul3(first, second, dims=((1,), (0,))):
    return (
        mul(first[0], second[0], dims) + mul(first[0], second[1], dims) + mul(first[1], second[0], dims)
    )


def mul3_few(first, second):
    rows = first[0].shape[0]
    both = mul(jnp.concatenate(first, 0), second[0])
    return both[:rows] + both[rows:] + mul(first[0], second[1])


def pair(ref):
    return ref[0], ref[1]


def div_sg(number):
    return (number * 41529) >> 22


def offset(grid):
    return ((grid - SG // 2) * (KP // 2) + 51 * 64) // 51 - 64 + KP // 2


def lanes_of(shape):
    return lax.broadcasted_iota(jnp.int32, shape, 1)


def slot_numbers():
    shape = (SLOTS // 128, 128)
    return lax.broadcasted_iota(jnp.int32, shape, 0) * 128 + lanes_of(shape)


def start_all(sources, targets, sems):
    copies = [
        pltpu.make_async_copy(source, target, sems.at[place])
        for place, (source, target) in enumerate(zip(sources, targets))
    ]
    for copy in copies:
        copy.start()
    return copies


def wait_all(copies):
    for copy in copies:
        copy.wait()


def project_kernel(
    index_hbm, count_hbm, weight_hbm, mask_hbm, cols_hbm, own_hbm, out_ref,
    index_ref, count_ref, weight_ref, mask_ref, cols_ref, own_ref, sems,
):
    me = lax.axis_index("src")
    copies = start_all(
        (mask_hbm, cols_hbm, own_hbm.at[me], index_hbm, count_hbm, weight_hbm),
        (mask_ref, cols_ref, own_ref, index_ref, count_ref, weight_ref),
        sems,
    )
    copies[0].wait()
    transmit = split(jnp.tanh(mask_ref[...]))
    copies[1].wait()
    projected = mul3_few(transmit, pair(cols_ref))
    wait_all(copies[2:])
    edge = split(projected[:, KS:])
    cos_rows = (own_ref[0, :ROWS, :KS], own_ref[1, :ROWS, :KS])
    sin_rows = (own_ref[0, ROWS:, :KS], own_ref[1, ROWS:, :KS])
    contract = ((0,), (0,))
    edge_rows = mul3(edge, cos_rows, contract)[0:8] + mul3(edge, sin_rows, contract)[8:16]
    shape = (PACK - EDGE, 128)
    lane = lanes_of(shape)
    sub = lax.broadcasted_iota(jnp.int32, shape, 0)
    count = count_ref[0]
    meta = jnp.where(lane == 2 * CAP, count.astype(F32), 0.0)
    for slot in range(CAP):
        point = index_ref[slot]
        grid_row = div_sg(point)
        grid_col = point - grid_row * SG
        code = offset(grid_row) * KP + offset(grid_col)
        meta = jnp.where(lane == slot, code.astype(F32), meta)
        meta = jnp.where(lane == CAP + slot, weight_ref[grid_row, grid_col], meta)
    tail = jnp.where(sub < 2, edge_rows, jnp.where(sub == 2, meta, 0.0))
    block = jnp.concatenate([projected[:, :KS], tail], 0)
    for place in range(GATHER):
        out_ref[place] = block


def unpack_spectrum(mine_ref, other_ref, waves_ref, core, unfold, re_ref, im_ref):
    total = jnp.zeros((2 * KS, KS), F32)
    edge = jnp.zeros((PACK - EDGE, KS), F32)
    for ref, which in ((mine_ref, core), (other_ref, 1 - core)):
        gathered = ref[...]
        high, low = split(gathered[:, :ROWS].reshape(GATHER * ROWS, KS))
        both = mul(waves_ref[which, 0], jnp.concatenate([high, low], 1))
        total = total + both[:, :KS] + both[:, KS:] + mul(waves_ref[which, 1], high)
        edge = edge + jnp.sum(gathered[:, EDGE:], 0)
    lower = lanes_of((KS, KS)) < KS // 2
    cos_part = total[:KS]
    sin_part = pltpu.roll(total[KS:], KS // 2, 1)
    near = cos_part + jnp.where(lower, sin_part, -sin_part)
    far = jnp.where(lower, cos_part - sin_part, -cos_part - sin_part)
    full = jnp.zeros((KS, 2 * KS), F32)
    for part in split(jnp.concatenate([near, far], 1)):
        full = full + mul(part, unfold)
    column = jnp.transpose(edge)
    lane = lanes_of((KS, KS))
    re_ref[...] = jnp.transpose(jnp.where(lane == 0, column[:, 0:1], full[:, :KS]))
    im_ref[...] = jnp.transpose(jnp.where(lane == 0, column[:, 1:2], full[:, KS:]))


def list_slots(rank, core, meta_ref, list_ref):
    listed = jnp.int32(0)
    before = jnp.int32(0)
    for index in range(SRC):
        row = (index >> 1) + ((index + core) & 1) * GATHER
        count = meta_ref[row, 2 * CAP].astype(jnp.int32)
        first = (rank - before) & (GROUP - 1)
        for turn in range(CAP // GROUP):
            position = first + turn * GROUP
            list_ref[listed] = row * META_LANES + position
            listed = listed + jnp.where(position < count, 1, 0)
        before = before + count
    for extra in range(BATCH):
        list_ref[listed + extra] = UNUSED
    return listed


def window(code, re_ref, im_ref, pupil):
    first = code >> 6
    rows = pl.ds(code & (KP - 1), KP)
    real = pltpu.roll(re_ref[rows, :], (KS - first) & (KS - 1), 1)
    imag = pltpu.roll(im_ref[rows, :], KP - first, 1)
    return jnp.where(lanes_of((KP, KS)) < KP, real, imag) * pupil


def transform(high, low, right, right_low):
    return mul(jnp.concatenate([high, low], 1), right) + mul(high, right_low)


def pull(high, low, right_t):
    both = mul(high, right_t)
    return both[:, :KS] + both[:, KS:] + mul(low, right_t[:, :KS])


def turn(values):
    pieces = [values[place * KP : (place + 1) * KP] for place in range(values.shape[0] // KP)]
    return jnp.concatenate(
        [jnp.transpose(jnp.concatenate([piece[:, :SUB], piece[:, SUB:]], 0)) for piece in pieces], 0
    )


def turn_back(values):
    turned = [jnp.transpose(values[place * SUB : (place + 1) * SUB]) for place in range(values.shape[0] // SUB)]
    return jnp.concatenate([jnp.concatenate([piece[:KP], piece[KP:]], 1) for piece in turned], 0)


IMAGE_TABLES = ("waves", "unfold", "right", "right_low", "pupil")


def image_kernel(*refs):
    inputs, refs = refs[:7], refs[7:]
    (sums_out, codes_out, weights_out, slots_out, listed_out, field_out), refs = refs[:6], refs[6:]
    buffers, refs = refs[:7], refs[7:]
    out_ref, re_ref, im_ref, field_ref, inner_ref, meta_ref, list_ref, sems, field_sems = refs
    mine_ref, other_ref, waves_ref, unfold_ref, right_ref, right_low_ref, pupil_ref = buffers
    me = lax.axis_index("src")
    core = me & 1
    metas = [
        pltpu.make_async_copy(
            inputs[place].at[:, META], meta_ref.at[pl.ds(place * GATHER, GATHER)], sems.at[len(inputs) + place]
        )
        for place in range(2)
    ]
    for copy in metas:
        copy.start()
    copies = start_all(inputs, buffers, sems)
    wait_all(metas + copies)
    rank = core + 2 * (me >> 5)
    listed = list_slots(rank, core, meta_ref, list_ref)
    listed_out[0] = listed
    unpack_spectrum(mine_ref, other_ref, waves_ref, core, unfold_ref[...], re_ref, im_ref)
    right, right_low = right_ref[...], right_low_ref[...]
    pupil = pupil_ref[...]
    out_ref[...] = jnp.zeros_like(out_ref)
    batches = (listed + BATCH - 1) // BATCH

    def store(index):
        return pltpu.make_async_copy(field_ref.at[index], field_out.at[index], field_sems.at[index])

    def first_stage(index):
        masked = []
        for place in range(BATCH):
            position = index * BATCH + place
            where = list_ref[position]
            row, lane = where >> 5, where & (META_LANES - 1)
            code = meta_ref[row, lane].astype(jnp.int32)
            codes_out[position] = code
            weights_out[position] = meta_ref[row, CAP + lane]
            source = 2 * (row & (GATHER - 1)) + ((core + (row >> 5)) & 1)
            slots_out[position] = jnp.where(lane == UNUSED, -1, source * CAP + lane)
            masked.append(window(code, re_ref, im_ref, pupil))
        values = transform(*split(jnp.concatenate(masked, 0)), right, right_low)
        inner_ref[0], inner_ref[1] = split(turn(values))

    def step(index, total):
        base = index * BATCH
        values = transform(inner_ref[0], inner_ref[1], right, right_low)
        field_ref[index] = values
        store(index).start()
        acc = out_ref[0:SUB, :]
        for place in range(BATCH):
            weight = weights_out[base + place]
            piece = values[place * SUB : (place + 1) * SUB]
            squares = piece * piece
            acc = acc + weight * (squares[:, :SUB] + squares[:, SUB:])
            total = total + weight
        out_ref[0:SUB, :] = acc
        first_stage(jnp.minimum(index + 1, batches - 1))
        return total

    first_stage(0)
    total = lax.fori_loop(0, batches, step, jnp.float32(0.0))
    out_ref[SUB:SUMS, :] = jnp.full((SUMS - SUB, 128), total, F32)
    last = pltpu.make_async_copy(out_ref, sums_out, sems.at[len(inputs) + 2])
    last.start()

    def finish(index, carry):
        store(index).wait()
        return carry

    lax.fori_loop(0, batches, finish, 0)
    last.wait()


GRAD_TABLES = (
    "interp", "interp_t", "right_t", "fold", "flip", "pupil",
)


def grad_kernel(*refs):
    sums_hbm, refs = refs[:GROUP], refs[GROUP:]
    (pixel_hbm, rects_hbm, rects_t_hbm, field_hbm), refs = refs[:4], refs[4:]
    lists_hbm, refs = refs[:4], refs[4:]
    tabs_hbm, refs = refs[: len(GRAD_TABLES)], refs[len(GRAD_TABLES) :]
    (out_ref, aerial_ref, loss_ref), refs = refs[:3], refs[3:]
    sums, refs = refs[:GROUP], refs[GROUP:]
    (pixel_ref, rects_ref, rects_t_ref, field_ref), refs = refs[:4], refs[4:]
    lists, refs = refs[:4], refs[4:]
    tabs, refs = refs[: len(GRAD_TABLES)], refs[len(GRAD_TABLES) :]
    spread_ref, aer_ref, cnt_ref, g_ref, rows_ref, grad_refs, inner_ref, sems, pixel_sems, field_sems = refs
    interp_ref, interp_t_ref, right_t_ref, fold_ref, flip_ref, pupil_ref = tabs
    codes_ref, weights_ref, slots_ref, listed_ref = lists
    me = lax.axis_index("src")
    half = NPIX // 2
    blocks = half // BLOCK

    firsts = start_all(
        tuple(sums_hbm) + tuple(tabs_hbm[:2]) + (rects_hbm, rects_t_hbm) + tuple(lists_hbm),
        tuple(sums) + tuple(tabs[:2]) + (rects_ref, rects_t_ref) + tuple(lists),
        sems,
    )
    pixel_copies = [
        pltpu.make_async_copy(
            pixel_hbm.at[pl.ds(place * BLOCK, BLOCK)], pixel_ref.at[pl.ds(place * BLOCK, BLOCK)], pixel_sems.at[place]
        )
        for place in range(2 * blocks)
    ]
    for place in range(blocks):
        pixel_copies[place].start()
        pixel_copies[blocks + place].start()
    begun = len(firsts)
    rest = [
        pltpu.make_async_copy(source, target, sems.at[begun + place])
        for place, (source, target) in enumerate(
            zip(tabs_hbm[2:], tabs[2:])
        )
    ]
    for copy in rest:
        copy.start()

    def load(index):
        return pltpu.make_async_copy(field_hbm.at[index], field_ref.at[index], field_sems.at[index])

    wait_all(firsts)
    batches = (listed_ref[0] + BATCH - 1) // BATCH

    def begin(index, carry):
        load(index).start()
        return carry

    lax.fori_loop(0, batches, begin, 0)
    image = sums[0][...]
    for ref in sums[1:]:
        image = image + ref[...]
    total = image[SUB : SUB + 1, 0:1]
    scaled = image[0:SUB] / total
    top, bottom = scaled[: SUB // 2], scaled[SUB // 2 :]
    lower = lanes_of((BLOCK, SUB)) < SUB // 2
    zero = jnp.zeros((SUB // 2, half), BF16)
    samples = []
    for parity in range(2):
        high, low = split(top - bottom if parity else top + bottom)
        samples.append(jnp.concatenate([high, high, low, jnp.zeros_like(low)], 0))
        table = interp_t_ref[parity]
        lows = [zero, table[SUB // 2 :]] if parity else [table[SUB // 2 :], zero]
        spread_ref[parity] = jnp.concatenate([table[: SUB // 2], table[: SUB // 2]] + lows, 0)

    col = lax.broadcasted_iota(jnp.int32, (128, NPIX), 1)
    col_in = ((col >= rects_ref[:, 2:3]) & (col < rects_ref[:, 3:4])).astype(F32).astype(BF16)

    def prepare(place):
        table_rows = pl.ds(place * BLOCK, BLOCK)
        parts = []
        for parity in range(2):
            table = interp_ref[parity, table_rows, :]
            parts.append(mul(jnp.concatenate([table, table], 1), samples[parity]))
        for first, values in ((place * BLOCK, parts[0] + parts[1]), (half + place * BLOCK, parts[0] - parts[1])):
            rows = pl.ds(first, BLOCK)
            turned = pltpu.roll(values, SUB // 2, 1)
            sides = jnp.where(lower, values + turned, turned - values)
            high = sides.astype(BF16)
            wide = high.astype(F32)
            low = pltpu.roll(sides - wide, SUB // 2, 1)
            even_in = jnp.concatenate([jnp.where(lower, wide, low).astype(BF16), high], 1)
            odd_in = jnp.concatenate([jnp.where(lower, low, wide).astype(BF16), high], 1)
            even, odd = mul(even_in, spread_ref[0]), mul(odd_in, spread_ref[1])
            aer_ref[rows, :half] = even + odd
            aer_ref[rows, half:] = even - odd
            row = lax.broadcasted_iota(jnp.int32, (BLOCK, 128), 0) + first
            row_in = ((row >= rects_t_ref[0:1, :]) & (row < rects_t_ref[1:2, :])).astype(F32).astype(BF16)
            cnt_ref[rows, :] = mul(row_in, col_in)

    loss = jnp.zeros((CHUNK, NPIX), F32)

    def chunk_gradient(first, loss):
        rows = pl.ds(first, CHUNK)
        wave = jnp.tanh((STEEP / 2.0) * aer_ref[rows, :] - (STEEP * THRESH / 2.0))
        mismatch = 0.5 * wave + (0.5 - jnp.minimum(cnt_ref[rows, :], 1.0))
        weighted = pixel_ref[rows, :] * mismatch
        return weighted * ((STEEP / 2.0) - (STEEP / 2.0) * (wave * wave)), loss + weighted * mismatch

    totals = [None, None]
    for place in range(blocks):
        prepare(place)
    for place in range(blocks):
        pixel_copies[place].wait()
        pixel_copies[blocks + place].wait()
        for index in range(BLOCK // CHUNK):
            near, loss = chunk_gradient(place * BLOCK + index * CHUNK, loss)
            far, loss = chunk_gradient(half + place * BLOCK + index * CHUNK, loss)
            rows = pl.ds(index * CHUNK, CHUNK)
            for parity, values in ((0, near + far), (1, near - far)):
                g_ref[place, parity, 0, rows, :], g_ref[place, parity, 1, rows, :] = split(values)
        for parity in range(2):
            table = interp_t_ref[parity, :, pl.ds(place * BLOCK, BLOCK)]
            both = mul(table, g_ref[place, parity, 0])
            part = both[: SUB // 2] + both[SUB // 2 :] + mul(table[: SUB // 2], g_ref[place, parity, 1])
            totals[parity] = part if place == 0 else rows_ref[parity] + part
            rows_ref[parity] = totals[parity]

    reduced = jnp.concatenate([totals[0] + totals[1], totals[0] - totals[1]], 0)
    below = lanes_of((SUB, SUB)) < SUB // 2
    sides = []
    for parity in range(2):
        left_half, right_half = reduced[:, :half], reduced[:, half:]
        high, low = split(left_half - right_half if parity else left_half + right_half)
        both = mul(jnp.concatenate([high, low], 0), interp_ref[parity])
        first, second = both[:SUB], both[SUB:]
        second = jnp.where(below, second, pltpu.roll(second, SUB // 2, 1))
        sides.append(first + pltpu.roll(first, SUB // 2, 1) + second)
    kernel = sides[0] + jnp.where(below, sides[1], -sides[1])
    wait_all(rest)
    aerial_ref[...] = aer_ref[pl.ds(pl.multiple_of(me * ROWS, ROWS), ROWS), :]
    loss_ref[0] = jnp.sum(loss) / (NPIX * NPIX)
    right_t = right_t_ref[...]
    pupil = pupil_ref[...]
    common = jnp.sum(kernel * scaled)
    grad_refs[...] = jnp.zeros_like(grad_refs)
    number = slot_numbers()
    lane = lanes_of((KP, KS))
    kernel2 = jnp.concatenate([kernel, kernel], 1)

    def finish_load(index, carry):
        load(index).wait()
        return carry

    lax.fori_loop(0, batches, finish_load, 0)

    def first_stage(index, terms):
        cotangents = []
        for place in range(BATCH):
            piece = field_ref[index, pl.ds(place * SUB, SUB), :]
            cotangent = piece * kernel2
            strength = jnp.sum(piece * cotangent, axis=(0, 1), keepdims=True)
            terms = jnp.where(number == slots_ref[index * BATCH + place], strength - common, terms)
            cotangents.append(cotangent)
        values = pull(*split(jnp.concatenate(cotangents, 0)), right_t)
        inner_ref[0], inner_ref[1] = split(turn_back(values))
        return terms

    def back(index, terms):
        grads = pull(inner_ref[0], inner_ref[1], right_t)
        for place in range(BATCH):
            scaled_grad = grads[place * KP : (place + 1) * KP] * pupil * (2.0 * weights_ref[index * BATCH + place])
            code = codes_ref[index * BATCH + place]
            first = code >> 6
            rows = pl.ds(code & (KP - 1), KP)
            grad_refs[0, rows, :] += pltpu.roll(jnp.where(lane < KP, scaled_grad, 0.0), first, 1)
            grad_refs[1, rows, :] += pltpu.roll(jnp.where(lane < KP, 0.0, scaled_grad), first + KP, 1)
        return first_stage(jnp.minimum(index + 1, batches - 1), terms)

    terms = first_stage(0, jnp.zeros(number.shape, F32))
    terms = lax.fori_loop(0, batches, back, terms)
    real_t, imag_t = grad_refs[0] / total, grad_refs[1] / total
    real, imag = jnp.transpose(real_t), jnp.transpose(imag_t)
    sub = lax.broadcasted_iota(jnp.int32, (8, KS), 0)
    edge = jnp.where(sub == 0, real_t[0:1], imag_t[0:1])
    kept = jnp.zeros((KS, KS), F32)
    mirrored = jnp.zeros((EDGE_ROWS, KS), F32)
    for part in split(jnp.concatenate([real, imag], 1)):
        folded = mul(part, fold_ref[...])
        kept = kept + folded[:, :KS]
        mirrored = mirrored + mul(flip_ref[...], folded[:, KS:].astype(BF16))
    out_ref[0:KS, :] = kept + mirrored[0:KS]
    out_ref[MIRROR_ROW:EDGE_ROWS, :] = mirrored[KS:]
    out_ref[EDGE_ROWS:TERM_ROWS, :] = jnp.where(sub < 2, edge, 0.0)
    blank = jnp.zeros((GRAD - TERM_ROWS - SLOTS // 128, 128), F32)
    out_ref[TERM_ROWS:GRAD, :] = jnp.concatenate([terms / (total * NPIX), blank], 0)


def mask_kernel(*refs):
    packs_hbm, refs = refs[:GROUP], refs[GROUP:]
    (mask_hbm, own_hbm, cols_hbm, out_ref, slot_ref), refs = refs[:5], refs[5:]
    packs, refs = refs[:GROUP], refs[GROUP:]
    mask_ref, own_ref, cols_ref, terms_vmem, terms_smem, sems = refs
    me = lax.axis_index("src")
    copies = start_all(
        tuple(packs_hbm) + (own_hbm.at[me], cols_hbm, mask_hbm), tuple(packs) + (own_ref, cols_ref, mask_ref), sems
    )
    wait_all(copies[:GROUP])
    packed = packs[0][...]
    for ref in packs[1:]:
        packed = packed + ref[...]
    terms_vmem[...] = packed[TERM_ROWS:GRAD]
    fetch = pltpu.make_async_copy(terms_vmem, terms_smem, sems.at[GROUP + 3])
    fetch.start()
    copies[GROUP].wait()
    used = EDGE_ROWS
    pulled = mul3((own_ref[0, :, :used], own_ref[1, :, :used]), split(packed[0:used]))
    sin_part = pltpu.roll(pulled[ROWS:], KS // 2, 1)
    lane = lanes_of((ROWS, KS))
    main = pulled[:ROWS] + jnp.where(lane < KS // 2, -sin_part, sin_part)
    edge = packed[EDGE_ROWS:TERM_ROWS]
    blank = jnp.zeros((KS - 16, KS), F32)
    none = jnp.zeros((8, KS), F32)
    cos_rows = (own_ref[0, :ROWS, :KS], own_ref[1, :ROWS, :KS])
    sin_rows = (own_ref[0, ROWS:, :KS], own_ref[1, ROWS:, :KS])
    contract = ((1,), (1,))
    side = mul3(cos_rows, split(jnp.concatenate([edge, none, blank], 0)), contract) + mul3(
        sin_rows, split(jnp.concatenate([none, edge, blank], 0)), contract
    )
    gathered = split(jnp.concatenate([main, side], 1))
    wait_all(copies[GROUP + 1 :])
    transmit = jnp.tanh(mask_ref[...])
    out_ref[...] = mul3_few(gathered, pair(cols_ref)) * (1.0 - transmit * transmit)
    fetch.wait()
    for slot in range(CAP):
        place = me * CAP + slot
        slot_ref[slot] = terms_smem[place >> 7, place & 127]


def exchange(value, others):
    received = [value]
    for other in others:
        pairs = [(index, index ^ other) for index in range(SRC)]
        received.append(lax.ppermute(value, "src", pairs))
    return received


MIB = 1024 * 1024


def run(kernel, name, operands, outputs, scratch):
    smem = pl.BlockSpec(memory_space=pltpu.SMEM)
    hbm = pl.BlockSpec(memory_space=pltpu.HBM)
    vmem = pl.BlockSpec(memory_space=pltpu.VMEM)
    kinds = {"smem": smem, "hbm": hbm, "vmem": vmem}
    return pl.pallas_call(
        kernel,
        in_specs=[hbm] * len(operands),
        out_specs=[kinds[kind] for kind, unused, unused in outputs],
        out_shape=[jax.ShapeDtypeStruct(shape, dtype) for unused, shape, dtype in outputs],
        scratch_shapes=scratch,
        compiler_params=pltpu.CompilerParams(vmem_limit_bytes=60 * MIB),
        name=name,
    )(*operands)


def body(mask_param, pixel_weight, source_weight, point_index, point_count, target_rects):
    table = tables()
    vmem = lambda array: pltpu.VMEM(array.shape, array.dtype)
    smem = lambda array: pltpu.SMEM(array.shape, array.dtype)
    dma = lambda count: pltpu.SemaphoreType.DMA((count,))

    (block,) = run(
        project_kernel,
        "project",
        [point_index, point_count, source_weight, mask_param, table["cols"], table["own"]],
        [("vmem", (GATHER, PACK, 128), F32)],
        [
            smem(point_index), smem(point_count), smem(source_weight), vmem(mask_param), vmem(table["cols"]),
            vmem(table["own"][0]), dma(6),
        ],
    )

    same_core = [list(range(core, SRC, 2)) for core in range(2)]
    mine = lax.all_to_all(block, "src", 0, 0, axis_index_groups=same_core, tiled=True)
    unused, other = exchange(mine, CORE)

    operands = [mine, other] + [table[name] for name in IMAGE_TABLES]
    listed = SLOTS // GROUP + BATCH
    sums, codes, weights, slots, count, field = run(
        image_kernel,
        "image",
        operands,
        [
            ("hbm", (SUMS, 128), F32),
            ("smem", (listed,), jnp.int32),
            ("smem", (listed,), F32),
            ("smem", (listed,), jnp.int32),
            ("smem", (1,), jnp.int32),
            ("hbm", (BATCHES, BATCH * SUB, 2 * SUB), F32),
        ],
        [vmem(array) for array in operands]
        + [
            pltpu.VMEM((SUMS, 128), F32),
            pltpu.VMEM((KS, KS), F32),
            pltpu.VMEM((KS, KS), F32),
            pltpu.VMEM((BATCHES, BATCH * SUB, 2 * SUB), F32),
            pltpu.VMEM((2, BATCH * SUB, KS), BF16),
            pltpu.SMEM((SRC, 128), F32),
            pltpu.SMEM((listed,), jnp.int32),
            dma(10),
            dma(BATCHES),
        ],
    )

    all_sums = exchange(sums, GROUP_DEVICES)
    rects_t = target_rects.T
    lists = [codes, weights, slots, count]
    constants = [table[name] for name in GRAD_TABLES]
    grad, aerial, loss = run(
        grad_kernel,
        "gradient",
        all_sums + [pixel_weight, target_rects, rects_t, field] + lists + constants,
        [("vmem", (GRAD, 128), F32), ("vmem", (ROWS, NPIX), F32), ("smem", (1,), F32)],
        [vmem(array) for array in all_sums + [pixel_weight, target_rects, rects_t, field]]
        + [smem(array) for array in lists]
        + [vmem(array) for array in constants]
        + [
            pltpu.VMEM((2, 2 * SUB, NPIX // 2), BF16),
            pltpu.VMEM((NPIX, NPIX), F32),
            pltpu.VMEM((NPIX, NPIX), F32),
            pltpu.VMEM((NPIX // 2 // BLOCK, 2, 2, BLOCK, NPIX), BF16),
            pltpu.VMEM((2, SUB // 2, NPIX), F32),
            pltpu.VMEM((2, KS, KS), F32),
            pltpu.VMEM((2, BATCH * KP, 2 * SUB), BF16),
            dma(GROUP + 2 + len(lists) + len(constants)),
            dma(NPIX // BLOCK),
            dma(BATCHES),
        ],
    )

    grads = exchange(grad, GROUP_DEVICES)
    operands = grads + [mask_param, table["own"], table["cols_t"]]
    mask_grad, source_grad = run(
        mask_kernel,
        "mask",
        operands,
        [("vmem", (ROWS, NPIX), F32), ("smem", (CAP,), F32)],
        [vmem(array) for array in grads]
        + [
            vmem(mask_param), vmem(table["own"][0]), vmem(table["cols_t"]), pltpu.VMEM((8, 128), F32),
            pltpu.SMEM((8, 128), F32), dma(GROUP + 4),
        ],
    )
    return mask_grad, aerial, source_grad, loss


def solution(mesh):
    in_specs = (P(("clip", "src"), None), P("clip", None), P(), P("src"), P("src"), P("clip", None))
    out_specs = (P(("clip", "src"), None), P(("clip", "src"), None), P(("clip", "src")), P("clip"))
    return jax.shard_map(body, mesh=mesh, in_specs=in_specs, out_specs=out_specs, check_vma=False)
```

```python
import functools
import math

import jax
import jax.numpy as jnp
import ml_dtypes
import numpy as np
from jax import lax
from jax.experimental import pallas as pl
from jax.experimental.pallas import tpu as pltpu
from jax.sharding import PartitionSpec as P

NPIX = 1024
KS = 128
KP = 64
SG = 101
CAP = 8
SRC = 64
SLOTS = SRC * CAP
ROWS = NPIX // SRC
SUB = 128
BLOCK = 256
CHUNK = 16
STEEP = 10.0
THRESH = 0.3

EDGE = ROWS
META = EDGE + 2
PACK = 24
META_LANES = 32
UNUSED = 3 * CAP
GATHER = 32
SUMS = 136
MIRROR_ROW = KS
EDGE_ROWS = KS + 8
TERM_ROWS = KS + 16
GRAD = KS + 24

CORE = (1,)
GROUP_DEVICES = (1, 32, 33)
GROUP = 4
BATCH = 8
BATCHES = SLOTS // GROUP // BATCH

F32 = jnp.float32
BF16 = jnp.bfloat16


def halves(table):
    table = np.asarray(table, np.float64)
    high = table.astype(ml_dtypes.bfloat16)
    low = (table - high.astype(np.float64)).astype(ml_dtypes.bfloat16)
    return np.stack([high, low])


def angles(left, right, period):
    return 2.0 * math.pi * np.mod(np.multiply.outer(left, right), period) / period


@functools.lru_cache(None)
def tables():
    pixels = np.arange(NPIX)
    cols = np.zeros((NPIX, 2 * KS))
    phase = angles(pixels, np.arange(KS // 2), NPIX)
    cols[:, : KS // 2] = np.cos(phase)
    cols[:, KS // 2 : KS] = -np.sin(phase)
    edge = angles(pixels, -KS // 2, NPIX)
    cols[:, KS] = np.cos(edge)
    cols[:, KS + 1] = -np.sin(edge)
    cols[:, KS + 8] = -np.sin(edge)
    cols[:, KS + 9] = -np.cos(edge)
    cols /= NPIX

    phase = angles(np.arange(KS + 1) - KS // 2, pixels, NPIX).reshape(KS + 1, SRC, ROWS)
    wave = np.stack([np.cos(phase), np.sin(phase)]) / NPIX
    by_core = wave[:, :KS].reshape(2 * KS, GATHER, 2, ROWS).transpose(2, 0, 1, 3)
    waves = by_core.reshape(2, 2 * KS, GATHER * ROWS)
    own = np.zeros((SRC, 2 * ROWS, 2 * KS))
    own[:, :, : KS + 1] = wave.transpose(2, 0, 3, 1).reshape(SRC, 2 * ROWS, KS + 1)

    half = KS // 2
    keep = np.zeros((KS, 2 * KS))
    mirror = np.zeros((KS, 2 * KS))
    for freq in range(half):
        keep[freq, half + freq] = 1.0
        keep[half + freq, KS + half + freq] = 1.0
        if freq:
            mirror[freq, half - freq] = 1.0
            mirror[half + freq, KS + half - freq] = 1.0
    flip = np.zeros((EDGE_ROWS, KS))
    flip[KS - np.arange(KS), np.arange(KS)] = 1.0
    conj = mirror * np.where(np.arange(KS) < half, 1.0, -1.0)[:, None]

    phase = angles(np.arange(KP) - KP // 2, np.arange(SUB), SUB)
    cos_part, sin_part = np.cos(phase), np.sin(phase)
    right = np.block([[cos_part, sin_part], [-sin_part, cos_part]])

    shift = pixels[: NPIX // 2, None] - (NPIX // SUB) * np.arange(SUB // 2)[None, :]
    interp = np.zeros((2, NPIX // 2, SUB // 2))
    interp[0] = 1.0
    for freq in range(1, SUB // 2):
        interp[freq % 2] += 2.0 * np.cos(2.0 * math.pi * np.mod(freq * shift, NPIX) / NPIX)
    interp /= SUB

    freq = np.arange(KP) - KP // 2
    pupil = (freq[:, None] ** 2 + freq[None, :] ** 2 < (KP // 2) ** 2).astype(np.float32)
    as_bf16 = lambda table: table.astype(ml_dtypes.bfloat16)
    high_low = lambda table, axis: np.concatenate(list(halves(table)), axis)
    twice = lambda table, axis: np.concatenate([halves(table)[0]] * 2, axis)
    return dict(
        cols=halves(cols),
        cols_t=halves(cols.T),
        waves=halves(waves).transpose(1, 0, 2, 3),
        own=halves(own).transpose(1, 0, 2, 3),
        unfold=as_bf16(np.concatenate([keep, mirror], 0)),
        fold=as_bf16(np.concatenate([keep.T, conj.T], 1)),
        flip=as_bf16(flip),
        right=twice(right, 0),
        right_low=halves(right)[1],
        right_t=high_low(right.T, 1),
        interp=high_low(interp, 2),
        interp_t=high_low(interp.transpose(0, 2, 1), 1),
        pupil=np.concatenate([pupil, pupil], 1),
    )


def split(values):
    high = values.astype(BF16)
    low = (values - high.astype(F32)).astype(BF16)
    return high, low


def mul(first, second, dims=((1,), (0,))):
    return lax.dot_general(first, second, (dims, ((), ())), preferred_element_type=F32)


def mul3(first, second, dims=((1,), (0,))):
    return (
        mul(first[0], second[0], dims) + mul(first[0], second[1], dims) + mul(first[1], second[0], dims)
    )


def mul3_few(first, second):
    rows = first[0].shape[0]
    both = mul(jnp.concatenate(first, 0), second[0])
    return both[:rows] + both[rows:] + mul(first[0], second[1])


def pair(ref):
    return ref[0], ref[1]


def div_sg(number):
    return (number * 41529) >> 22


def offset(grid):
    return ((grid - SG // 2) * (KP // 2) + 51 * 64) // 51 - 64 + KP // 2


def lanes_of(shape):
    return lax.broadcasted_iota(jnp.int32, shape, 1)


def slot_numbers():
    shape = (SLOTS // 128, 128)
    return lax.broadcasted_iota(jnp.int32, shape, 0) * 128 + lanes_of(shape)


def start_all(sources, targets, sems):
    copies = [
        pltpu.make_async_copy(source, target, sems.at[place])
        for place, (source, target) in enumerate(zip(sources, targets))
    ]
    for copy in copies:
        copy.start()
    return copies


def wait_all(copies):
    for copy in copies:
        copy.wait()


def project_kernel(
    index_hbm, count_hbm, weight_hbm, mask_hbm, cols_hbm, own_hbm, out_ref,
    index_ref, count_ref, weight_ref, mask_ref, cols_ref, own_ref, sems,
):
    me = lax.axis_index("src")
    copies = start_all(
        (mask_hbm, cols_hbm, own_hbm.at[me], index_hbm, count_hbm, weight_hbm),
        (mask_ref, cols_ref, own_ref, index_ref, count_ref, weight_ref),
        sems,
    )
    copies[0].wait()
    transmit = split(jnp.tanh(mask_ref[...]))
    copies[1].wait()
    projected = mul3_few(transmit, pair(cols_ref))
    wait_all(copies[2:])
    edge = split(projected[:, KS:])
    cos_rows = (own_ref[0, :ROWS, :KS], own_ref[1, :ROWS, :KS])
    sin_rows = (own_ref[0, ROWS:, :KS], own_ref[1, ROWS:, :KS])
    contract = ((0,), (0,))
    edge_rows = mul3(edge, cos_rows, contract)[0:8] + mul3(edge, sin_rows, contract)[8:16]
    shape = (PACK - EDGE, 128)
    lane = lanes_of(shape)
    sub = lax.broadcasted_iota(jnp.int32, shape, 0)
    count = count_ref[0]
    meta = jnp.where(lane == 2 * CAP, count.astype(F32), 0.0)
    for slot in range(CAP):
        point = index_ref[slot]
        grid_row = div_sg(point)
        grid_col = point - grid_row * SG
        code = offset(grid_row) * KP + offset(grid_col)
        meta = jnp.where(lane == slot, code.astype(F32), meta)
        meta = jnp.where(lane == CAP + slot, weight_ref[grid_row, grid_col], meta)
    tail = jnp.where(sub < 2, edge_rows, jnp.where(sub == 2, meta, 0.0))
    block = jnp.concatenate([projected[:, :KS], tail], 0)
    for place in range(GATHER):
        out_ref[place] = block


def unpack_spectrum(mine_ref, other_ref, waves_ref, core, unfold, re_ref, im_ref):
    total = jnp.zeros((2 * KS, KS), F32)
    edge = jnp.zeros((PACK - EDGE, KS), F32)
    for ref, which in ((mine_ref, core), (other_ref, 1 - core)):
        gathered = ref[...]
        high, low = split(gathered[:, :ROWS].reshape(GATHER * ROWS, KS))
        both = mul(waves_ref[which, 0], jnp.concatenate([high, low], 1))
        total = total + both[:, :KS] + both[:, KS:] + mul(waves_ref[which, 1], high)
        edge = edge + jnp.sum(gathered[:, EDGE:], 0)
    lower = lanes_of((KS, KS)) < KS // 2
    cos_part = total[:KS]
    sin_part = pltpu.roll(total[KS:], KS // 2, 1)
    near = cos_part + jnp.where(lower, sin_part, -sin_part)
    far = jnp.where(lower, cos_part - sin_part, -cos_part - sin_part)
    full = jnp.zeros((KS, 2 * KS), F32)
    for part in split(jnp.concatenate([near, far], 1)):
        full = full + mul(part, unfold)
    column = jnp.transpose(edge)
    lane = lanes_of((KS, KS))
    re_ref[...] = jnp.transpose(jnp.where(lane == 0, column[:, 0:1], full[:, :KS]))
    im_ref[...] = jnp.transpose(jnp.where(lane == 0, column[:, 1:2], full[:, KS:]))


def list_slots(rank, core, meta_ref, list_ref):
    listed = jnp.int32(0)
    before = jnp.int32(0)
    for index in range(SRC):
        row = (index >> 1) + ((index + core) & 1) * GATHER
        count = meta_ref[row, 2 * CAP].astype(jnp.int32)
        first = (rank - before) & (GROUP - 1)
        for turn in range(CAP // GROUP):
            position = first + turn * GROUP
            list_ref[listed] = row * META_LANES + position
            listed = listed + jnp.where(position < count, 1, 0)
        before = before + count
    for extra in range(BATCH):
        list_ref[listed + extra] = UNUSED
    return listed


def window(code, re_ref, im_ref, pupil):
    first = code >> 6
    rows = pl.ds(code & (KP - 1), KP)
    real = pltpu.roll(re_ref[rows, :], (KS - first) & (KS - 1), 1)
    imag = pltpu.roll(im_ref[rows, :], KP - first, 1)
    return jnp.where(lanes_of((KP, KS)) < KP, real, imag) * pupil


def transform(high, low, right, right_low):
    return mul(jnp.concatenate([high, low], 1), right) + mul(high, right_low)


def pull(high, low, right_t):
    both = mul(high, right_t)
    return both[:, :KS] + both[:, KS:] + mul(low, right_t[:, :KS])


def turn(values):
    pieces = [values[place * KP : (place + 1) * KP] for place in range(values.shape[0] // KP)]
    return jnp.concatenate(
        [jnp.transpose(jnp.concatenate([piece[:, :SUB], piece[:, SUB:]], 0)) for piece in pieces], 0
    )


def turn_back(values):
    turned = [jnp.transpose(values[place * SUB : (place + 1) * SUB]) for place in range(values.shape[0] // SUB)]
    return jnp.concatenate([jnp.concatenate([piece[:KP], piece[KP:]], 1) for piece in turned], 0)


IMAGE_TABLES = ("waves", "unfold", "right", "right_low", "pupil")


def image_kernel(*refs):
    inputs, refs = refs[:7], refs[7:]
    (sums_out, codes_out, weights_out, slots_out, listed_out, field_out), refs = refs[:6], refs[6:]
    out_ref, re_ref, im_ref, field_ref, inner_ref, meta_ref, list_ref, sems, field_sems = refs
    mine_ref, other_ref, waves_ref, unfold_ref, right_ref, right_low_ref, pupil_ref = inputs
    me = lax.axis_index("src")
    core = me & 1
    metas = [
        pltpu.make_async_copy(
            inputs[place].at[:, META], meta_ref.at[pl.ds(place * GATHER, GATHER)], sems.at[place]
        )
        for place in range(2)
    ]
    for copy in metas:
        copy.start()
    wait_all(metas)
    rank = core + 2 * (me >> 5)
    listed = list_slots(rank, core, meta_ref, list_ref)
    listed_out[0] = listed
    unpack_spectrum(mine_ref, other_ref, waves_ref, core, unfold_ref[...], re_ref, im_ref)
    right, right_low = right_ref[...], right_low_ref[...]
    pupil = pupil_ref[...]
    out_ref[...] = jnp.zeros_like(out_ref)
    batches = (listed + BATCH - 1) // BATCH

    def store(index):
        return pltpu.make_async_copy(field_ref.at[index], field_out.at[index], field_sems.at[index])

    def first_stage(index):
        masked = []
        for place in range(BATCH):
            position = index * BATCH + place
            where = list_ref[position]
            row, lane = where >> 5, where & (META_LANES - 1)
            code = meta_ref[row, lane].astype(jnp.int32)
            codes_out[position] = code
            weights_out[position] = meta_ref[row, CAP + lane]
            source = 2 * (row & (GATHER - 1)) + ((core + (row >> 5)) & 1)
            slots_out[position] = jnp.where(lane == UNUSED, -1, source * CAP + lane)
            masked.append(window(code, re_ref, im_ref, pupil))
        values = transform(*split(jnp.concatenate(masked, 0)), right, right_low)
        inner_ref[0], inner_ref[1] = split(turn(values))

    def step(index, total):
        base = index * BATCH
        values = transform(inner_ref[0], inner_ref[1], right, right_low)
        field_ref[index] = values
        store(index).start()
        acc = out_ref[0:SUB, :]
        for place in range(BATCH):
            weight = weights_out[base + place]
            piece = values[place * SUB : (place + 1) * SUB]
            squares = piece * piece
            acc = acc + weight * (squares[:, :SUB] + squares[:, SUB:])
            total = total + weight
        out_ref[0:SUB, :] = acc
        first_stage(jnp.minimum(index + 1, batches - 1))
        return total

    first_stage(0)
    total = lax.fori_loop(0, batches, step, jnp.float32(0.0))
    out_ref[SUB:SUMS, :] = jnp.full((SUMS - SUB, 128), total, F32)
    last = pltpu.make_async_copy(out_ref, sums_out, sems.at[2])
    last.start()

    def finish(index, carry):
        store(index).wait()
        return carry

    lax.fori_loop(0, batches, finish, 0)
    last.wait()


GRAD_TABLES = (
    "interp", "interp_t", "right_t", "fold", "flip", "pupil",
)


def grad_kernel(*refs):
    sums, refs = refs[:GROUP], refs[GROUP:]
    (pixel_hbm, rects_hbm, rects_t_hbm, field_hbm), refs = refs[:4], refs[4:]
    lists_hbm, refs = refs[:4], refs[4:]
    tabs_hbm, refs = refs[: len(GRAD_TABLES)], refs[len(GRAD_TABLES) :]
    (out_ref, aerial_ref, loss_ref), refs = refs[:3], refs[3:]
    (pixel_ref, rects_ref, rects_t_ref, field_ref), refs = refs[:4], refs[4:]
    lists, refs = refs[:4], refs[4:]
    tabs, refs = refs[: len(GRAD_TABLES)], refs[len(GRAD_TABLES) :]
    spread_ref, aer_ref, cnt_ref, g_ref, rows_ref, grad_refs, inner_ref, sems, pixel_sems, field_sems = refs
    interp_ref, interp_t_ref, right_t_ref, fold_ref, flip_ref, pupil_ref = tabs
    codes_ref, weights_ref, slots_ref, listed_ref = lists
    me = lax.axis_index("src")
    half = NPIX // 2
    blocks = half // BLOCK

    firsts = start_all(
        tuple(tabs_hbm[:2]) + (rects_hbm, rects_t_hbm) + tuple(lists_hbm),
        tuple(tabs[:2]) + (rects_ref, rects_t_ref) + tuple(lists),
        sems,
    )
    pixel_copies = [
        pltpu.make_async_copy(
            pixel_hbm.at[pl.ds(place * BLOCK, BLOCK)], pixel_ref.at[pl.ds(place * BLOCK, BLOCK)], pixel_sems.at[place]
        )
        for place in range(2 * blocks)
    ]
    for place in range(blocks):
        pixel_copies[place].start()
        pixel_copies[blocks + place].start()
    begun = len(firsts)
    rest = [
        pltpu.make_async_copy(source, target, sems.at[begun + place])
        for place, (source, target) in enumerate(
            zip(tabs_hbm[2:], tabs[2:])
        )
    ]
    for copy in rest:
        copy.start()

    def load(index):
        return pltpu.make_async_copy(field_hbm.at[index], field_ref.at[index], field_sems.at[index])

    wait_all(firsts)
    batches = (listed_ref[0] + BATCH - 1) // BATCH

    def begin(index, carry):
        load(index).start()
        return carry

    lax.fori_loop(0, batches, begin, 0)
    image = sums[0][...]
    for ref in sums[1:]:
        image = image + ref[...]
    total = image[SUB : SUB + 1, 0:1]
    scaled = image[0:SUB] / total
    top, bottom = scaled[: SUB // 2], scaled[SUB // 2 :]
    lower = lanes_of((BLOCK, SUB)) < SUB // 2
    zero = jnp.zeros((SUB // 2, half), BF16)
    samples = []
    for parity in range(2):
        high, low = split(top - bottom if parity else top + bottom)
        samples.append(jnp.concatenate([high, high, low, jnp.zeros_like(low)], 0))
        table = interp_t_ref[parity]
        lows = [zero, table[SUB // 2 :]] if parity else [table[SUB // 2 :], zero]
        spread_ref[parity] = jnp.concatenate([table[: SUB // 2], table[: SUB // 2]] + lows, 0)

    col = lax.broadcasted_iota(jnp.int32, (128, NPIX), 1)
    col_in = ((col >= rects_ref[:, 2:3]) & (col < rects_ref[:, 3:4])).astype(F32).astype(BF16)

    def prepare(place):
        table_rows = pl.ds(place * BLOCK, BLOCK)
        parts = []
        for parity in range(2):
            table = interp_ref[parity, table_rows, :]
            parts.append(mul(jnp.concatenate([table, table], 1), samples[parity]))
        for first, values in ((place * BLOCK, parts[0] + parts[1]), (half + place * BLOCK, parts[0] - parts[1])):
            rows = pl.ds(first, BLOCK)
            turned = pltpu.roll(values, SUB // 2, 1)
            sides = jnp.where(lower, values + turned, turned - values)
            high = sides.astype(BF16)
            wide = high.astype(F32)
            low = pltpu.roll(sides - wide, SUB // 2, 1)
            even_in = jnp.concatenate([jnp.where(lower, wide, low).astype(BF16), high], 1)
            odd_in = jnp.concatenate([jnp.where(lower, low, wide).astype(BF16), high], 1)
            even, odd = mul(even_in, spread_ref[0]), mul(odd_in, spread_ref[1])
            aer_ref[rows, :half] = even + odd
            aer_ref[rows, half:] = even - odd
            row = lax.broadcasted_iota(jnp.int32, (BLOCK, 128), 0) + first
            row_in = ((row >= rects_t_ref[0:1, :]) & (row < rects_t_ref[1:2, :])).astype(F32).astype(BF16)
            cnt_ref[rows, :] = mul(row_in, col_in)

    loss = jnp.zeros((CHUNK, NPIX), F32)

    def chunk_gradient(first, loss):
        rows = pl.ds(first, CHUNK)
        wave = jnp.tanh((STEEP / 2.0) * aer_ref[rows, :] - (STEEP * THRESH / 2.0))
        mismatch = 0.5 * wave + (0.5 - jnp.minimum(cnt_ref[rows, :], 1.0))
        weighted = pixel_ref[rows, :] * mismatch
        return weighted * ((STEEP / 2.0) - (STEEP / 2.0) * (wave * wave)), loss + weighted * mismatch

    totals = [None, None]
    for place in range(blocks):
        prepare(place)
    for place in range(blocks):
        pixel_copies[place].wait()
        pixel_copies[blocks + place].wait()
        for index in range(BLOCK // CHUNK):
            near, loss = chunk_gradient(place * BLOCK + index * CHUNK, loss)
            far, loss = chunk_gradient(half + place * BLOCK + index * CHUNK, loss)
            rows = pl.ds(index * CHUNK, CHUNK)
            for parity, values in ((0, near + far), (1, near - far)):
                g_ref[place, parity, 0, rows, :], g_ref[place, parity, 1, rows, :] = split(values)
        for parity in range(2):
            table = interp_t_ref[parity, :, pl.ds(place * BLOCK, BLOCK)]
            both = mul(table, g_ref[place, parity, 0])
            part = both[: SUB // 2] + both[SUB // 2 :] + mul(table[: SUB // 2], g_ref[place, parity, 1])
            totals[parity] = part if place == 0 else rows_ref[parity] + part
            rows_ref[parity] = totals[parity]

    reduced = jnp.concatenate([totals[0] + totals[1], totals[0] - totals[1]], 0)
    below = lanes_of((SUB, SUB)) < SUB // 2
    sides = []
    for parity in range(2):
        left_half, right_half = reduced[:, :half], reduced[:, half:]
        high, low = split(left_half - right_half if parity else left_half + right_half)
        both = mul(jnp.concatenate([high, low], 0), interp_ref[parity])
        first, second = both[:SUB], both[SUB:]
        second = jnp.where(below, second, pltpu.roll(second, SUB // 2, 1))
        sides.append(first + pltpu.roll(first, SUB // 2, 1) + second)
    kernel = sides[0] + jnp.where(below, sides[1], -sides[1])
    wait_all(rest)
    aerial_ref[...] = aer_ref[pl.ds(pl.multiple_of(me * ROWS, ROWS), ROWS), :]
    loss_ref[0] = jnp.sum(loss) / (NPIX * NPIX)
    right_t = right_t_ref[...]
    pupil = pupil_ref[...]
    common = jnp.sum(kernel * scaled)
    grad_refs[...] = jnp.zeros_like(grad_refs)
    number = slot_numbers()
    lane = lanes_of((KP, KS))
    kernel2 = jnp.concatenate([kernel, kernel], 1)

    def finish_load(index, carry):
        load(index).wait()
        return carry

    lax.fori_loop(0, batches, finish_load, 0)

    def first_stage(index, terms):
        cotangents = []
        for place in range(BATCH):
            piece = field_ref[index, pl.ds(place * SUB, SUB), :]
            cotangent = piece * kernel2
            strength = jnp.sum(piece * cotangent, axis=(0, 1), keepdims=True)
            terms = jnp.where(number == slots_ref[index * BATCH + place], strength - common, terms)
            cotangents.append(cotangent)
        values = pull(*split(jnp.concatenate(cotangents, 0)), right_t)
        inner_ref[0], inner_ref[1] = split(turn_back(values))
        return terms

    def back(index, terms):
        grads = pull(inner_ref[0], inner_ref[1], right_t)
        for place in range(BATCH):
            scaled_grad = grads[place * KP : (place + 1) * KP] * pupil * (2.0 * weights_ref[index * BATCH + place])
            code = codes_ref[index * BATCH + place]
            first = code >> 6
            rows = pl.ds(code & (KP - 1), KP)
            grad_refs[0, rows, :] += pltpu.roll(jnp.where(lane < KP, scaled_grad, 0.0), first, 1)
            grad_refs[1, rows, :] += pltpu.roll(jnp.where(lane < KP, 0.0, scaled_grad), first + KP, 1)
        return first_stage(jnp.minimum(index + 1, batches - 1), terms)

    terms = first_stage(0, jnp.zeros(number.shape, F32))
    terms = lax.fori_loop(0, batches, back, terms)
    real_t, imag_t = grad_refs[0] / total, grad_refs[1] / total
    real, imag = jnp.transpose(real_t), jnp.transpose(imag_t)
    sub = lax.broadcasted_iota(jnp.int32, (8, KS), 0)
    edge = jnp.where(sub == 0, real_t[0:1], imag_t[0:1])
    kept = jnp.zeros((KS, KS), F32)
    mirrored = jnp.zeros((EDGE_ROWS, KS), F32)
    for part in split(jnp.concatenate([real, imag], 1)):
        folded = mul(part, fold_ref[...])
        kept = kept + folded[:, :KS]
        mirrored = mirrored + mul(flip_ref[...], folded[:, KS:].astype(BF16))
    out_ref[0:KS, :] = kept + mirrored[0:KS]
    out_ref[MIRROR_ROW:EDGE_ROWS, :] = mirrored[KS:]
    out_ref[EDGE_ROWS:TERM_ROWS, :] = jnp.where(sub < 2, edge, 0.0)
    blank = jnp.zeros((GRAD - TERM_ROWS - SLOTS // 128, 128), F32)
    out_ref[TERM_ROWS:GRAD, :] = jnp.concatenate([terms / (total * NPIX), blank], 0)


def mask_kernel(*refs):
    packs, refs = refs[:GROUP], refs[GROUP:]
    mask_ref, own_hbm, cols_ref, out_ref, slot_ref, own_ref, terms_vmem, terms_smem, sems = refs
    me = lax.axis_index("src")
    table = pltpu.make_async_copy(own_hbm.at[me], own_ref, sems.at[0])
    table.start()
    packed = packs[0][...]
    for ref in packs[1:]:
        packed = packed + ref[...]
    terms_vmem[...] = packed[TERM_ROWS:GRAD]
    fetch = pltpu.make_async_copy(terms_vmem, terms_smem, sems.at[1])
    fetch.start()
    table.wait()
    used = EDGE_ROWS
    pulled = mul3((own_ref[0, :, :used], own_ref[1, :, :used]), split(packed[0:used]))
    sin_part = pltpu.roll(pulled[ROWS:], KS // 2, 1)
    lane = lanes_of((ROWS, KS))
    main = pulled[:ROWS] + jnp.where(lane < KS // 2, -sin_part, sin_part)
    edge = packed[EDGE_ROWS:TERM_ROWS]
    blank = jnp.zeros((KS - 16, KS), F32)
    none = jnp.zeros((8, KS), F32)
    cos_rows = (own_ref[0, :ROWS, :KS], own_ref[1, :ROWS, :KS])
    sin_rows = (own_ref[0, ROWS:, :KS], own_ref[1, ROWS:, :KS])
    contract = ((1,), (1,))
    side = mul3(cos_rows, split(jnp.concatenate([edge, none, blank], 0)), contract) + mul3(
        sin_rows, split(jnp.concatenate([none, edge, blank], 0)), contract
    )
    gathered = split(jnp.concatenate([main, side], 1))
    transmit = jnp.tanh(mask_ref[...])
    out_ref[...] = mul3_few(gathered, pair(cols_ref)) * (1.0 - transmit * transmit)
    fetch.wait()
    for slot in range(CAP):
        place = me * CAP + slot
        slot_ref[slot] = terms_smem[place >> 7, place & 127]


def exchange(value, others):
    received = [value]
    for other in others:
        pairs = [(index, index ^ other) for index in range(SRC)]
        received.append(lax.ppermute(value, "src", pairs))
    return received


MIB = 1024 * 1024


def run(kernel, name, operands, outputs, scratch, limit, in_vmem=()):
    smem = pl.BlockSpec(memory_space=pltpu.SMEM)
    hbm = pl.BlockSpec(memory_space=pltpu.HBM)
    vmem = pl.BlockSpec(memory_space=pltpu.VMEM)
    kinds = {"smem": smem, "hbm": hbm, "vmem": vmem}
    return pl.pallas_call(
        kernel,
        in_specs=[vmem if place in in_vmem else hbm for place in range(len(operands))],
        out_specs=[kinds[kind] for kind, unused, unused in outputs],
        out_shape=[jax.ShapeDtypeStruct(shape, dtype) for unused, shape, dtype in outputs],
        scratch_shapes=scratch,
        compiler_params=pltpu.CompilerParams(vmem_limit_bytes=limit * MIB),
        name=name,
    )(*operands)


def body(mask_param, pixel_weight, source_weight, point_index, point_count, target_rects):
    table = tables()
    vmem = lambda array: pltpu.VMEM(array.shape, array.dtype)
    smem = lambda array: pltpu.SMEM(array.shape, array.dtype)
    dma = lambda count: pltpu.SemaphoreType.DMA((count,))

    (block,) = run(
        project_kernel,
        "project",
        [point_index, point_count, source_weight, mask_param, table["cols"], table["own"]],
        [("vmem", (GATHER, PACK, 128), F32)],
        [
            smem(point_index), smem(point_count), smem(source_weight), vmem(mask_param), vmem(table["cols"]),
            vmem(table["own"][0]), dma(6),
        ],
        60,
    )

    same_core = [list(range(core, SRC, 2)) for core in range(2)]
    mine = lax.all_to_all(block, "src", 0, 0, axis_index_groups=same_core, tiled=True)
    unused, other = exchange(mine, CORE)

    operands = [mine, other] + [table[name] for name in IMAGE_TABLES]
    listed = SLOTS // GROUP + BATCH
    sums, codes, weights, slots, count, field = run(
        image_kernel,
        "image",
        operands,
        [
            ("hbm", (SUMS, 128), F32),
            ("smem", (listed,), jnp.int32),
            ("smem", (listed,), F32),
            ("smem", (listed,), jnp.int32),
            ("smem", (1,), jnp.int32),
            ("hbm", (BATCHES, BATCH * SUB, 2 * SUB), F32),
        ],
        [
            pltpu.VMEM((SUMS, 128), F32),
            pltpu.VMEM((KS, KS), F32),
            pltpu.VMEM((KS, KS), F32),
            pltpu.VMEM((BATCHES, BATCH * SUB, 2 * SUB), F32),
            pltpu.VMEM((2, BATCH * SUB, KS), BF16),
            pltpu.SMEM((SRC, 128), F32),
            pltpu.SMEM((listed,), jnp.int32),
            dma(3),
            dma(BATCHES),
        ],
        44,
        range(len(operands)),
    )

    all_sums = exchange(sums, GROUP_DEVICES)
    rects_t = target_rects.T
    lists = [codes, weights, slots, count]
    constants = [table[name] for name in GRAD_TABLES]
    grad, aerial, loss = run(
        grad_kernel,
        "gradient",
        all_sums + [pixel_weight, target_rects, rects_t, field] + lists + constants,
        [("vmem", (GRAD, 128), F32), ("vmem", (ROWS, NPIX), F32), ("smem", (1,), F32)],
        [vmem(array) for array in [pixel_weight, target_rects, rects_t, field]]
        + [smem(array) for array in lists]
        + [vmem(array) for array in constants]
        + [
            pltpu.VMEM((2, 2 * SUB, NPIX // 2), BF16),
            pltpu.VMEM((NPIX, NPIX), F32),
            pltpu.VMEM((NPIX, NPIX), F32),
            pltpu.VMEM((NPIX // 2 // BLOCK, 2, 2, BLOCK, NPIX), BF16),
            pltpu.VMEM((2, SUB // 2, NPIX), F32),
            pltpu.VMEM((2, KS, KS), F32),
            pltpu.VMEM((2, BATCH * KP, 2 * SUB), BF16),
            dma(GROUP + 2 + len(lists) + len(constants)),
            dma(NPIX // BLOCK),
            dma(BATCHES),
        ],
        52,
        range(GROUP),
    )

    grads = exchange(grad, GROUP_DEVICES)
    operands = grads + [mask_param, table["own"], table["cols_t"]]
    mask_grad, source_grad = run(
        mask_kernel,
        "mask",
        operands,
        [("vmem", (ROWS, NPIX), F32), ("smem", (CAP,), F32)],
        [vmem(table["own"][0]), pltpu.VMEM((8, 128), F32), pltpu.SMEM((8, 128), F32), dma(2)],
        32,
        [place for place in range(len(operands)) if place != GROUP + 1],
    )
    return mask_grad, aerial, source_grad, loss


def solution(mesh):
    in_specs = (P(("clip", "src"), None), P("clip", None), P(), P("src"), P("src"), P("clip", None))
    out_specs = (P(("clip", "src"), None), P(("clip", "src"), None), P(("clip", "src")), P("clip"))
    return jax.shard_map(body, mesh=mesh, in_specs=in_specs, out_specs=out_specs, check_vma=False)
```

```python
import functools
import math

import jax
import jax.numpy as jnp
import ml_dtypes
import numpy as np
from jax import lax
from jax.experimental import pallas as pl
from jax.experimental.pallas import tpu as pltpu
from jax.sharding import PartitionSpec as P

NPIX = 1024
KS = 128
KP = 64
SG = 101
CAP = 8
SRC = 64
SLOTS = SRC * CAP
ROWS = NPIX // SRC
SUB = 128
BLOCK = 256
CHUNK = 16
STEEP = 10.0
THRESH = 0.3

EDGE = ROWS
META = EDGE + 2
PACK = 24
META_LANES = 32
UNUSED = 3 * CAP
GATHER = 32
SUMS = 136
MIRROR_ROW = KS
EDGE_ROWS = KS + 8
TERM_ROWS = KS + 16
GRAD = KS + 24

CORE = (1,)
GROUP_DEVICES = (32, 33, 1)
GROUP = 4
BATCH = 8
BATCHES = SLOTS // GROUP // BATCH

F32 = jnp.float32
BF16 = jnp.bfloat16


def halves(table):
    table = np.asarray(table, np.float64)
    high = table.astype(ml_dtypes.bfloat16)
    low = (table - high.astype(np.float64)).astype(ml_dtypes.bfloat16)
    return np.stack([high, low])


def angles(left, right, period):
    return 2.0 * math.pi * np.mod(np.multiply.outer(left, right), period) / period


@functools.lru_cache(None)
def tables():
    pixels = np.arange(NPIX)
    cols = np.zeros((NPIX, 2 * KS))
    phase = angles(pixels, np.arange(KS // 2), NPIX)
    cols[:, : KS // 2] = np.cos(phase)
    cols[:, KS // 2 : KS] = -np.sin(phase)
    edge = angles(pixels, -KS // 2, NPIX)
    cols[:, KS] = np.cos(edge)
    cols[:, KS + 1] = -np.sin(edge)
    cols[:, KS + 8] = -np.sin(edge)
    cols[:, KS + 9] = -np.cos(edge)
    cols /= NPIX

    phase = angles(np.arange(KS + 1) - KS // 2, pixels, NPIX).reshape(KS + 1, SRC, ROWS)
    wave = np.stack([np.cos(phase), np.sin(phase)]) / NPIX
    by_core = wave[:, :KS].reshape(2 * KS, GATHER, 2, ROWS).transpose(2, 0, 1, 3)
    waves = by_core.reshape(2, 2 * KS, GATHER * ROWS)
    own = np.zeros((SRC, 2 * ROWS, 2 * KS))
    own[:, :, : KS + 1] = wave.transpose(2, 0, 3, 1).reshape(SRC, 2 * ROWS, KS + 1)

    half = KS // 2
    keep = np.zeros((KS, 2 * KS))
    mirror = np.zeros((KS, 2 * KS))
    for freq in range(half):
        keep[freq, half + freq] = 1.0
        keep[half + freq, KS + half + freq] = 1.0
        if freq:
            mirror[freq, half - freq] = 1.0
            mirror[half + freq, KS + half - freq] = 1.0
    flip = np.zeros((EDGE_ROWS, KS))
    flip[KS - np.arange(KS), np.arange(KS)] = 1.0
    conj = mirror * np.where(np.arange(KS) < half, 1.0, -1.0)[:, None]

    phase = angles(np.arange(KP) - KP // 2, np.arange(SUB), SUB)
    cos_part, sin_part = np.cos(phase), np.sin(phase)
    right = np.block([[cos_part, sin_part], [-sin_part, cos_part]])

    shift = pixels[: NPIX // 2, None] - (NPIX // SUB) * np.arange(SUB // 2)[None, :]
    interp = np.zeros((2, NPIX // 2, SUB // 2))
    interp[0] = 1.0
    for freq in range(1, SUB // 2):
        interp[freq % 2] += 2.0 * np.cos(2.0 * math.pi * np.mod(freq * shift, NPIX) / NPIX)
    interp /= SUB

    freq = np.arange(KP) - KP // 2
    pupil = (freq[:, None] ** 2 + freq[None, :] ** 2 < (KP // 2) ** 2).astype(np.float32)
    as_bf16 = lambda table: table.astype(ml_dtypes.bfloat16)
    high_low = lambda table, axis: np.concatenate(list(halves(table)), axis)
    twice = lambda table, axis: np.concatenate([halves(table)[0]] * 2, axis)
    return dict(
        cols=halves(cols),
        cols_t=halves(cols.T),
        waves=halves(waves).transpose(1, 0, 2, 3),
        own=halves(own).transpose(1, 0, 2, 3),
        unfold=as_bf16(np.concatenate([keep, mirror], 0)),
        fold=as_bf16(np.concatenate([keep.T, conj.T], 1)),
        flip=as_bf16(flip),
        right=twice(right, 0),
        right_low=halves(right)[1],
        right_t=high_low(right.T, 1),
        interp=high_low(interp, 2),
        interp_t=high_low(interp.transpose(0, 2, 1), 1),
        pupil=np.concatenate([pupil, pupil], 1),
    )


def split(values):
    high = values.astype(BF16)
    low = (values - high.astype(F32)).astype(BF16)
    return high, low


def mul(first, second, dims=((1,), (0,))):
    return lax.dot_general(first, second, (dims, ((), ())), preferred_element_type=F32)


def mul3(first, second, dims=((1,), (0,))):
    return (
        mul(first[0], second[0], dims) + mul(first[0], second[1], dims) + mul(first[1], second[0], dims)
    )


def mul3_few(first, second):
    rows = first[0].shape[0]
    both = mul(jnp.concatenate(first, 0), second[0])
    return both[:rows] + both[rows:] + mul(first[0], second[1])


def pair(ref):
    return ref[0], ref[1]


def div_sg(number):
    return (number * 41529) >> 22


def offset(grid):
    return ((grid - SG // 2) * (KP // 2) + 51 * 64) // 51 - 64 + KP // 2


def lanes_of(shape):
    return lax.broadcasted_iota(jnp.int32, shape, 1)


def slot_numbers():
    shape = (SLOTS // 128, 128)
    return lax.broadcasted_iota(jnp.int32, shape, 0) * 128 + lanes_of(shape)


def start_all(sources, targets, sems):
    copies = [
        pltpu.make_async_copy(source, target, sems.at[place])
        for place, (source, target) in enumerate(zip(sources, targets))
    ]
    for copy in copies:
        copy.start()
    return copies


def wait_all(copies):
    for copy in copies:
        copy.wait()


def project_kernel(
    index_hbm, count_hbm, weight_hbm, mask_hbm, cols_hbm, own_hbm, out_ref,
    index_ref, count_ref, weight_ref, mask_ref, cols_ref, own_ref, sems,
):
    me = lax.axis_index("src")
    copies = start_all(
        (mask_hbm, cols_hbm, own_hbm.at[me], index_hbm, count_hbm, weight_hbm),
        (mask_ref, cols_ref, own_ref, index_ref, count_ref, weight_ref),
        sems,
    )
    copies[0].wait()
    transmit = split(jnp.tanh(mask_ref[...]))
    copies[1].wait()
    projected = mul3_few(transmit, pair(cols_ref))
    wait_all(copies[2:])
    edge = split(projected[:, KS:])
    cos_rows = (own_ref[0, :ROWS, :KS], own_ref[1, :ROWS, :KS])
    sin_rows = (own_ref[0, ROWS:, :KS], own_ref[1, ROWS:, :KS])
    contract = ((0,), (0,))
    edge_rows = mul3(edge, cos_rows, contract)[0:8] + mul3(edge, sin_rows, contract)[8:16]
    shape = (PACK - EDGE, 128)
    lane = lanes_of(shape)
    sub = lax.broadcasted_iota(jnp.int32, shape, 0)
    count = count_ref[0]
    meta = jnp.where(lane == 2 * CAP, count.astype(F32), 0.0)
    for slot in range(CAP):
        point = index_ref[slot]
        grid_row = div_sg(point)
        grid_col = point - grid_row * SG
        code = offset(grid_row) * KP + offset(grid_col)
        meta = jnp.where(lane == slot, code.astype(F32), meta)
        meta = jnp.where(lane == CAP + slot, weight_ref[grid_row, grid_col], meta)
    tail = jnp.where(sub < 2, edge_rows, jnp.where(sub == 2, meta, 0.0))
    block = jnp.concatenate([projected[:, :KS], tail], 0)
    for place in range(GATHER):
        out_ref[place] = block


def transform_rows(mine_ref, other_ref, waves_ref, core):
    total = jnp.zeros((2 * KS, KS), F32)
    edge = jnp.zeros((PACK - EDGE, KS), F32)
    for ref, which in ((mine_ref, core), (other_ref, 1 - core)):
        gathered = ref[...]
        high, low = split(gathered[:, :ROWS].reshape(GATHER * ROWS, KS))
        both = mul(waves_ref[which, 0], jnp.concatenate([high, low], 1))
        total = total + both[:, :KS] + both[:, KS:] + mul(waves_ref[which, 1], high)
        edge = edge + jnp.sum(gathered[:, EDGE:], 0)
    return total, edge


def unpack_spectrum(total, edge, unfold, re_ref, im_ref):
    lower = lanes_of((KS, KS)) < KS // 2
    cos_part = total[:KS]
    sin_part = pltpu.roll(total[KS:], KS // 2, 1)
    near = cos_part + jnp.where(lower, sin_part, -sin_part)
    far = jnp.where(lower, cos_part - sin_part, -cos_part - sin_part)
    full = jnp.zeros((KS, 2 * KS), F32)
    for part in split(jnp.concatenate([near, far], 1)):
        full = full + mul(part, unfold)
    column = jnp.transpose(edge)
    lane = lanes_of((KS, KS))
    re_ref[...] = jnp.transpose(jnp.where(lane == 0, column[:, 0:1], full[:, :KS]))
    im_ref[...] = jnp.transpose(jnp.where(lane == 0, column[:, 1:2], full[:, KS:]))


def list_slots(rank, core, meta_ref, list_ref):
    listed = jnp.int32(0)
    before = jnp.int32(0)
    for index in range(SRC):
        row = (index >> 1) + ((index + core) & 1) * GATHER
        count = meta_ref[row, 2 * CAP].astype(jnp.int32)
        first = (rank - before) & (GROUP - 1)
        for turn in range(CAP // GROUP):
            position = first + turn * GROUP
            list_ref[listed] = row * META_LANES + position
            listed = listed + jnp.where(position < count, 1, 0)
        before = before + count
    for extra in range(BATCH):
        list_ref[listed + extra] = UNUSED
    return listed


def window(code, re_ref, im_ref, pupil):
    first = code >> 6
    rows = pl.ds(code & (KP - 1), KP)
    real = pltpu.roll(re_ref[rows, :], (KS - first) & (KS - 1), 1)
    imag = pltpu.roll(im_ref[rows, :], KP - first, 1)
    return jnp.where(lanes_of((KP, KS)) < KP, real, imag) * pupil


def transform(high, low, right, right_low):
    return mul(jnp.concatenate([high, low], 1), right) + mul(high, right_low)


def pull(high, low, right_t):
    both = mul(high, right_t)
    return both[:, :KS] + both[:, KS:] + mul(low, right_t[:, :KS])


def turn(values):
    pieces = [values[place * KP : (place + 1) * KP] for place in range(values.shape[0] // KP)]
    return jnp.concatenate(
        [jnp.transpose(jnp.concatenate([piece[:, :SUB], piece[:, SUB:]], 0)) for piece in pieces], 0
    )


def turn_back(values):
    turned = [jnp.transpose(values[place * SUB : (place + 1) * SUB]) for place in range(values.shape[0] // SUB)]
    return jnp.concatenate([jnp.concatenate([piece[:KP], piece[KP:]], 1) for piece in turned], 0)


IMAGE_TABLES = ("waves", "unfold", "right", "right_low", "pupil")


def image_kernel(*refs):
    inputs, refs = refs[:7], refs[7:]
    (sums_out, codes_out, weights_out, slots_out, listed_out, field_out), refs = refs[:6], refs[6:]
    out_ref, re_ref, im_ref, field_ref, inner_ref, meta_ref, list_ref, sems, field_sems = refs
    mine_ref, other_ref, waves_ref, unfold_ref, right_ref, right_low_ref, pupil_ref = inputs
    me = lax.axis_index("src")
    core = me & 1
    metas = [
        pltpu.make_async_copy(
            inputs[place].at[:, META], meta_ref.at[pl.ds(place * GATHER, GATHER)], sems.at[place]
        )
        for place in range(2)
    ]
    for copy in metas:
        copy.start()
    total, edge = transform_rows(mine_ref, other_ref, waves_ref, core)
    wait_all(metas)
    rank = core + 2 * (me >> 5)
    listed = list_slots(rank, core, meta_ref, list_ref)
    listed_out[0] = listed
    unpack_spectrum(total, edge, unfold_ref[...], re_ref, im_ref)
    right, right_low = right_ref[...], right_low_ref[...]
    pupil = pupil_ref[...]
    out_ref[...] = jnp.zeros_like(out_ref)
    batches = (listed + BATCH - 1) // BATCH

    def store(index):
        return pltpu.make_async_copy(field_ref.at[index], field_out.at[index], field_sems.at[index])

    def first_stage(index):
        masked = []
        for place in range(BATCH):
            position = index * BATCH + place
            where = list_ref[position]
            row, lane = where >> 5, where & (META_LANES - 1)
            code = meta_ref[row, lane].astype(jnp.int32)
            codes_out[position] = code
            weights_out[position] = meta_ref[row, CAP + lane]
            source = 2 * (row & (GATHER - 1)) + ((core + (row >> 5)) & 1)
            slots_out[position] = jnp.where(lane == UNUSED, -1, source * CAP + lane)
            masked.append(window(code, re_ref, im_ref, pupil))
        values = transform(*split(jnp.concatenate(masked, 0)), right, right_low)
        inner_ref[0], inner_ref[1] = split(turn(values))

    def second_stage(index, total):
        base = index * BATCH
        values = transform(inner_ref[0], inner_ref[1], right, right_low)
        field_ref[index] = values
        store(index).start()
        acc = out_ref[0:SUB, :]
        for place in range(BATCH):
            weight = weights_out[base + place]
            piece = values[place * SUB : (place + 1) * SUB]
            squares = piece * piece
            acc = acc + weight * (squares[:, :SUB] + squares[:, SUB:])
            total = total + weight
        out_ref[0:SUB, :] = acc
        return total

    def step(index, total):
        total = second_stage(index, total)
        first_stage(index + 1)
        return total

    first_stage(0)
    total = lax.fori_loop(0, batches - 1, step, jnp.float32(0.0))
    total = second_stage(batches - 1, total)
    out_ref[SUB:SUMS, :] = jnp.full((SUMS - SUB, 128), total, F32)
    last = pltpu.make_async_copy(out_ref, sums_out, sems.at[2])
    last.start()

    def finish(index, carry):
        store(index).wait()
        return carry

    lax.fori_loop(0, batches, finish, 0)
    last.wait()


GRAD_TABLES = (
    "interp", "interp_t", "right_t", "fold", "flip", "pupil",
)


KEPT_IN_HBM = (GROUP, GROUP + 3, GROUP + 4, GROUP + 5, GROUP + 6, GROUP + 7)


def grad_kernel(*refs):
    sums, refs = refs[:GROUP], refs[GROUP:]
    (pixel_hbm, rects_ref, rects_t_ref, field_hbm), refs = refs[:4], refs[4:]
    lists_hbm, refs = refs[:4], refs[4:]
    tabs, refs = refs[: len(GRAD_TABLES)], refs[len(GRAD_TABLES) :]
    (out_ref, aerial_ref, loss_ref), refs = refs[:3], refs[3:]
    (pixel_ref, field_ref), refs = refs[:2], refs[2:]
    lists, refs = refs[:4], refs[4:]
    spread_ref, aer_ref, cnt_ref, g_ref, rows_ref, grad_refs, inner_ref, sems, pixel_sems, field_sems = refs
    interp_ref, interp_t_ref, right_t_ref, fold_ref, flip_ref, pupil_ref = tabs
    codes_ref, weights_ref, slots_ref, listed_ref = lists
    me = lax.axis_index("src")
    half = NPIX // 2
    blocks = half // BLOCK

    firsts = start_all(lists_hbm, lists, sems)
    pixel_copies = [
        pltpu.make_async_copy(
            pixel_hbm.at[pl.ds(place * BLOCK, BLOCK)], pixel_ref.at[pl.ds(place * BLOCK, BLOCK)], pixel_sems.at[place]
        )
        for place in range(2 * blocks)
    ]
    for place in range(blocks):
        pixel_copies[place].start()
        pixel_copies[blocks + place].start()
    def load(index):
        return pltpu.make_async_copy(field_hbm.at[index], field_ref.at[index], field_sems.at[index])

    image = sums[0][...]
    for ref in sums[1:]:
        image = image + ref[...]
    total = image[SUB : SUB + 1, 0:1]
    scaled = image[0:SUB] / total
    top, bottom = scaled[: SUB // 2], scaled[SUB // 2 :]
    lower = lanes_of((BLOCK, SUB)) < SUB // 2
    zero = jnp.zeros((SUB // 2, half), BF16)
    samples = []
    for parity in range(2):
        high, low = split(top - bottom if parity else top + bottom)
        samples.append(jnp.concatenate([high, high, low, jnp.zeros_like(low)], 0))
        table = interp_t_ref[parity]
        lows = [zero, table[SUB // 2 :]] if parity else [table[SUB // 2 :], zero]
        spread_ref[parity] = jnp.concatenate([table[: SUB // 2], table[: SUB // 2]] + lows, 0)

    col = lax.broadcasted_iota(jnp.int32, (128, NPIX), 1)
    col_in = ((col >= rects_ref[:, 2:3]) & (col < rects_ref[:, 3:4])).astype(F32).astype(BF16)

    def prepare(place):
        table_rows = pl.ds(place * BLOCK, BLOCK)
        parts = []
        for parity in range(2):
            table = interp_ref[parity, table_rows, :]
            parts.append(mul(jnp.concatenate([table, table], 1), samples[parity]))
        for first, values in ((place * BLOCK, parts[0] + parts[1]), (half + place * BLOCK, parts[0] - parts[1])):
            rows = pl.ds(first, BLOCK)
            turned = pltpu.roll(values, SUB // 2, 1)
            sides = jnp.where(lower, values + turned, turned - values)
            high = sides.astype(BF16)
            wide = high.astype(F32)
            low = pltpu.roll(sides - wide, SUB // 2, 1)
            even_in = jnp.concatenate([jnp.where(lower, wide, low).astype(BF16), high], 1)
            odd_in = jnp.concatenate([jnp.where(lower, low, wide).astype(BF16), high], 1)
            even, odd = mul(even_in, spread_ref[0]), mul(odd_in, spread_ref[1])
            aer_ref[rows, :half] = even + odd
            aer_ref[rows, half:] = even - odd
            row = lax.broadcasted_iota(jnp.int32, (BLOCK, 128), 0) + first
            row_in = ((row >= rects_t_ref[0:1, :]) & (row < rects_t_ref[1:2, :])).astype(F32).astype(BF16)
            cnt_ref[rows, :] = mul(row_in, col_in)

    loss = jnp.zeros((CHUNK, NPIX), F32)

    def chunk_gradient(first, loss):
        rows = pl.ds(first, CHUNK)
        wave = jnp.tanh((STEEP / 2.0) * aer_ref[rows, :] - (STEEP * THRESH / 2.0))
        mismatch = 0.5 * wave + (0.5 - jnp.minimum(cnt_ref[rows, :], 1.0))
        weighted = pixel_ref[rows, :] * mismatch
        return weighted * ((STEEP / 2.0) - (STEEP / 2.0) * (wave * wave)), loss + weighted * mismatch

    totals = [None, None]
    for place in range(blocks):
        prepare(place)
    wait_all(firsts)
    batches = (listed_ref[0] + BATCH - 1) // BATCH

    def begin(index, carry):
        load(index).start()
        return carry

    lax.fori_loop(0, batches, begin, 0)
    for place in range(blocks):
        pixel_copies[place].wait()
        pixel_copies[blocks + place].wait()
        for index in range(BLOCK // CHUNK):
            near, loss = chunk_gradient(place * BLOCK + index * CHUNK, loss)
            far, loss = chunk_gradient(half + place * BLOCK + index * CHUNK, loss)
            rows = pl.ds(index * CHUNK, CHUNK)
            for parity, values in ((0, near + far), (1, near - far)):
                g_ref[place, parity, 0, rows, :], g_ref[place, parity, 1, rows, :] = split(values)
        for parity in range(2):
            table = interp_t_ref[parity, :, pl.ds(place * BLOCK, BLOCK)]
            both = mul(table, g_ref[place, parity, 0])
            part = both[: SUB // 2] + both[SUB // 2 :] + mul(table[: SUB // 2], g_ref[place, parity, 1])
            totals[parity] = part if place == 0 else rows_ref[parity] + part
            rows_ref[parity] = totals[parity]

    reduced = jnp.concatenate([totals[0] + totals[1], totals[0] - totals[1]], 0)
    below = lanes_of((SUB, SUB)) < SUB // 2
    sides = []
    for parity in range(2):
        left_half, right_half = reduced[:, :half], reduced[:, half:]
        high, low = split(left_half - right_half if parity else left_half + right_half)
        both = mul(jnp.concatenate([high, low], 0), interp_ref[parity])
        first, second = both[:SUB], both[SUB:]
        second = jnp.where(below, second, pltpu.roll(second, SUB // 2, 1))
        sides.append(first + pltpu.roll(first, SUB // 2, 1) + second)
    kernel = sides[0] + jnp.where(below, sides[1], -sides[1])
    aerial_ref[...] = aer_ref[pl.ds(pl.multiple_of(me * ROWS, ROWS), ROWS), :]
    loss_ref[0] = jnp.sum(loss) / (NPIX * NPIX)
    right_t = right_t_ref[...]
    pupil = pupil_ref[...]
    common = jnp.sum(kernel * scaled)
    grad_refs[...] = jnp.zeros_like(grad_refs)
    number = slot_numbers()
    lane = lanes_of((KP, KS))
    kernel2 = jnp.concatenate([kernel, kernel], 1)

    def finish_load(index, carry):
        load(index).wait()
        return carry

    lax.fori_loop(0, batches, finish_load, 0)

    def first_stage(index, terms):
        cotangents = []
        for place in range(BATCH):
            piece = field_ref[index, pl.ds(place * SUB, SUB), :]
            cotangent = piece * kernel2
            strength = jnp.sum(piece * cotangent, axis=(0, 1), keepdims=True)
            terms = jnp.where(number == slots_ref[index * BATCH + place], strength - common, terms)
            cotangents.append(cotangent)
        values = pull(*split(jnp.concatenate(cotangents, 0)), right_t)
        inner_ref[0], inner_ref[1] = split(turn_back(values))
        return terms

    def second_stage(index):
        grads = pull(inner_ref[0], inner_ref[1], right_t)
        for place in range(BATCH):
            scaled_grad = grads[place * KP : (place + 1) * KP] * pupil * (2.0 * weights_ref[index * BATCH + place])
            code = codes_ref[index * BATCH + place]
            first = code >> 6
            rows = pl.ds(code & (KP - 1), KP)
            grad_refs[0, rows, :] += pltpu.roll(jnp.where(lane < KP, scaled_grad, 0.0), first, 1)
            grad_refs[1, rows, :] += pltpu.roll(jnp.where(lane < KP, 0.0, scaled_grad), first + KP, 1)

    def back(index, terms):
        second_stage(index)
        return first_stage(index + 1, terms)

    terms = first_stage(0, jnp.zeros(number.shape, F32))
    terms = lax.fori_loop(0, batches - 1, back, terms)
    second_stage(batches - 1)
    real_t, imag_t = grad_refs[0] / total, grad_refs[1] / total
    real, imag = jnp.transpose(real_t), jnp.transpose(imag_t)
    sub = lax.broadcasted_iota(jnp.int32, (8, KS), 0)
    edge = jnp.where(sub == 0, real_t[0:1], imag_t[0:1])
    kept = jnp.zeros((KS, KS), F32)
    mirrored = jnp.zeros((EDGE_ROWS, KS), F32)
    for part in split(jnp.concatenate([real, imag], 1)):
        folded = mul(part, fold_ref[...])
        kept = kept + folded[:, :KS]
        mirrored = mirrored + mul(flip_ref[...], folded[:, KS:].astype(BF16))
    out_ref[0:KS, :] = kept + mirrored[0:KS]
    out_ref[MIRROR_ROW:EDGE_ROWS, :] = mirrored[KS:]
    out_ref[EDGE_ROWS:TERM_ROWS, :] = jnp.where(sub < 2, edge, 0.0)
    blank = jnp.zeros((GRAD - TERM_ROWS - SLOTS // 128, 128), F32)
    out_ref[TERM_ROWS:GRAD, :] = jnp.concatenate([terms / (total * NPIX), blank], 0)


def mask_kernel(*refs):
    packs, refs = refs[:GROUP], refs[GROUP:]
    mask_ref, own_hbm, cols_ref, out_ref, slot_ref, own_ref, terms_vmem, terms_smem, sems = refs
    me = lax.axis_index("src")
    table = pltpu.make_async_copy(own_hbm.at[me], own_ref, sems.at[0])
    table.start()
    packed = packs[0][...]
    for ref in packs[1:]:
        packed = packed + ref[...]
    terms_vmem[...] = packed[TERM_ROWS:GRAD]
    fetch = pltpu.make_async_copy(terms_vmem, terms_smem, sems.at[1])
    fetch.start()
    table.wait()
    used = EDGE_ROWS
    pulled = mul3((own_ref[0, :, :used], own_ref[1, :, :used]), split(packed[0:used]))
    sin_part = pltpu.roll(pulled[ROWS:], KS // 2, 1)
    lane = lanes_of((ROWS, KS))
    main = pulled[:ROWS] + jnp.where(lane < KS // 2, -sin_part, sin_part)
    edge = packed[EDGE_ROWS:TERM_ROWS]
    blank = jnp.zeros((KS - 16, KS), F32)
    none = jnp.zeros((8, KS), F32)
    cos_rows = (own_ref[0, :ROWS, :KS], own_ref[1, :ROWS, :KS])
    sin_rows = (own_ref[0, ROWS:, :KS], own_ref[1, ROWS:, :KS])
    contract = ((1,), (1,))
    side = mul3(cos_rows, split(jnp.concatenate([edge, none, blank], 0)), contract) + mul3(
        sin_rows, split(jnp.concatenate([none, edge, blank], 0)), contract
    )
    gathered = split(jnp.concatenate([main, side], 1))
    transmit = jnp.tanh(mask_ref[...])
    out_ref[...] = mul3_few(gathered, pair(cols_ref)) * (1.0 - transmit * transmit)
    fetch.wait()
    for slot in range(CAP):
        place = me * CAP + slot
        slot_ref[slot] = terms_smem[place >> 7, place & 127]


def exchange(value, others):
    received = [value]
    for other in others:
        pairs = [(index, index ^ other) for index in range(SRC)]
        received.append(lax.ppermute(value, "src", pairs))
    return received


MIB = 1024 * 1024


def run(kernel, name, operands, outputs, scratch, limit, in_vmem=()):
    smem = pl.BlockSpec(memory_space=pltpu.SMEM)
    hbm = pl.BlockSpec(memory_space=pltpu.HBM)
    vmem = pl.BlockSpec(memory_space=pltpu.VMEM)
    kinds = {"smem": smem, "hbm": hbm, "vmem": vmem}
    return pl.pallas_call(
        kernel,
        in_specs=[vmem if place in in_vmem else hbm for place in range(len(operands))],
        out_specs=[kinds[kind] for kind, unused, unused in outputs],
        out_shape=[jax.ShapeDtypeStruct(shape, dtype) for unused, shape, dtype in outputs],
        scratch_shapes=scratch,
        compiler_params=pltpu.CompilerParams(vmem_limit_bytes=limit * MIB),
        name=name,
    )(*operands)


def body(mask_param, pixel_weight, source_weight, point_index, point_count, target_rects):
    table = tables()
    vmem = lambda array: pltpu.VMEM(array.shape, array.dtype)
    smem = lambda array: pltpu.SMEM(array.shape, array.dtype)
    dma = lambda count: pltpu.SemaphoreType.DMA((count,))

    (block,) = run(
        project_kernel,
        "project",
        [point_index, point_count, source_weight, mask_param, table["cols"], table["own"]],
        [("vmem", (GATHER, PACK, 128), F32)],
        [
            smem(point_index), smem(point_count), smem(source_weight), vmem(mask_param), vmem(table["cols"]),
            vmem(table["own"][0]), dma(6),
        ],
        60,
    )

    same_core = [list(range(core, SRC, 2)) for core in range(2)]
    mine = lax.all_to_all(block, "src", 0, 0, axis_index_groups=same_core, tiled=True)
    unused, other = exchange(mine, CORE)

    operands = [mine, other] + [table[name] for name in IMAGE_TABLES]
    listed = SLOTS // GROUP + BATCH
    sums, codes, weights, slots, count, field = run(
        image_kernel,
        "image",
        operands,
        [
            ("hbm", (SUMS, 128), F32),
            ("smem", (listed,), jnp.int32),
            ("smem", (listed,), F32),
            ("smem", (listed,), jnp.int32),
            ("smem", (1,), jnp.int32),
            ("hbm", (BATCHES, BATCH * SUB, 2 * SUB), F32),
        ],
        [
            pltpu.VMEM((SUMS, 128), F32),
            pltpu.VMEM((KS, KS), F32),
            pltpu.VMEM((KS, KS), F32),
            pltpu.VMEM((BATCHES, BATCH * SUB, 2 * SUB), F32),
            pltpu.VMEM((2, BATCH * SUB, KS), BF16),
            pltpu.SMEM((SRC, 128), F32),
            pltpu.SMEM((listed,), jnp.int32),
            dma(3),
            dma(BATCHES),
        ],
        44,
        range(len(operands)),
    )

    all_sums = exchange(sums, GROUP_DEVICES)
    rects_t = target_rects.T
    lists = [codes, weights, slots, count]
    constants = [table[name] for name in GRAD_TABLES]
    grad, aerial, loss = run(
        grad_kernel,
        "gradient",
        all_sums + [pixel_weight, target_rects, rects_t, field] + lists + constants,
        [("vmem", (GRAD, 128), F32), ("vmem", (ROWS, NPIX), F32), ("smem", (1,), F32)],
        [vmem(array) for array in [pixel_weight, field]]
        + [smem(array) for array in lists]
        + [
            pltpu.VMEM((2, 2 * SUB, NPIX // 2), BF16),
            pltpu.VMEM((NPIX, NPIX), F32),
            pltpu.VMEM((NPIX, NPIX), F32),
            pltpu.VMEM((NPIX // 2 // BLOCK, 2, 2, BLOCK, NPIX), BF16),
            pltpu.VMEM((2, SUB // 2, NPIX), F32),
            pltpu.VMEM((2, KS, KS), F32),
            pltpu.VMEM((2, BATCH * KP, 2 * SUB), BF16),
            dma(len(lists)),
            dma(NPIX // BLOCK),
            dma(BATCHES),
        ],
        52,
        [place for place in range(GROUP + 8 + len(constants)) if place not in KEPT_IN_HBM],
    )

    grads = exchange(grad, GROUP_DEVICES)
    operands = grads + [mask_param, table["own"], table["cols_t"]]
    mask_grad, source_grad = run(
        mask_kernel,
        "mask",
        operands,
        [("vmem", (ROWS, NPIX), F32), ("smem", (CAP,), F32)],
        [vmem(table["own"][0]), pltpu.VMEM((8, 128), F32), pltpu.SMEM((8, 128), F32), dma(2)],
        32,
        [place for place in range(len(operands)) if place != GROUP + 1],
    )
    return mask_grad, aerial, source_grad, loss


def solution(mesh):
    in_specs = (P(("clip", "src"), None), P("clip", None), P(), P("src"), P("src"), P("clip", None))
    out_specs = (P(("clip", "src"), None), P(("clip", "src"), None), P(("clip", "src")), P("clip"))
    return jax.shard_map(body, mesh=mesh, in_specs=in_specs, out_specs=out_specs, check_vma=False)
```

```python
import functools
import math

import jax
import jax.numpy as jnp
import ml_dtypes
import numpy as np
from jax import lax
from jax.experimental import pallas as pl
from jax.experimental.pallas import tpu as pltpu
from jax.sharding import PartitionSpec as P

NPIX = 1024
KS = 128
KP = 64
SG = 101
CAP = 8
SRC = 64
SLOTS = SRC * CAP
ROWS = NPIX // SRC
SUB = 128
BLOCK = 256
CHUNK = 16
STEEP = 10.0
THRESH = 0.3

EDGE = ROWS
META = EDGE + 2
PACK = 24
META_LANES = 32
UNUSED = 3 * CAP
GATHER = 32
SUMS = 136
MIRROR_ROW = KS
EDGE_ROWS = KS + 8
TERM_ROWS = KS + 16
GRAD = KS + 24

CORE = (1,)
GROUP_DEVICES = (32, 33, 1)
GROUP = 4
BATCH = 8
BATCHES = SLOTS // GROUP // BATCH

F32 = jnp.float32
BF16 = jnp.bfloat16


def halves(table):
    table = np.asarray(table, np.float64)
    high = table.astype(ml_dtypes.bfloat16)
    low = (table - high.astype(np.float64)).astype(ml_dtypes.bfloat16)
    return np.stack([high, low])


def angles(left, right, period):
    return 2.0 * math.pi * np.mod(np.multiply.outer(left, right), period) / period


@functools.lru_cache(None)
def tables():
    pixels = np.arange(NPIX)
    cols = np.zeros((NPIX, 2 * KS))
    phase = angles(pixels, np.arange(KS // 2), NPIX)
    cols[:, : KS // 2] = np.cos(phase)
    cols[:, KS // 2 : KS] = -np.sin(phase)
    edge = angles(pixels, -KS // 2, NPIX)
    cols[:, KS] = np.cos(edge)
    cols[:, KS + 1] = -np.sin(edge)
    cols[:, KS + 8] = -np.sin(edge)
    cols[:, KS + 9] = -np.cos(edge)
    cols /= NPIX

    phase = angles(np.arange(KS + 1) - KS // 2, pixels, NPIX).reshape(KS + 1, SRC, ROWS)
    wave = np.stack([np.cos(phase), np.sin(phase)]) / NPIX
    by_core = wave[:, :KS].reshape(2 * KS, GATHER, 2, ROWS).transpose(2, 0, 1, 3)
    waves = by_core.reshape(2, 2 * KS, GATHER * ROWS)
    own = np.zeros((SRC, 2 * ROWS, 2 * KS))
    own[:, :, : KS + 1] = wave.transpose(2, 0, 3, 1).reshape(SRC, 2 * ROWS, KS + 1)

    half = KS // 2
    keep = np.zeros((KS, 2 * KS))
    mirror = np.zeros((KS, 2 * KS))
    for freq in range(half):
        keep[freq, half + freq] = 1.0
        keep[half + freq, KS + half + freq] = 1.0
        if freq:
            mirror[freq, half - freq] = 1.0
            mirror[half + freq, KS + half - freq] = 1.0
    flip = np.zeros((EDGE_ROWS, KS))
    flip[KS - np.arange(KS), np.arange(KS)] = 1.0
    conj = mirror * np.where(np.arange(KS) < half, 1.0, -1.0)[:, None]

    phase = angles(np.arange(KP) - KP // 2, np.arange(SUB), SUB)
    cos_part, sin_part = np.cos(phase), np.sin(phase)
    right = np.block([[cos_part, sin_part], [-sin_part, cos_part]])

    shift = pixels[: NPIX // 2, None] - (NPIX // SUB) * np.arange(SUB // 2)[None, :]
    interp = np.zeros((2, NPIX // 2, SUB // 2))
    interp[0] = 1.0
    for freq in range(1, SUB // 2):
        interp[freq % 2] += 2.0 * np.cos(2.0 * math.pi * np.mod(freq * shift, NPIX) / NPIX)
    interp /= SUB

    freq = np.arange(KP) - KP // 2
    pupil = (freq[:, None] ** 2 + freq[None, :] ** 2 < (KP // 2) ** 2).astype(np.float32)
    as_bf16 = lambda table: table.astype(ml_dtypes.bfloat16)
    high_low = lambda table, axis: np.concatenate(list(halves(table)), axis)
    twice = lambda table, axis: np.concatenate([halves(table)[0]] * 2, axis)
    return dict(
        cols=halves(cols),
        cols_t=halves(cols.T),
        waves=halves(waves).transpose(1, 0, 2, 3),
        own=halves(own).transpose(1, 0, 2, 3),
        unfold=as_bf16(np.concatenate([keep, mirror], 0)),
        fold=as_bf16(np.concatenate([keep.T, conj.T], 1)),
        flip=as_bf16(flip),
        right=twice(right, 0),
        right_low=halves(right)[1],
        right_t=high_low(right.T, 1),
        interp=high_low(interp, 2),
        interp_t=high_low(interp.transpose(0, 2, 1), 1),
        pupil=np.concatenate([pupil, pupil], 1),
    )


def split(values):
    high = values.astype(BF16)
    low = (values - high.astype(F32)).astype(BF16)
    return high, low


def mul(first, second, dims=((1,), (0,))):
    return lax.dot_general(first, second, (dims, ((), ())), preferred_element_type=F32)


def mul3(first, second, dims=((1,), (0,))):
    return (
        mul(first[0], second[0], dims) + mul(first[0], second[1], dims) + mul(first[1], second[0], dims)
    )


def mul3_few(first, second):
    rows = first[0].shape[0]
    both = mul(jnp.concatenate(first, 0), second[0])
    return both[:rows] + both[rows:] + mul(first[0], second[1])


def pair(ref):
    return ref[0], ref[1]


def div_sg(number):
    return (number * 41529) >> 22


def offset(grid):
    return ((grid - SG // 2) * (KP // 2) + 51 * 64) // 51 - 64 + KP // 2


def lanes_of(shape):
    return lax.broadcasted_iota(jnp.int32, shape, 1)


def slot_numbers():
    shape = (SLOTS // 128, 128)
    return lax.broadcasted_iota(jnp.int32, shape, 0) * 128 + lanes_of(shape)


def start_all(sources, targets, sems):
    copies = [
        pltpu.make_async_copy(source, target, sems.at[place])
        for place, (source, target) in enumerate(zip(sources, targets))
    ]
    for copy in copies:
        copy.start()
    return copies


def wait_all(copies):
    for copy in copies:
        copy.wait()


def project_kernel(
    index_hbm, count_hbm, weight_hbm, mask_hbm, cols_hbm, own_hbm, out_ref,
    index_ref, count_ref, weight_ref, mask_ref, cols_ref, own_ref, sems,
):
    me = lax.axis_index("src")
    copies = start_all(
        (mask_hbm, cols_hbm, own_hbm.at[me], index_hbm, count_hbm, weight_hbm),
        (mask_ref, cols_ref, own_ref, index_ref, count_ref, weight_ref),
        sems,
    )
    copies[0].wait()
    transmit = split(jnp.tanh(mask_ref[...]))
    copies[1].wait()
    projected = mul3_few(transmit, pair(cols_ref))
    wait_all(copies[2:])
    edge = split(projected[:, KS:])
    cos_rows = (own_ref[0, :ROWS, :KS], own_ref[1, :ROWS, :KS])
    sin_rows = (own_ref[0, ROWS:, :KS], own_ref[1, ROWS:, :KS])
    contract = ((0,), (0,))
    edge_rows = mul3(edge, cos_rows, contract)[0:8] + mul3(edge, sin_rows, contract)[8:16]
    shape = (PACK - EDGE, 128)
    lane = lanes_of(shape)
    sub = lax.broadcasted_iota(jnp.int32, shape, 0)
    count = count_ref[0]
    meta = jnp.where(lane == 2 * CAP, count.astype(F32), 0.0)
    for slot in range(CAP):
        point = index_ref[slot]
        grid_row = div_sg(point)
        grid_col = point - grid_row * SG
        code = offset(grid_row) * KP + offset(grid_col)
        meta = jnp.where(lane == slot, code.astype(F32), meta)
        meta = jnp.where(lane == CAP + slot, weight_ref[grid_row, grid_col], meta)
    tail = jnp.where(sub < 2, edge_rows, jnp.where(sub == 2, meta, 0.0))
    block = jnp.concatenate([projected[:, :KS], tail], 0)
    for place in range(GATHER):
        out_ref[place] = block


def transform_rows(mine_ref, other_ref, waves_ref, core):
    total = jnp.zeros((2 * KS, KS), F32)
    edge = jnp.zeros((PACK - EDGE, KS), F32)
    for ref, which in ((mine_ref, core), (other_ref, 1 - core)):
        gathered = ref[...]
        high, low = split(gathered[:, :ROWS].reshape(GATHER * ROWS, KS))
        both = mul(waves_ref[which, 0], jnp.concatenate([high, low], 1))
        total = total + both[:, :KS] + both[:, KS:] + mul(waves_ref[which, 1], high)
        edge = edge + jnp.sum(gathered[:, EDGE:], 0)
    return total, edge


def unpack_spectrum(total, edge, unfold, re_ref, im_ref):
    lower = lanes_of((KS, KS)) < KS // 2
    cos_part = total[:KS]
    sin_part = pltpu.roll(total[KS:], KS // 2, 1)
    near = cos_part + jnp.where(lower, sin_part, -sin_part)
    far = jnp.where(lower, cos_part - sin_part, -cos_part - sin_part)
    full = jnp.zeros((KS, 2 * KS), F32)
    for part in split(jnp.concatenate([near, far], 1)):
        full = full + mul(part, unfold)
    column = jnp.transpose(edge)
    lane = lanes_of((KS, KS))
    re_ref[...] = jnp.transpose(jnp.where(lane == 0, column[:, 0:1], full[:, :KS]))
    im_ref[...] = jnp.transpose(jnp.where(lane == 0, column[:, 1:2], full[:, KS:]))


def list_slots(rank, core, meta_ref, list_ref):
    listed = jnp.int32(0)
    before = jnp.int32(0)
    for index in range(SRC):
        row = (index >> 1) + ((index + core) & 1) * GATHER
        count = meta_ref[row, 2 * CAP].astype(jnp.int32)
        first = (rank - before) & (GROUP - 1)
        for turn in range(CAP // GROUP):
            position = first + turn * GROUP
            list_ref[listed] = row * META_LANES + position
            listed = listed + jnp.where(position < count, 1, 0)
        before = before + count
    for extra in range(BATCH):
        list_ref[listed + extra] = UNUSED
    return listed


def window(code, re_ref, im_ref, pupil):
    first = code >> 6
    rows = pl.ds(code & (KP - 1), KP)
    real = pltpu.roll(re_ref[rows, :], (KS - first) & (KS - 1), 1)
    imag = pltpu.roll(im_ref[rows, :], KP - first, 1)
    return jnp.where(lanes_of((KP, KS)) < KP, real, imag) * pupil


def transform(high, low, right, right_low):
    return mul(jnp.concatenate([high, low], 1), right) + mul(high, right_low)


def pull(high, low, right_t):
    both = mul(high, right_t)
    return both[:, :KS] + both[:, KS:] + mul(low, right_t[:, :KS])


def turn(values):
    pieces = [values[place * KP : (place + 1) * KP] for place in range(values.shape[0] // KP)]
    return jnp.concatenate(
        [jnp.transpose(jnp.concatenate([piece[:, :SUB], piece[:, SUB:]], 0)) for piece in pieces], 0
    )


def turn_back(values):
    turned = [jnp.transpose(values[place * SUB : (place + 1) * SUB]) for place in range(values.shape[0] // SUB)]
    return jnp.concatenate([jnp.concatenate([piece[:KP], piece[KP:]], 1) for piece in turned], 0)


IMAGE_TABLES = ("waves", "unfold", "right", "right_low", "pupil")


def image_kernel(*refs):
    inputs, refs = refs[:7], refs[7:]
    (sums_out, codes_out, weights_out, slots_out, listed_out, field_out), refs = refs[:6], refs[6:]
    out_ref, re_ref, im_ref, field_ref, inner_ref, meta_ref, list_ref, sems, field_sems = refs
    mine_ref, other_ref, waves_ref, unfold_ref, right_ref, right_low_ref, pupil_ref = inputs
    me = lax.axis_index("src")
    core = me & 1
    metas = [
        pltpu.make_async_copy(
            inputs[place].at[:, META], meta_ref.at[pl.ds(place * GATHER, GATHER)], sems.at[place]
        )
        for place in range(2)
    ]
    for copy in metas:
        copy.start()
    total, edge = transform_rows(mine_ref, other_ref, waves_ref, core)
    wait_all(metas)
    rank = core + 2 * (me >> 5)
    listed = list_slots(rank, core, meta_ref, list_ref)
    listed_out[0] = listed
    unpack_spectrum(total, edge, unfold_ref[...], re_ref, im_ref)
    right, right_low = right_ref[...], right_low_ref[...]
    pupil = pupil_ref[...]
    out_ref[...] = jnp.zeros_like(out_ref)
    batches = (listed + BATCH - 1) // BATCH

    def store(index):
        return pltpu.make_async_copy(field_ref.at[index], field_out.at[index], field_sems.at[index])

    def first_stage(index):
        masked = []
        for place in range(BATCH):
            position = index * BATCH + place
            where = list_ref[position]
            row, lane = where >> 5, where & (META_LANES - 1)
            code = meta_ref[row, lane].astype(jnp.int32)
            codes_out[position] = code
            weights_out[position] = meta_ref[row, CAP + lane]
            source = 2 * (row & (GATHER - 1)) + ((core + (row >> 5)) & 1)
            slots_out[position] = jnp.where(lane == UNUSED, -1, source * CAP + lane)
            masked.append(window(code, re_ref, im_ref, pupil))
        values = transform(*split(jnp.concatenate(masked, 0)), right, right_low)
        inner_ref[0], inner_ref[1] = split(turn(values))

    def second_stage(index, total):
        base = index * BATCH
        values = transform(inner_ref[0], inner_ref[1], right, right_low)
        field_ref[index] = values
        store(index).start()
        acc = out_ref[0:SUB, :]
        for place in range(BATCH):
            weight = weights_out[base + place]
            piece = values[place * SUB : (place + 1) * SUB]
            squares = piece * piece
            acc = acc + weight * (squares[:, :SUB] + squares[:, SUB:])
            total = total + weight
        out_ref[0:SUB, :] = acc
        return total

    def step(index, total):
        total = second_stage(index, total)
        first_stage(index + 1)
        return total

    first_stage(0)
    total = lax.fori_loop(0, batches - 1, step, jnp.float32(0.0))
    total = second_stage(batches - 1, total)
    out_ref[SUB:SUMS, :] = jnp.full((SUMS - SUB, 128), total, F32)
    last = pltpu.make_async_copy(out_ref, sums_out, sems.at[2])
    last.start()

    def finish(index, carry):
        store(index).wait()
        return carry

    lax.fori_loop(0, batches, finish, 0)
    last.wait()


GRAD_TABLES = (
    "interp", "interp_t", "right_t", "fold", "flip", "pupil",
)


KEPT_IN_HBM = (GROUP, GROUP + 3, GROUP + 4, GROUP + 5, GROUP + 6, GROUP + 7)


def grad_kernel(*refs):
    sums, refs = refs[:GROUP], refs[GROUP:]
    (pixel_hbm, rects_ref, rects_t_ref, field_hbm), refs = refs[:4], refs[4:]
    lists_hbm, refs = refs[:4], refs[4:]
    tabs, refs = refs[: len(GRAD_TABLES)], refs[len(GRAD_TABLES) :]
    (out_ref, aerial_ref, loss_ref), refs = refs[:3], refs[3:]
    (pixel_ref, field_ref), refs = refs[:2], refs[2:]
    lists, refs = refs[:4], refs[4:]
    spread_ref, aer_ref, cnt_ref, g_ref, rows_ref, grad_refs, inner_ref, sems, pixel_sems, field_sems = refs
    interp_ref, interp_t_ref, right_t_ref, fold_ref, flip_ref, pupil_ref = tabs
    codes_ref, weights_ref, slots_ref, listed_ref = lists
    me = lax.axis_index("src")
    half = NPIX // 2
    blocks = half // BLOCK

    firsts = start_all(lists_hbm, lists, sems)
    pixel_copies = [
        pltpu.make_async_copy(
            pixel_hbm.at[pl.ds(place * BLOCK, BLOCK)], pixel_ref.at[pl.ds(place * BLOCK, BLOCK)], pixel_sems.at[place]
        )
        for place in range(2 * blocks)
    ]
    for place in range(blocks):
        pixel_copies[place].start()
        pixel_copies[blocks + place].start()
    def load(index):
        return pltpu.make_async_copy(field_hbm.at[index], field_ref.at[index], field_sems.at[index])

    image = sums[0][...]
    for ref in sums[1:]:
        image = image + ref[...]
    total = image[SUB : SUB + 1, 0:1]
    scaled = image[0:SUB] / total
    top, bottom = scaled[: SUB // 2], scaled[SUB // 2 :]
    lower = lanes_of((BLOCK, SUB)) < SUB // 2
    zero = jnp.zeros((SUB // 2, half), BF16)
    samples = []
    for parity in range(2):
        high, low = split(top - bottom if parity else top + bottom)
        samples.append(jnp.concatenate([high, high, low, jnp.zeros_like(low)], 0))
        table = interp_t_ref[parity]
        lows = [zero, table[SUB // 2 :]] if parity else [table[SUB // 2 :], zero]
        spread_ref[parity] = jnp.concatenate([table[: SUB // 2], table[: SUB // 2]] + lows, 0)

    col = lax.broadcasted_iota(jnp.int32, (128, NPIX), 1)
    col_in = ((col >= rects_ref[:, 2:3]) & (col < rects_ref[:, 3:4])).astype(F32).astype(BF16)

    def prepare(place):
        table_rows = pl.ds(place * BLOCK, BLOCK)
        parts = []
        for parity in range(2):
            table = interp_ref[parity, table_rows, :]
            parts.append(mul(jnp.concatenate([table, table], 1), samples[parity]))
        for first, values in ((place * BLOCK, parts[0] + parts[1]), (half + place * BLOCK, parts[0] - parts[1])):
            rows = pl.ds(first, BLOCK)
            turned = pltpu.roll(values, SUB // 2, 1)
            sides = jnp.where(lower, values + turned, turned - values)
            high = sides.astype(BF16)
            wide = high.astype(F32)
            low = pltpu.roll(sides - wide, SUB // 2, 1)
            even_in = jnp.concatenate([jnp.where(lower, wide, low).astype(BF16), high], 1)
            odd_in = jnp.concatenate([jnp.where(lower, low, wide).astype(BF16), high], 1)
            even, odd = mul(even_in, spread_ref[0]), mul(odd_in, spread_ref[1])
            aer_ref[rows, :half] = even + odd
            aer_ref[rows, half:] = even - odd
            row = lax.broadcasted_iota(jnp.int32, (BLOCK, 128), 0) + first
            row_in = ((row >= rects_t_ref[0:1, :]) & (row < rects_t_ref[1:2, :])).astype(F32).astype(BF16)
            cnt_ref[rows, :] = mul(row_in, col_in)

    loss = jnp.zeros((CHUNK, NPIX), F32)

    def chunk_gradient(first, loss):
        rows = pl.ds(first, CHUNK)
        wave = jnp.tanh((STEEP / 2.0) * aer_ref[rows, :] - (STEEP * THRESH / 2.0))
        mismatch = 0.5 * wave + (0.5 - jnp.minimum(cnt_ref[rows, :], 1.0))
        weighted = pixel_ref[rows, :] * mismatch
        return weighted * ((STEEP / 2.0) - (STEEP / 2.0) * (wave * wave)), loss + weighted * mismatch

    totals = [None, None]
    prepare(0)
    wait_all(firsts)
    batches = (listed_ref[0] + BATCH - 1) // BATCH

    def begin(index, carry):
        load(index).start()
        return carry

    lax.fori_loop(0, batches, begin, 0)
    for place in range(1, blocks):
        prepare(place)
    for place in range(blocks):
        pixel_copies[place].wait()
        pixel_copies[blocks + place].wait()
        for index in range(BLOCK // CHUNK):
            near, loss = chunk_gradient(place * BLOCK + index * CHUNK, loss)
            far, loss = chunk_gradient(half + place * BLOCK + index * CHUNK, loss)
            rows = pl.ds(index * CHUNK, CHUNK)
            for parity, values in ((0, near + far), (1, near - far)):
                g_ref[place, parity, 0, rows, :], g_ref[place, parity, 1, rows, :] = split(values)
        for parity in range(2):
            table = interp_t_ref[parity, :, pl.ds(place * BLOCK, BLOCK)]
            both = mul(table, g_ref[place, parity, 0])
            part = both[: SUB // 2] + both[SUB // 2 :] + mul(table[: SUB // 2], g_ref[place, parity, 1])
            totals[parity] = part if place == 0 else rows_ref[parity] + part
            rows_ref[parity] = totals[parity]

    reduced = jnp.concatenate([totals[0] + totals[1], totals[0] - totals[1]], 0)
    below = lanes_of((SUB, SUB)) < SUB // 2
    sides = []
    for parity in range(2):
        left_half, right_half = reduced[:, :half], reduced[:, half:]
        high, low = split(left_half - right_half if parity else left_half + right_half)
        both = mul(jnp.concatenate([high, low], 0), interp_ref[parity])
        first, second = both[:SUB], both[SUB:]
        second = jnp.where(below, second, pltpu.roll(second, SUB // 2, 1))
        sides.append(first + pltpu.roll(first, SUB // 2, 1) + second)
    kernel = sides[0] + jnp.where(below, sides[1], -sides[1])
    aerial_ref[...] = aer_ref[pl.ds(pl.multiple_of(me * ROWS, ROWS), ROWS), :]
    loss_ref[0] = jnp.sum(loss) / (NPIX * NPIX)
    right_t = right_t_ref[...]
    pupil = pupil_ref[...]
    common = jnp.sum(kernel * scaled)
    grad_refs[...] = jnp.zeros_like(grad_refs)
    number = slot_numbers()
    lane = lanes_of((KP, KS))
    kernel2 = jnp.concatenate([kernel, kernel], 1)

    def finish_load(index, carry):
        load(index).wait()
        return carry

    lax.fori_loop(0, batches, finish_load, 0)

    def first_stage(index, terms):
        cotangents = []
        for place in range(BATCH):
            piece = field_ref[index, pl.ds(place * SUB, SUB), :]
            cotangent = piece * kernel2
            strength = jnp.sum(piece * cotangent, axis=(0, 1), keepdims=True)
            terms = jnp.where(number == slots_ref[index * BATCH + place], strength - common, terms)
            cotangents.append(cotangent)
        values = pull(*split(jnp.concatenate(cotangents, 0)), right_t)
        inner_ref[0], inner_ref[1] = split(turn_back(values))
        return terms

    def second_stage(index):
        grads = pull(inner_ref[0], inner_ref[1], right_t)
        for place in range(BATCH):
            scaled_grad = grads[place * KP : (place + 1) * KP] * pupil * (2.0 * weights_ref[index * BATCH + place])
            code = codes_ref[index * BATCH + place]
            first = code >> 6
            rows = pl.ds(code & (KP - 1), KP)
            grad_refs[0, rows, :] += pltpu.roll(jnp.where(lane < KP, scaled_grad, 0.0), first, 1)
            grad_refs[1, rows, :] += pltpu.roll(jnp.where(lane < KP, 0.0, scaled_grad), first + KP, 1)

    def back(index, terms):
        second_stage(index)
        return first_stage(index + 1, terms)

    terms = first_stage(0, jnp.zeros(number.shape, F32))
    terms = lax.fori_loop(0, batches - 1, back, terms)
    second_stage(batches - 1)
    real_t, imag_t = grad_refs[0] / total, grad_refs[1] / total
    real, imag = jnp.transpose(real_t), jnp.transpose(imag_t)
    sub = lax.broadcasted_iota(jnp.int32, (8, KS), 0)
    edge = jnp.where(sub == 0, real_t[0:1], imag_t[0:1])
    kept = jnp.zeros((KS, KS), F32)
    mirrored = jnp.zeros((EDGE_ROWS, KS), F32)
    for part in split(jnp.concatenate([real, imag], 1)):
        folded = mul(part, fold_ref[...])
        kept = kept + folded[:, :KS]
        mirrored = mirrored + mul(flip_ref[...], folded[:, KS:].astype(BF16))
    out_ref[0:KS, :] = kept + mirrored[0:KS]
    out_ref[MIRROR_ROW:EDGE_ROWS, :] = mirrored[KS:]
    out_ref[EDGE_ROWS:TERM_ROWS, :] = jnp.where(sub < 2, edge, 0.0)
    blank = jnp.zeros((GRAD - TERM_ROWS - SLOTS // 128, 128), F32)
    out_ref[TERM_ROWS:GRAD, :] = jnp.concatenate([terms / (total * NPIX), blank], 0)


def mask_kernel(*refs):
    packs, refs = refs[:GROUP], refs[GROUP:]
    mask_ref, own_hbm, cols_ref, out_ref, slot_ref, own_ref, terms_vmem, terms_smem, sems = refs
    me = lax.axis_index("src")
    table = pltpu.make_async_copy(own_hbm.at[me], own_ref, sems.at[0])
    table.start()
    packed = packs[0][...]
    for ref in packs[1:]:
        packed = packed + ref[...]
    terms_vmem[...] = packed[TERM_ROWS:GRAD]
    fetch = pltpu.make_async_copy(terms_vmem, terms_smem, sems.at[1])
    fetch.start()
    table.wait()
    used = EDGE_ROWS
    pulled = mul3((own_ref[0, :, :used], own_ref[1, :, :used]), split(packed[0:used]))
    sin_part = pltpu.roll(pulled[ROWS:], KS // 2, 1)
    lane = lanes_of((ROWS, KS))
    main = pulled[:ROWS] + jnp.where(lane < KS // 2, -sin_part, sin_part)
    edge = packed[EDGE_ROWS:TERM_ROWS]
    blank = jnp.zeros((KS - 16, KS), F32)
    none = jnp.zeros((8, KS), F32)
    cos_rows = (own_ref[0, :ROWS, :KS], own_ref[1, :ROWS, :KS])
    sin_rows = (own_ref[0, ROWS:, :KS], own_ref[1, ROWS:, :KS])
    contract = ((1,), (1,))
    side = mul3(cos_rows, split(jnp.concatenate([edge, none, blank], 0)), contract) + mul3(
        sin_rows, split(jnp.concatenate([none, edge, blank], 0)), contract
    )
    gathered = split(jnp.concatenate([main, side], 1))
    transmit = jnp.tanh(mask_ref[...])
    out_ref[...] = mul3_few(gathered, pair(cols_ref)) * (1.0 - transmit * transmit)
    fetch.wait()
    for slot in range(CAP):
        place = me * CAP + slot
        slot_ref[slot] = terms_smem[place >> 7, place & 127]


def exchange(value, others):
    received = [value]
    for other in others:
        pairs = [(index, index ^ other) for index in range(SRC)]
        received.append(lax.ppermute(value, "src", pairs))
    return received


MIB = 1024 * 1024


def run(kernel, name, operands, outputs, scratch, limit, in_vmem=()):
    smem = pl.BlockSpec(memory_space=pltpu.SMEM)
    hbm = pl.BlockSpec(memory_space=pltpu.HBM)
    vmem = pl.BlockSpec(memory_space=pltpu.VMEM)
    kinds = {"smem": smem, "hbm": hbm, "vmem": vmem}
    return pl.pallas_call(
        kernel,
        in_specs=[vmem if place in in_vmem else hbm for place in range(len(operands))],
        out_specs=[kinds[kind] for kind, unused, unused in outputs],
        out_shape=[jax.ShapeDtypeStruct(shape, dtype) for unused, shape, dtype in outputs],
        scratch_shapes=scratch,
        compiler_params=pltpu.CompilerParams(vmem_limit_bytes=limit * MIB),
        name=name,
    )(*operands)


def body(mask_param, pixel_weight, source_weight, point_index, point_count, target_rects):
    table = tables()
    vmem = lambda array: pltpu.VMEM(array.shape, array.dtype)
    smem = lambda array: pltpu.SMEM(array.shape, array.dtype)
    dma = lambda count: pltpu.SemaphoreType.DMA((count,))

    (block,) = run(
        project_kernel,
        "project",
        [point_index, point_count, source_weight, mask_param, table["cols"], table["own"]],
        [("vmem", (GATHER, PACK, 128), F32)],
        [
            smem(point_index), smem(point_count), smem(source_weight), vmem(mask_param), vmem(table["cols"]),
            vmem(table["own"][0]), dma(6),
        ],
        60,
    )

    same_core = [list(range(core, SRC, 2)) for core in range(2)]
    mine = lax.all_to_all(block, "src", 0, 0, axis_index_groups=same_core, tiled=True)
    unused, other = exchange(mine, CORE)

    operands = [mine, other] + [table[name] for name in IMAGE_TABLES]
    listed = SLOTS // GROUP + BATCH
    sums, codes, weights, slots, count, field = run(
        image_kernel,
        "image",
        operands,
        [
            ("hbm", (SUMS, 128), F32),
            ("smem", (listed,), jnp.int32),
            ("smem", (listed,), F32),
            ("smem", (listed,), jnp.int32),
            ("smem", (1,), jnp.int32),
            ("hbm", (BATCHES, BATCH * SUB, 2 * SUB), F32),
        ],
        [
            pltpu.VMEM((SUMS, 128), F32),
            pltpu.VMEM((KS, KS), F32),
            pltpu.VMEM((KS, KS), F32),
            pltpu.VMEM((BATCHES, BATCH * SUB, 2 * SUB), F32),
            pltpu.VMEM((2, BATCH * SUB, KS), BF16),
            pltpu.SMEM((SRC, 128), F32),
            pltpu.SMEM((listed,), jnp.int32),
            dma(3),
            dma(BATCHES),
        ],
        44,
        range(len(operands)),
    )

    all_sums = exchange(sums, GROUP_DEVICES)
    rects_t = target_rects.T
    lists = [codes, weights, slots, count]
    constants = [table[name] for name in GRAD_TABLES]
    grad, aerial, loss = run(
        grad_kernel,
        "gradient",
        all_sums + [pixel_weight, target_rects, rects_t, field] + lists + constants,
        [("vmem", (GRAD, 128), F32), ("vmem", (ROWS, NPIX), F32), ("smem", (1,), F32)],
        [vmem(array) for array in [pixel_weight, field]]
        + [smem(array) for array in lists]
        + [
            pltpu.VMEM((2, 2 * SUB, NPIX // 2), BF16),
            pltpu.VMEM((NPIX, NPIX), F32),
            pltpu.VMEM((NPIX, NPIX), F32),
            pltpu.VMEM((NPIX // 2 // BLOCK, 2, 2, BLOCK, NPIX), BF16),
            pltpu.VMEM((2, SUB // 2, NPIX), F32),
            pltpu.VMEM((2, KS, KS), F32),
            pltpu.VMEM((2, BATCH * KP, 2 * SUB), BF16),
            dma(len(lists)),
            dma(NPIX // BLOCK),
            dma(BATCHES),
        ],
        52,
        [place for place in range(GROUP + 8 + len(constants)) if place not in KEPT_IN_HBM],
    )

    grads = exchange(grad, GROUP_DEVICES)
    operands = grads + [mask_param, table["own"], table["cols_t"]]
    mask_grad, source_grad = run(
        mask_kernel,
        "mask",
        operands,
        [("vmem", (ROWS, NPIX), F32), ("smem", (CAP,), F32)],
        [vmem(table["own"][0]), pltpu.VMEM((8, 128), F32), pltpu.SMEM((8, 128), F32), dma(2)],
        32,
        [place for place in range(len(operands)) if place != GROUP + 1],
    )
    return mask_grad, aerial, source_grad, loss


def solution(mesh):
    in_specs = (P(("clip", "src"), None), P("clip", None), P(), P("src"), P("src"), P("clip", None))
    out_specs = (P(("clip", "src"), None), P(("clip", "src"), None), P(("clip", "src")), P("clip"))
    return jax.shard_map(body, mesh=mesh, in_specs=in_specs, out_specs=out_specs, check_vma=False)
```
